32 devices in a mesh: seq: 4 (over y, x), dp: 8 (over z, core).
Axes of the slice: x: 2, y: 2, z: 4, core: 2. Of those that a mesh axis runs over, the one named last changes fastest.
Arguments:
- tokens: bfloat16 [8, 1024, 1152], P('dp', 'seq'), may hold values from -6 to 6
- cotangent: bfloat16 [8, 1024, 1152], P('dp', 'seq'), may hold values from -6 to 6
- picture_starts: int32 [8, 2], P('dp'), may hold values from 0 to 768, as said below
- query_weight: float32 [1152, 1152], P('seq'), may hold values from -0.1875 to 0.1875
- key_matrix: float32 [1152, 384], P('seq'), may hold values from -0.1875 to 0.1875
- value_matrix: float32 [1152, 384], P('seq'), may hold values from -0.1875 to 0.1875
- out_weight: float32 [1152, 1152], P('seq'), may hold values from -2.5 to 2.5
- gate_weight: float32 [1152, 3072], P('seq'), may hold values from -0.1875 to 0.1875
- up_weight: float32 [1152, 3072], P('seq'), may hold values from -0.1875 to 0.1875
- down_weight: float32 [3072, 1152], P('seq'), may hold values from -0.109375 to 0.109375
- attention_gain: float32 [1152], P('seq'), may hold values from 0.3 to 2.5
- feed_gain: float32 [1152], P('seq'), may hold values from 0.3 to 2.5
- query_moment: float32 [1152, 1152], P('seq'), may hold values from -6 to 6
- key_velocity: float32 [1152, 384], P('seq'), may hold values from -6 to 6
- value_velocity: float32 [1152, 384], P('seq'), may hold values from -6 to 6
- out_moment: float32 [1152, 1152], P('seq'), may hold values from -6 to 6
- gate_moment: float32 [1152, 3072], P('seq'), may hold values from -6 to 6
- up_moment: float32 [1152, 3072], P('seq'), may hold values from -6 to 6
- down_moment: float32 [3072, 1152], P('seq'), may hold values from -6 to 6
- attention_moment: float32 [1152], P('seq'), may hold values from -6 to 6
- feed_moment: float32 [1152], P('seq'), may hold values from -6 to 6
Outputs:
- layer_output: bfloat16 [8, 1024, 1152], P('dp', 'seq')
- input_gradient: float32 [8, 1024, 1152], P('dp', 'seq')
- query_momentum: float32 [1152, 1152], P('seq')
- key_momentum: float32 [1152, 384], P('seq')
- value_momentum: float32 [1152, 384], P('seq')
- out_momentum: float32 [1152, 1152], P('seq')
- gate_momentum: float32 [1152, 3072], P('seq')
- up_momentum: float32 [1152, 3072], P('seq')
- down_momentum: float32 [3072, 1152], P('seq')
- attention_momentum: float32 [1152], P('seq')
- feed_momentum: float32 [1152], P('seq')
- query_updated: float32 [1152, 1152], P('seq')
- key_updated: float32 [1152, 384], P('seq')
- value_updated: float32 [1152, 384], P('seq')
- out_updated: float32 [1152, 1152], P('seq')
- gate_updated: float32 [1152, 3072], P('seq')
- up_updated: float32 [1152, 3072], P('seq')
- down_updated: float32 [3072, 1152], P('seq')
- attention_updated: float32 [1152], P('seq')
- feed_updated: float32 [1152], P('seq')
- gradient_norm: float32 [], replicated
The draws below stay inside these ranges and needn't reach their ends.
Inputs may be any that keep to these rules, and one draw needn't show every extreme that they name: `picture_starts`: row s holds the first positions of the 2 picture pieces of sequence s, each 256 positions long; piece p lies within positions p * 512 to (p + 1) * 512 - 1, so pieces ascend and never meet.
All inputs are finite; a program needn't handle non-finite values.
Results may differ from the reference program's by a relative error of at most 0.015.
Values may be sent and summed in bfloat16 or wider, within the bound.
No kernel may reach another device: no remote copies, remote signals or barrier semaphores. Data moves between devices by JAX's collectives and lax.ppermute only.
A program may use at most 256 MiB of HBM per device.

```python
import math
from functools import partial
import jax
import jax.numpy as jnp
from jax import lax

MODEL_WIDTH = 1152
QUERY_HEAD_COUNT = 18
KEY_VALUE_HEADS = 6
HEAD_SIZE = 64
FF = 3072
PIECE = 256
LENGTH = 1024
PICS = 2
SEQS = 8
PARAMS = 14158080


def draw_picture_starts(key, part):
    slot_width = LENGTH // PICS
    offsets = jax.random.randint(key, (SEQS, PICS), 0, slot_width - PIECE + 1)
    return (offsets + slot_width * jnp.arange(PICS, dtype=jnp.int32)[None, :]).astype(jnp.int32)


def draw_attention_gain(key, part):
    place = jnp.arange(MODEL_WIDTH, dtype=jnp.float32) / MODEL_WIDTH
    rough = jax.random.uniform(jax.random.fold_in(key, 11), (MODEL_WIDTH,), jnp.float32, 0.85, 1.15)
    return (0.5 * 3.0 ** place * rough).astype(jnp.float32)


def draw_feed_gain(key, part):
    place = jnp.arange(MODEL_WIDTH, dtype=jnp.float32) / MODEL_WIDTH
    rough = jax.random.uniform(jax.random.fold_in(key, 23), (MODEL_WIDTH,), jnp.float32, 0.85, 1.15)
    return (0.5 * 3.0 ** place * rough).astype(jnp.float32)


def block_scale(stream_key, extent, split, low, top_value):
    gain, own = 1.0, jax.random.fold_in(stream_key, 6)
    for axis_at, shards_of in split:
        draws = jnp.exp(jax.random.uniform(jax.random.fold_in(own, axis_at), (shards_of,), jnp.float32, low / len(split), top_value / len(split)))
        gain = gain * jnp.repeat(draws, extent[axis_at] // shards_of).reshape([-1 if axis == axis_at else 1 for axis in range(len(extent))])
    return gain


def scatter_about(key, dims, deviation, reach, shards=(), kind=jnp.bfloat16):
    entries = deviation * jax.random.normal(key, dims, jnp.float32)
    if shards:
        entries = entries * block_scale(key, dims, shards, -0.22, 0.18)
    return jnp.clip(entries, -reach, reach).astype(kind)


def setup_inputs(seed: int = 0) -> dict:
    splits = jax.random.split(jax.random.key(seed), 22)
    tokens = scatter_about(splits[0], (SEQS, LENGTH, MODEL_WIDTH), 1.0, 6.0, ((0, 8), (1, 4)))
    cotangent = scatter_about(splits[1], (SEQS, LENGTH, MODEL_WIDTH), 1.0, 6.0, ((0, 8), (1, 4)))
    picture_starts = draw_picture_starts(jax.random.fold_in(splits[21], 71), 0)
    query_weight = scatter_about(splits[3], (MODEL_WIDTH, QUERY_HEAD_COUNT * HEAD_SIZE), MODEL_WIDTH ** -0.5, 0.1875, ((0, 4),), jnp.float32)
    key_matrix = scatter_about(splits[4], (MODEL_WIDTH, KEY_VALUE_HEADS * HEAD_SIZE), MODEL_WIDTH ** -0.5, 0.1875, ((0, 4),), jnp.float32)
    value_matrix = scatter_about(splits[5], (MODEL_WIDTH, KEY_VALUE_HEADS * HEAD_SIZE), MODEL_WIDTH ** -0.5, 0.1875, ((0, 4),), jnp.float32)
    out_weight = scatter_about(splits[6], (QUERY_HEAD_COUNT * HEAD_SIZE, MODEL_WIDTH), (max(1, 5 * MODEL_WIDTH // LENGTH)) ** -0.5, 2.5, ((0, 4),), jnp.float32)
    gate_weight = scatter_about(splits[7], (MODEL_WIDTH, FF), MODEL_WIDTH ** -0.5, 0.1875, ((0, 4),), jnp.float32)
    up_weight = scatter_about(splits[8], (MODEL_WIDTH, FF), MODEL_WIDTH ** -0.5, 0.1875, ((0, 4),), jnp.float32)
    down_weight = scatter_about(splits[9], (FF, MODEL_WIDTH), FF ** -0.5, 0.109375, ((0, 4),), jnp.float32)
    attention_gain = draw_attention_gain(jax.random.fold_in(splits[21], 71), 0)
    feed_gain = draw_feed_gain(jax.random.fold_in(splits[21], 71), 0)
    query_moment = scatter_about(splits[12], (MODEL_WIDTH, QUERY_HEAD_COUNT * HEAD_SIZE), 1.0, 6.0, ((0, 4),), jnp.float32)
    key_velocity = scatter_about(splits[13], (MODEL_WIDTH, KEY_VALUE_HEADS * HEAD_SIZE), 1.0, 6.0, ((0, 4),), jnp.float32)
    value_velocity = scatter_about(splits[14], (MODEL_WIDTH, KEY_VALUE_HEADS * HEAD_SIZE), 1.0, 6.0, ((0, 4),), jnp.float32)
    out_moment = scatter_about(splits[15], (QUERY_HEAD_COUNT * HEAD_SIZE, MODEL_WIDTH), 1.0, 6.0, ((0, 4),), jnp.float32)
    gate_moment = scatter_about(splits[16], (MODEL_WIDTH, FF), 1.0, 6.0, ((0, 4),), jnp.float32)
    up_moment = scatter_about(splits[17], (MODEL_WIDTH, FF), 1.0, 6.0, ((0, 4),), jnp.float32)
    down_moment = scatter_about(splits[18], (FF, MODEL_WIDTH), 1.0, 6.0, ((0, 4),), jnp.float32)
    attention_moment = scatter_about(splits[19], (MODEL_WIDTH,), 1.0, 6.0, ((0, 4),), jnp.float32)
    feed_moment = scatter_about(splits[20], (MODEL_WIDTH,), 1.0, 6.0, ((0, 4),), jnp.float32)
    return dict(tokens=tokens, cotangent=cotangent, picture_starts=picture_starts, query_weight=query_weight, key_matrix=key_matrix, value_matrix=value_matrix, out_weight=out_weight, gate_weight=gate_weight, up_weight=up_weight, down_weight=down_weight, attention_gain=attention_gain, feed_gain=feed_gain, query_moment=query_moment, key_velocity=key_velocity, value_velocity=value_velocity, out_moment=out_moment, gate_moment=gate_moment, up_moment=up_moment, down_moment=down_moment, attention_moment=attention_moment, feed_moment=feed_moment)


learning_rate = 0.25
weight_decay = 0.1
momentum_beta = 0.5

@jax.custom_vjp
def reduced_precision(v):
    return lax.optimization_barrier(v.astype(jnp.bfloat16)).astype(jnp.float32)

@jax.custom_vjp
def reduced_pullback(v):
    return v

def low_keep(v):
    return (reduced_precision(v), None)

def low_pass(kept, grad):
    return (grad,)

def back_keep(v):
    return (v, None)

def back_low(kept, grad):
    return (reduced_precision(grad),)
reduced_precision.defvjp(low_keep, low_pass)
reduced_pullback.defvjp(back_keep, back_low)

def exact_product(left, right):
    return jnp.dot(left, right, precision=lax.Precision.HIGHEST, preferred_element_type=jnp.float32)

def rms_scale(values, scaling):
    return values * lax.rsqrt(lax.optimization_barrier(jnp.mean(values * values, axis=-1, keepdims=True)) + 1e-05) * scaling

def apply_rotary(values, token_positions):
    half_width = values.shape[-1] // 2
    frequency = 10000.0 ** (-jnp.arange(half_width, dtype=jnp.float32) / half_width)
    angles = token_positions.astype(jnp.float32)[:, None] * frequency[None, :]
    cosine = jnp.cos(angles)[:, None, :]
    sine_part = jnp.sin(angles)[:, None, :]
    leading = values[..., :half_width]
    trailing = values[..., half_width:]
    return jnp.concatenate([leading * cosine - trailing * sine_part, trailing * cosine + leading * sine_part], axis=-1)

def swiglu(gate_values, up_values):
    return jax.nn.silu(gate_values) * up_values

def piece_number(token_positions, starts):
    inside = (token_positions[:, None] >= starts[None, :]) & (token_positions[:, None] < starts[None, :] + PIECE)
    numbers = jnp.arange(starts.shape[0], dtype=jnp.int32) + 1
    return lax.optimization_barrier(jnp.sum(jnp.where(inside, numbers[None, :], 0), axis=1)).astype(jnp.int32) - 1

def visible(query_position, query_piece, key_position, key_piece):
    earlier = key_position[None, :] <= query_position[:, None]
    same_piece = (query_piece[:, None] == key_piece[None, :]) & (query_piece[:, None] >= 0)
    return earlier | same_piece

def layer(layer_input, weights, token_positions, pieces):
    full_query, complete_key, complete_value, full_out, full_gate, full_up, full_down, gain_one, gain_two = weights
    rows_of_sequence = layer_input.shape[0]
    heads_per_group = QUERY_HEAD_COUNT // KEY_VALUE_HEADS
    first_activation = reduced_precision(rms_scale(layer_input, gain_one))
    rotated_query = reduced_precision(apply_rotary(reduced_pullback(exact_product(first_activation, full_query)).reshape(rows_of_sequence, QUERY_HEAD_COUNT, HEAD_SIZE), token_positions))
    rotated_key = reduced_precision(apply_rotary(reduced_pullback(exact_product(first_activation, complete_key)).reshape(rows_of_sequence, KEY_VALUE_HEADS, HEAD_SIZE), token_positions))
    value_reduced = reduced_precision(reduced_pullback(exact_product(first_activation, complete_value))).reshape(rows_of_sequence, KEY_VALUE_HEADS, HEAD_SIZE)
    rows_per_block = math.gcd(512, rows_of_sequence)
    count_of_blocks = rows_of_sequence // rows_per_block
    query_block_list = rotated_query.reshape(count_of_blocks, rows_per_block, KEY_VALUE_HEADS, heads_per_group, HEAD_SIZE)
    position_blocks = token_positions.reshape(count_of_blocks, rows_per_block)
    piece_blocks = pieces.reshape(count_of_blocks, rows_per_block)

    def attend(block_data):
        query_block, query_position, query_piece = block_data
        raw_scores = jnp.einsum('qhgd,khd->hgqk', query_block, rotated_key, precision=lax.Precision.HIGHEST)
        scores = reduced_pullback(raw_scores * 0.125)
        allowed = visible(query_position, query_piece, token_positions, pieces)
        exponent = jnp.where(allowed[None, None], jnp.exp(scores), 0.0)
        totals = lax.optimization_barrier(jnp.sum(exponent, axis=-1))
        summed = reduced_pullback(jnp.einsum('hgqk,khd->qhgd', reduced_precision(exponent), value_reduced, precision=lax.Precision.HIGHEST))
        return summed / jnp.transpose(totals, (2, 0, 1))[..., None]
    attended = lax.map(jax.checkpoint(attend), (query_block_list, position_blocks, piece_blocks))
    attention = reduced_precision(reduced_pullback(attended.reshape(rows_of_sequence, QUERY_HEAD_COUNT * HEAD_SIZE)))
    residual = layer_input + reduced_pullback(exact_product(attention, full_out))
    act_two = reduced_precision(rms_scale(residual, gain_two))
    gate_linear = reduced_pullback(exact_product(act_two, full_gate))
    up_linear = reduced_pullback(exact_product(act_two, full_up))
    hidden = reduced_precision(swiglu(gate_linear, up_linear))
    return residual + reduced_pullback(exact_product(hidden, full_down))

def reference(tokens, cotangent, picture_starts, query_weight, key_matrix, value_matrix, out_weight, gate_weight, up_weight, down_weight, attention_gain, feed_gain, query_moment, key_velocity, value_velocity, out_moment, gate_moment, up_moment, down_moment, attention_moment, feed_moment):
    masters = (query_weight, key_matrix, value_matrix, out_weight, gate_weight, up_weight, down_weight, attention_gain, feed_gain)
    moments = (query_moment, key_velocity, value_velocity, out_moment, gate_moment, up_moment, down_moment, attention_moment, feed_moment)
    weights = tuple((reduced_precision(master) for master in masters))
    token_positions = jnp.arange(LENGTH, dtype=jnp.int32)

    def one_sequence(running, inputs):
        sequence_tokens, sequence_cotangent, starts = inputs
        pieces = piece_number(token_positions, starts)
        forward = partial(layer, token_positions=token_positions, pieces=pieces)
        layer_out, pullback = jax.vjp(forward, sequence_tokens.astype(jnp.float32), weights)
        input_grad, weight_grads = pullback(sequence_cotangent.astype(jnp.float32))
        running = tuple((before + gradient for before, gradient in zip(running, weight_grads)))
        return (running, (layer_out.astype(jnp.bfloat16), input_grad))
    zero_grads = tuple((jnp.zeros(master.shape, jnp.float32) for master in masters))
    gradients, (layer_output, input_gradient) = lax.scan(one_sequence, zero_grads, (tokens, cotangent, picture_starts))
    squares = jnp.float32(0.0)
    for gradient in gradients:
        squares = squares + jnp.sum(gradient * gradient)
    gradient_norm = jnp.sqrt(squares)
    clip_factor = jnp.minimum(1.0, jnp.sqrt(jnp.float32(PARAMS)) / (gradient_norm + 1e-06))
    momenta = [momentum_beta * moment + clip_factor * gradient for moment, gradient in zip(moments, gradients)]
    updated = [master * (1.0 - learning_rate * weight_decay) - learning_rate * momentum for master, momentum in zip(masters, momenta)]
    return (layer_output, input_gradient, momenta[0], momenta[1], momenta[2], momenta[3], momenta[4], momenta[5], momenta[6], momenta[7], momenta[8], updated[0], updated[1], updated[2], updated[3], updated[4], updated[5], updated[6], updated[7], updated[8], gradient_norm)
```

```python
from functools import partial
import math

import jax
import jax.numpy as jnp
from jax import lax
from jax.sharding import PartitionSpec as P

QUERY_HEAD_COUNT = 18
KEY_VALUE_HEADS = 6
HEAD_SIZE = 64
PIECE = 256
PARAMS = 14158080


learning_rate = 0.25
weight_decay = 0.1
momentum_beta = 0.5


def rms_scale(values, scaling):
    return values * lax.rsqrt(jnp.mean(values * values, axis=-1, keepdims=True) + 1e-05) * scaling


def apply_rotary(values, token_positions):
    half_width = values.shape[-1] // 2
    frequency = 10000.0 ** (-jnp.arange(half_width, dtype=jnp.float32) / half_width)
    angles = token_positions.astype(jnp.float32)[:, None] * frequency[None, :]
    cosine = jnp.cos(angles)[:, None, :]
    sine_part = jnp.sin(angles)[:, None, :]
    leading = values[..., :half_width]
    trailing = values[..., half_width:]
    return jnp.concatenate(
        [leading * cosine - trailing * sine_part, trailing * cosine + leading * sine_part], axis=-1
    )


def swiglu(gate_values, up_values):
    return jax.nn.silu(gate_values) * up_values


def piece_number(token_positions, starts):
    inside = (token_positions[:, None] >= starts[None, :]) & (
        token_positions[:, None] < starts[None, :] + PIECE
    )
    numbers = jnp.arange(starts.shape[0], dtype=jnp.int32) + 1
    return jnp.sum(jnp.where(inside, numbers[None, :], 0), axis=1) - 1


def visible(query_position, query_piece, key_position, key_piece):
    earlier = key_position[None, :] <= query_position[:, None]
    same_piece = (query_piece[:, None] == key_piece[None, :]) & (query_piece[:, None] >= 0)
    return earlier | same_piece


def per_device(
    tokens,
    cotangent,
    picture_starts,
    query_weight,
    key_matrix,
    value_matrix,
    out_weight,
    gate_weight,
    up_weight,
    down_weight,
    attention_gain,
    feed_gain,
    query_moment,
    key_velocity,
    value_velocity,
    out_moment,
    gate_moment,
    up_moment,
    down_moment,
    attention_moment,
    feed_moment,
):
    masters = (
        query_weight,
        key_matrix,
        value_matrix,
        out_weight,
        gate_weight,
        up_weight,
        down_weight,
        attention_gain,
        feed_gain,
    )
    moments = (
        query_moment,
        key_velocity,
        value_velocity,
        out_moment,
        gate_moment,
        up_moment,
        down_moment,
        attention_moment,
        feed_moment,
    )
    shard_query = query_weight.astype(jnp.bfloat16)
    shard_key = key_matrix.astype(jnp.bfloat16)
    shard_value = value_matrix.astype(jnp.bfloat16)
    shard_out = out_weight.astype(jnp.bfloat16)
    shard_gate = gate_weight.astype(jnp.bfloat16)
    shard_up = up_weight.astype(jnp.bfloat16)
    shard_down = down_weight.astype(jnp.bfloat16)
    shard_gain_one = attention_gain.astype(jnp.bfloat16)
    shard_gain_two = feed_gain.astype(jnp.bfloat16)
    gathered = (
        lax.all_gather(shard_query, "seq", axis=0, tiled=True),
        lax.all_gather(shard_key, "seq", axis=0, tiled=True),
        lax.all_gather(shard_value, "seq", axis=0, tiled=True),
        lax.all_gather(shard_out, "seq", axis=0, tiled=True),
        lax.all_gather(shard_gate, "seq", axis=0, tiled=True),
        lax.all_gather(shard_up, "seq", axis=0, tiled=True),
        lax.all_gather(shard_down, "seq", axis=0, tiled=True),
        lax.all_gather(shard_gain_one, "seq", axis=0, tiled=True),
        lax.all_gather(shard_gain_two, "seq", axis=0, tiled=True),
    )
    full_query, complete_key, complete_value, full_out, full_gate, full_up, full_down = gathered[:7]
    gain_one = gathered[7].astype(jnp.float32)
    gain_two = gathered[8].astype(jnp.float32)
    group_size = lax.axis_size("seq")
    local_rows = tokens.shape[1]
    sequence_length = local_rows * group_size
    heads_per_group = QUERY_HEAD_COUNT // KEY_VALUE_HEADS
    token_positions = lax.axis_index("seq") * local_rows + jnp.arange(local_rows, dtype=jnp.int32)
    starts = picture_starts[0]
    query_piece = piece_number(token_positions, starts)
    key_positions = jnp.arange(sequence_length, dtype=jnp.int32)
    key_pieces = piece_number(key_positions, starts)
    layer_input = tokens[0].astype(jnp.float32)
    normed_one, pull_norm_one = jax.vjp(rms_scale, layer_input, gain_one)
    first_activation = normed_one.astype(jnp.bfloat16)
    rotation = partial(apply_rotary, token_positions=token_positions)
    query_linear = jnp.dot(
        first_activation, full_query, preferred_element_type=jnp.float32
    ).reshape(local_rows, QUERY_HEAD_COUNT, HEAD_SIZE)
    rotated_query, pull_query = jax.vjp(rotation, query_linear)
    query_reduced = rotated_query.astype(jnp.bfloat16).reshape(
        local_rows, KEY_VALUE_HEADS, heads_per_group, HEAD_SIZE
    )
    key_linear = jnp.dot(
        first_activation, complete_key, preferred_element_type=jnp.float32
    ).reshape(local_rows, KEY_VALUE_HEADS, HEAD_SIZE)
    rotated_key, key_pullback = jax.vjp(rotation, key_linear)
    key_reduced = rotated_key.astype(jnp.bfloat16).reshape(local_rows, KEY_VALUE_HEADS * HEAD_SIZE)
    value_reduced = jnp.dot(
        first_activation, complete_value, preferred_element_type=jnp.float32
    ).astype(jnp.bfloat16)
    every_key_row, every_value_row = (
        lax.all_gather(key_reduced, "seq", axis=0, tiled=True),
        lax.all_gather(value_reduced, "seq", axis=0, tiled=True),
    )
    every_key_row = every_key_row.reshape(sequence_length, KEY_VALUE_HEADS, HEAD_SIZE)
    every_value_row = every_value_row.reshape(sequence_length, KEY_VALUE_HEADS, HEAD_SIZE)
    rows_per_block = math.gcd(512, sequence_length)
    count_of_blocks = sequence_length // rows_per_block
    last_position = token_positions[local_rows - 1]
    last_piece = query_piece[local_rows - 1]

    def needed(number):
        first_row = number * rows_per_block
        return (first_row <= last_position) | (last_piece >= 0) & (
            key_pieces[first_row] == last_piece
        )

    def block_scores(number):
        first_row = number * rows_per_block
        key_block = lax.dynamic_slice_in_dim(every_key_row, first_row, rows_per_block, 0)
        value_block = lax.dynamic_slice_in_dim(every_value_row, first_row, rows_per_block, 0)
        allowed = visible(
            token_positions,
            query_piece,
            lax.dynamic_slice_in_dim(key_positions, first_row, rows_per_block, 0),
            lax.dynamic_slice_in_dim(key_pieces, first_row, rows_per_block, 0),
        )
        raw_scores = jnp.einsum(
            "qhgd,khd->hgqk", query_reduced, key_block, preferred_element_type=jnp.float32
        )
        exponent = jnp.where(allowed[None, None], jnp.exp(raw_scores * 0.125), 0.0)
        return (key_block, value_block, exponent)

    def unchanged(current):
        return current

    def forward_step(number, running):

        def forward_compute(current):
            summed, totals = current
            key_block, value_block, exponent = block_scores(number)
            summed = summed + jnp.einsum(
                "hgqk,khd->hgqd",
                exponent.astype(jnp.bfloat16),
                value_block,
                preferred_element_type=jnp.float32,
            )
            return (summed, totals + jnp.sum(exponent, axis=-1))

        return lax.cond(needed(number), forward_compute, unchanged, running)

    initial_sum = jnp.zeros((KEY_VALUE_HEADS, heads_per_group, local_rows, HEAD_SIZE), jnp.float32)
    initial_total = jnp.zeros((KEY_VALUE_HEADS, heads_per_group, local_rows), jnp.float32)
    summed, totals = lax.fori_loop(0, count_of_blocks, forward_step, (initial_sum, initial_total))
    attended = summed / totals[..., None]
    attention = (
        jnp.transpose(attended, (2, 0, 1, 3))
        .reshape(local_rows, QUERY_HEAD_COUNT * HEAD_SIZE)
        .astype(jnp.bfloat16)
    )
    residual = layer_input + jnp.dot(attention, full_out, preferred_element_type=jnp.float32)
    normed_two, pull_norm_two = jax.vjp(rms_scale, residual, gain_two)
    act_two = normed_two.astype(jnp.bfloat16)
    gate_linear = jnp.dot(act_two, full_gate, preferred_element_type=jnp.float32)
    up_linear = jnp.dot(act_two, full_up, preferred_element_type=jnp.float32)
    hidden_full, pull_swiglu = jax.vjp(swiglu, gate_linear, up_linear)
    hidden = hidden_full.astype(jnp.bfloat16)
    layer_out = residual + jnp.dot(hidden, full_down, preferred_element_type=jnp.float32)
    output = layer_out.astype(jnp.bfloat16)[None]
    upstream = cotangent[0].astype(jnp.float32)
    upstream_low = upstream.astype(jnp.bfloat16)
    grad_down = jnp.einsum("nf,nd->fd", hidden, upstream_low, preferred_element_type=jnp.float32)
    grad_hidden = jnp.einsum(
        "nd,fd->nf", upstream_low, full_down, preferred_element_type=jnp.float32
    )
    grad_gate_full, grad_up_full = pull_swiglu(grad_hidden)
    gate_back = grad_gate_full.astype(jnp.bfloat16)
    up_back = grad_up_full.astype(jnp.bfloat16)
    grad_gate = jnp.einsum("nd,nf->df", act_two, gate_back, preferred_element_type=jnp.float32)
    grad_up = jnp.einsum("nd,nf->df", act_two, up_back, preferred_element_type=jnp.float32)
    grad_act_two = jnp.einsum(
        "nf,df->nd", gate_back, full_gate, preferred_element_type=jnp.float32
    ) + jnp.einsum("nf,df->nd", up_back, full_up, preferred_element_type=jnp.float32)
    residual_norm_grad, grad_gain_two = pull_norm_two(grad_act_two)
    grad_residual = upstream + residual_norm_grad
    residual_back = grad_residual.astype(jnp.bfloat16)
    grad_out = jnp.einsum("nk,nd->kd", attention, residual_back, preferred_element_type=jnp.float32)
    attention_pullback = jnp.einsum(
        "nd,kd->nk", residual_back, full_out, preferred_element_type=jnp.float32
    ).astype(jnp.bfloat16)
    attention_pullback = jnp.transpose(
        attention_pullback.reshape(local_rows, KEY_VALUE_HEADS, heads_per_group, HEAD_SIZE),
        (1, 2, 0, 3),
    )
    back_full = attention_pullback.astype(jnp.float32)
    scaled_back = (back_full / totals[..., None]).astype(jnp.bfloat16)
    total_back = -jnp.sum(back_full * attended, axis=-1) / totals
    query_heads = jnp.transpose(query_reduced, (1, 2, 0, 3))

    def backward_step(number, running):

        def backward_compute(current):
            grad_query_sum, key_gradient_rows, value_gradient_rows = current
            first_row = number * rows_per_block
            key_block, value_block, exponent = block_scores(number)
            through = jnp.einsum(
                "hgqd,khd->hgqk", scaled_back, value_block, preferred_element_type=jnp.float32
            )
            score_back = (exponent * (through + total_back[..., None])).astype(jnp.bfloat16)
            grad_query_sum = (
                grad_query_sum
                + jnp.einsum(
                    "hgqk,khd->hgqd", score_back, key_block, preferred_element_type=jnp.float32
                )
                * 0.125
            )
            key_part = (
                jnp.einsum(
                    "hgqk,hgqd->khd", score_back, query_heads, preferred_element_type=jnp.float32
                )
                * 0.125
            )
            value_part = jnp.einsum(
                "hgqk,hgqd->khd",
                exponent.astype(jnp.bfloat16),
                scaled_back,
                preferred_element_type=jnp.float32,
            )
            key_gradient_rows = lax.dynamic_update_slice_in_dim(
                key_gradient_rows, key_part, first_row, 0
            )
            value_gradient_rows = lax.dynamic_update_slice_in_dim(
                value_gradient_rows, value_part, first_row, 0
            )
            return (grad_query_sum, key_gradient_rows, value_gradient_rows)

        return lax.cond(needed(number), backward_compute, unchanged, running)

    initial_query = jnp.zeros(
        (KEY_VALUE_HEADS, heads_per_group, local_rows, HEAD_SIZE), jnp.float32
    )
    initial_keys = jnp.zeros((sequence_length, KEY_VALUE_HEADS, HEAD_SIZE), jnp.float32)
    grad_query_sum, key_gradient_rows, value_gradient_rows = lax.fori_loop(
        0, count_of_blocks, backward_step, (initial_query, initial_keys, initial_keys)
    )
    local_key_rows, value_own = (
        lax.psum_scatter(
            key_gradient_rows.reshape(sequence_length, KEY_VALUE_HEADS * HEAD_SIZE),
            "seq",
            scatter_dimension=0,
            tiled=True,
        ),
        lax.psum_scatter(
            value_gradient_rows.reshape(sequence_length, KEY_VALUE_HEADS * HEAD_SIZE),
            "seq",
            scatter_dimension=0,
            tiled=True,
        ),
    )
    key_back = (
        key_pullback(local_key_rows.reshape(local_rows, KEY_VALUE_HEADS, HEAD_SIZE))[0]
        .reshape(local_rows, KEY_VALUE_HEADS * HEAD_SIZE)
        .astype(jnp.bfloat16)
    )
    query_rot_grad = jnp.transpose(grad_query_sum, (2, 0, 1, 3)).reshape(
        local_rows, QUERY_HEAD_COUNT, HEAD_SIZE
    )
    query_back = (
        pull_query(query_rot_grad)[0]
        .reshape(local_rows, QUERY_HEAD_COUNT * HEAD_SIZE)
        .astype(jnp.bfloat16)
    )
    value_back = value_own.astype(jnp.bfloat16)
    grad_query = jnp.einsum(
        "nd,nk->dk", first_activation, query_back, preferred_element_type=jnp.float32
    )
    grad_key = jnp.einsum(
        "nd,nk->dk", first_activation, key_back, preferred_element_type=jnp.float32
    )
    grad_value = jnp.einsum(
        "nd,nk->dk", first_activation, value_back, preferred_element_type=jnp.float32
    )
    grad_act_one = jnp.einsum(
        "nk,dk->nd", query_back, full_query, preferred_element_type=jnp.float32
    )
    grad_act_one = grad_act_one + jnp.einsum(
        "nk,dk->nd", key_back, complete_key, preferred_element_type=jnp.float32
    )
    grad_act_one = grad_act_one + jnp.einsum(
        "nk,dk->nd", value_back, complete_value, preferred_element_type=jnp.float32
    )
    input_norm_grad, grad_gain_one = pull_norm_one(grad_act_one)
    input_grad = (grad_residual + input_norm_grad)[None]
    shard_grads = (
        lax.psum_scatter(grad_query, "seq", scatter_dimension=0, tiled=True),
        lax.psum_scatter(grad_key, "seq", scatter_dimension=0, tiled=True),
        lax.psum_scatter(grad_value, "seq", scatter_dimension=0, tiled=True),
        lax.psum_scatter(grad_out, "seq", scatter_dimension=0, tiled=True),
        lax.psum_scatter(grad_gate, "seq", scatter_dimension=0, tiled=True),
        lax.psum_scatter(grad_up, "seq", scatter_dimension=0, tiled=True),
        lax.psum_scatter(grad_down, "seq", scatter_dimension=0, tiled=True),
        lax.psum_scatter(grad_gain_one, "seq", scatter_dimension=0, tiled=True),
        lax.psum_scatter(grad_gain_two, "seq", scatter_dimension=0, tiled=True),
    )
    gradients = lax.psum(
        (
            shard_grads[0],
            shard_grads[1],
            shard_grads[2],
            shard_grads[3],
            shard_grads[4],
            shard_grads[5],
            shard_grads[6],
            shard_grads[7],
            shard_grads[8],
        ),
        "dp",
    )
    squares = jnp.float32(0.0)
    for gradient in gradients:
        squares = squares + jnp.sum(gradient * gradient)
    gradient_norm = jnp.sqrt(lax.psum(squares, "seq"))
    clip_factor = jnp.minimum(1.0, jnp.sqrt(jnp.float32(PARAMS)) / (gradient_norm + 1e-06))
    momenta = [
        momentum_beta * moment + clip_factor * gradient
        for moment, gradient in zip(moments, gradients)
    ]
    updated = [
        master * (1.0 - learning_rate * weight_decay) - learning_rate * momentum
        for master, momentum in zip(masters, momenta)
    ]
    return (
        output,
        input_grad,
        momenta[0],
        momenta[1],
        momenta[2],
        momenta[3],
        momenta[4],
        momenta[5],
        momenta[6],
        momenta[7],
        momenta[8],
        updated[0],
        updated[1],
        updated[2],
        updated[3],
        updated[4],
        updated[5],
        updated[6],
        updated[7],
        updated[8],
        gradient_norm,
    )


BF = jnp.bfloat16
F32 = jnp.float32


def swap_x(value):
    return lax.ppermute(value, "seq", [(i, i ^ 1) for i in range(4)])


def swap_y(value):
    return lax.ppermute(value, "seq", [(i, i ^ 2) for i in range(4)])


def swap_diagonal(value):
    return lax.ppermute(value, "seq", [(i, i ^ 3) for i in range(4)])


def swap_core(value):
    return lax.ppermute(value, "dp", [(i, i ^ 1) for i in range(8)])


def move_up(value):
    return lax.ppermute(value, "dp", [(i, i + 2) for i in range(6)])


def move_down(value):
    return lax.ppermute(value, "dp", [(i + 2, i) for i in range(6)])


def dot(left, right):
    return jnp.dot(left, right, preferred_element_type=F32)


def dot_rows(left, right):
    return lax.dot_general(left, right, (((0,), (0,)), ((), ())), preferred_element_type=F32)


def dot_transposed(left, right):
    return lax.dot_general(left, right, (((1,), (1,)), ((), ())), preferred_element_type=F32)


def gather_plane(first, second):
    x_first = swap_x(first)
    y_first = swap_y(first)
    x_second = swap_x(second)
    y_second = swap_y(second)
    d_first = swap_x(y_first)
    d_second = swap_y(x_second)
    return (x_first, x_second), (y_first, y_second), (d_first, d_second)


def scatter_plane(own, for_x, for_y, for_d):
    y_relay = swap_x(for_d[0].astype(BF))
    x_relay = swap_y(for_d[1].astype(BF))
    x_first = swap_x(for_x[0].astype(BF))
    y_second = swap_y(for_y[1].astype(BF))
    x_second = swap_x((for_x[1] + x_relay).astype(BF))
    y_first = swap_y((for_y[0] + y_relay).astype(BF))
    return own[0] + x_first + y_first, own[1] + x_second + y_second


def halves(value):
    middle = value.shape[0] // 2
    return value[:middle], value[middle:]


def scatter_line(chunks, place):
    def pick(number):
        return lax.dynamic_index_in_dim(chunks, jnp.clip(number, 0, 3), 0, keepdims=False)

    upward = downward = None
    for step in (1, 2, 3):
        up_part = pick(place + 4 - step).astype(F32)
        down_part = pick(place - 4 + step).astype(F32)
        if upward is not None:
            up_part = up_part + upward
            down_part = down_part + downward
        upward = move_up(up_part.astype(BF))
        downward = move_down(down_part.astype(BF))
    return pick(place).astype(F32) + upward + downward


def gather_line(own):
    below, above = [own], [own]
    for _ in range(3):
        below.append(move_up(below[-1]))
        above.append(move_down(above[-1]))
    return [own] + [above[j] + below[4 - j] for j in (1, 2, 3)]


def sum_everywhere(value):
    value = value + swap_core(value)
    value = value + swap_x(value)
    value = value + swap_y(value)
    value = value + lax.ppermute(value, "dp", [(i, i ^ 2) for i in range(8)])
    return value + lax.ppermute(value, "dp", [(i, i ^ 4) for i in range(8)])


def natural(blocks, own_place):
    result = jnp.stack(blocks)
    order = jnp.arange(4, dtype=jnp.int32) ^ own_place
    return result[order]


def put_rows(target, block, row):
    return lax.dynamic_update_slice(target, block, (row, jnp.int32(0)))


def fast_device(
    tokens,
    cotangent,
    picture_starts,
    query_weight,
    key_matrix,
    value_matrix,
    out_weight,
    gate_weight,
    up_weight,
    down_weight,
    attention_gain,
    feed_gain,
    query_moment,
    key_velocity,
    value_velocity,
    out_moment,
    gate_moment,
    up_moment,
    down_moment,
    attention_moment,
    feed_moment,
):
    masters = (
        query_weight,
        key_matrix,
        value_matrix,
        out_weight,
        gate_weight,
        up_weight,
        down_weight,
        attention_gain,
        feed_gain,
    )
    moments = (
        query_moment,
        key_velocity,
        value_velocity,
        out_moment,
        gate_moment,
        up_moment,
        down_moment,
        attention_moment,
        feed_moment,
    )
    me = lax.axis_index("seq")
    line = lax.axis_index("dp") // 2
    core = lax.axis_index("dp") % 2
    rows = tokens.shape[1]
    width = tokens.shape[2]
    shard = query_weight.shape[0]
    half = shard // 2
    hidden_own = down_weight.shape[0]
    kv_width = KEY_VALUE_HEADS * HEAD_SIZE
    group = QUERY_HEAD_COUNT // KEY_VALUE_HEADS
    places = [me, me ^ 1, me ^ 2, me ^ 3]

    gains = jnp.stack([attention_gain, feed_gain]).astype(BF)
    gains_x = swap_x(gains)
    gains_y = swap_y(gains)
    gains_d = swap_x(gains_y)
    all_gains = natural([gains, gains_x, gains_y, gains_d], me)
    gain_one = all_gains[:, 0].reshape(width).astype(F32)
    gain_two = all_gains[:, 1].reshape(width).astype(F32)

    def fetch_rows(shard_value):
        mine = lax.dynamic_slice_in_dim(shard_value, core * half, half, 0)
        pieces = gather_plane(*halves(mine))
        fetched = jnp.stack([jnp.concatenate(pair) for pair in pieces])
        other = swap_core(fetched)
        full = jnp.zeros((4 * shard, shard_value.shape[1]), BF)
        full = put_rows(full, shard_value, me * shard)
        for j in range(3):
            start = places[j + 1] * shard
            full = put_rows(full, fetched[j], start + core * half)
            full = put_rows(full, other[j], start + (1 - core) * half)
        return full

    shard_qkv = jnp.concatenate([query_weight, key_matrix, value_matrix], axis=1).astype(BF)
    full_qkv = fetch_rows(shard_qkv)
    full_out = fetch_rows(out_weight.astype(BF))

    shard_gate = gate_weight.astype(BF)
    shard_up = up_weight.astype(BF)

    def columns_for(place, first, count):
        at = (first, place * hidden_own)
        size = (count, hidden_own)
        return jnp.concatenate(
            [lax.dynamic_slice(shard_gate, at, size), lax.dynamic_slice(shard_up, at, size)], axis=1
        )

    sent = [columns_for(place, core * half, half) for place in places[1:]]
    fetched = [swap_x(sent[0]), swap_y(sent[1]), swap_diagonal(sent[2])]
    other = [swap_core(block) for block in fetched]
    full_gu = jnp.zeros((width, 2 * hidden_own), BF)
    full_gu = put_rows(full_gu, columns_for(me, jnp.int32(0), shard), me * shard)
    for j in range(3):
        start = places[j + 1] * shard
        full_gu = put_rows(full_gu, fetched[j], start + core * half)
        full_gu = put_rows(full_gu, other[j], start + (1 - core) * half)
    own_down = down_weight.astype(BF)

    token_positions = me * rows + jnp.arange(rows, dtype=jnp.int32)
    starts = picture_starts[0]
    query_piece = piece_number(token_positions, starts)
    key_positions = jnp.concatenate(
        [place * rows + jnp.arange(rows, dtype=jnp.int32) for place in places]
    )
    key_pieces = piece_number(key_positions, starts)
    allowed = visible(token_positions, query_piece, key_positions, key_pieces)

    upstream_low = cotangent[0]
    pieces = gather_plane(*halves(upstream_low))
    every_upstream = jnp.concatenate([upstream_low] + [part for pair in pieces for part in pair])

    layer_input = tokens[0].astype(F32)
    normed_one, pull_norm_one = jax.vjp(rms_scale, layer_input, gain_one)
    first_activation = normed_one.astype(BF)
    linear = dot(first_activation, full_qkv)
    rotation = partial(apply_rotary, token_positions=token_positions)
    heads_qk = QUERY_HEAD_COUNT + KEY_VALUE_HEADS
    rotated, pull_rotation = jax.vjp(
        rotation, linear[:, : width + kv_width].reshape(rows, heads_qk, HEAD_SIZE)
    )
    rotated = rotated.astype(BF)
    query = jnp.transpose(
        rotated[:, :QUERY_HEAD_COUNT].reshape(rows, KEY_VALUE_HEADS, group, HEAD_SIZE), (1, 2, 0, 3)
    ).reshape(KEY_VALUE_HEADS, group * rows, HEAD_SIZE)
    key_value = jnp.concatenate(
        [rotated[:, QUERY_HEAD_COUNT:].reshape(rows, kv_width), linear[:, width + kv_width :].astype(BF)],
        axis=1,
    )
    pieces = gather_plane(*halves(key_value))
    every_kv = jnp.concatenate([key_value] + [part for pair in pieces for part in pair])
    every_kv = jnp.transpose(
        every_kv.reshape(4 * rows, 2, KEY_VALUE_HEADS, HEAD_SIZE), (1, 2, 0, 3)
    )
    keys, values = every_kv[0], every_kv[1]
    mask = jnp.broadcast_to(allowed[None], (group, rows, 4 * rows)).reshape(group * rows, 4 * rows)
    scores = jnp.einsum("hqd,hkd->hqk", query, keys, preferred_element_type=F32)
    exponent = jnp.where(mask[None], jnp.exp(scores * 0.125), 0.0)
    totals = jnp.sum(exponent, axis=-1, keepdims=True)
    exponent_low = exponent.astype(BF)
    attended = (
        jnp.einsum("hqk,hkd->hqd", exponent_low, values, preferred_element_type=F32) / totals
    )

    def by_rows(value):
        value = value.reshape(KEY_VALUE_HEADS, group, rows, HEAD_SIZE)
        return jnp.transpose(value, (2, 0, 1, 3)).reshape(rows, width)

    attention = by_rows(attended).astype(BF)
    residual = layer_input + dot(attention, full_out)
    normed_two, pull_norm_two = jax.vjp(rms_scale, residual, gain_two)
    act_two = normed_two.astype(BF)

    pieces = gather_plane(*halves(act_two))
    every_act = jnp.concatenate([act_two] + [part for pair in pieces for part in pair])
    both = dot(every_act, full_gu)
    hidden_full, pull_swiglu = jax.vjp(swiglu, both[:, :hidden_own], both[:, hidden_own:])
    hidden = hidden_full.astype(BF)
    grad_hidden = dot_transposed(every_upstream, own_down)
    grad_gate_full, grad_up_full = pull_swiglu(grad_hidden)
    both_back = jnp.concatenate([grad_gate_full, grad_up_full], axis=1).astype(BF)
    grad_act = dot_transposed(both_back, full_gu)

    def token_blocks(value):
        return [halves(value[j * rows : (j + 1) * rows]) for j in range(4)]

    grad_act_two = jnp.concatenate(scatter_plane(*token_blocks(grad_act)))
    layer_part = dot(hidden, own_down)
    output = (residual + jnp.concatenate(scatter_plane(*token_blocks(layer_part)))).astype(BF)[None]
    grad_gu = dot_rows(every_act, both_back)
    grad_down = dot_rows(hidden, every_upstream)

    gu_parts = grad_gu.reshape(4, 2, half, 4, 2 * hidden_own // 4)
    gu_keep = lax.dynamic_index_in_dim(gu_parts, core, 1, keepdims=False)
    gu_send = lax.dynamic_index_in_dim(gu_parts, 1 - core, 1, keepdims=False)
    gu_pair = gu_keep + swap_core(gu_send.astype(BF))
    gu_own = scatter_line(jnp.transpose(gu_pair, (2, 0, 1, 3)), line).astype(BF)
    down_parts = grad_down.reshape(2, 4, hidden_own // 8, width)
    down_keep = lax.dynamic_index_in_dim(down_parts, core, 0, keepdims=False)
    down_send = lax.dynamic_index_in_dim(down_parts, 1 - core, 0, keepdims=False)
    down_pair = down_keep + swap_core(down_send.astype(BF))
    down_own = scatter_line(down_pair, line).astype(BF)
    gu_for = [lax.dynamic_index_in_dim(gu_own, place, 0, keepdims=False) for place in places]
    gu_mine = natural(
        [gu_for[0], swap_x(gu_for[1]), swap_y(gu_for[2]), swap_diagonal(gu_for[3])], me
    )

    upstream = upstream_low.astype(F32)
    residual_norm_grad, grad_gain_two = pull_norm_two(grad_act_two)
    grad_residual = upstream + residual_norm_grad
    residual_back = grad_residual.astype(BF)
    grad_out = dot_rows(attention, residual_back)
    attention_back = dot_transposed(residual_back, full_out).astype(BF)
    attention_back = jnp.transpose(
        attention_back.reshape(rows, KEY_VALUE_HEADS, group, HEAD_SIZE), (1, 2, 0, 3)
    ).reshape(KEY_VALUE_HEADS, group * rows, HEAD_SIZE)
    back_full = attention_back.astype(F32)
    scaled_back = (back_full / totals).astype(BF)
    total_back = -jnp.sum(back_full * attended, axis=-1, keepdims=True) / totals
    through = jnp.einsum("hqd,hkd->hqk", scaled_back, values, preferred_element_type=F32)
    score_back = (exponent * (through + total_back)).astype(BF)
    grad_query = by_rows(
        jnp.einsum("hqk,hkd->hqd", score_back, keys, preferred_element_type=F32) * 0.125
    )
    key_part = jnp.einsum("hqk,hqd->hkd", score_back, query, preferred_element_type=F32) * 0.125
    value_part = jnp.einsum("hqk,hqd->hkd", exponent_low, scaled_back, preferred_element_type=F32)
    kv_part = jnp.transpose(jnp.stack([key_part, value_part]), (2, 0, 1, 3)).reshape(
        4 * rows, 2 * kv_width
    )
    kv_own = jnp.concatenate(scatter_plane(*token_blocks(kv_part)))
    turned = jnp.concatenate([grad_query, kv_own[:, :kv_width]], axis=1)
    turned = pull_rotation(turned.reshape(rows, heads_qk, HEAD_SIZE))[0]
    linear_back = jnp.concatenate(
        [turned.reshape(rows, width + kv_width), kv_own[:, kv_width:]], axis=1
    ).astype(BF)
    grad_qkv = dot_rows(first_activation, linear_back)
    grad_act_one = dot_transposed(linear_back, full_qkv)
    input_norm_grad, grad_gain_one = pull_norm_one(grad_act_one)
    input_grad = (grad_residual + input_norm_grad)[None]

    def reduce_rows(gradient):
        columns = gradient.shape[1]
        parts = gradient.reshape(4, 2, half, columns)
        keep = lax.dynamic_index_in_dim(parts, core, 1, keepdims=False)
        send = lax.dynamic_index_in_dim(parts, 1 - core, 1, keepdims=False)
        pair = keep + swap_core(send.astype(BF))
        blocks = [
            halves(lax.dynamic_index_in_dim(pair, place, 0, keepdims=False)) for place in places
        ]
        return jnp.concatenate(scatter_plane(*blocks))

    grad_all = jnp.concatenate([reduce_rows(grad_qkv), reduce_rows(grad_out)], axis=1)
    quarter = grad_all.shape[1] // 4
    chunks = jnp.transpose(grad_all.reshape(half, 4, quarter), (1, 0, 2))
    all_own = scatter_line(chunks, line).astype(BF)

    grad_gains = sum_everywhere(jnp.stack([grad_gain_one, grad_gain_two]))
    squares = (
        jnp.sum(jnp.square(all_own.astype(F32)))
        + jnp.sum(jnp.square(gu_mine.astype(F32)))
        + jnp.sum(jnp.square(down_own.astype(F32)))
    )
    total_squares = sum_everywhere(jnp.broadcast_to(squares, (8, 128)))[0, 0]
    gradient_norm = jnp.sqrt(total_squares + jnp.sum(jnp.square(grad_gains)))
    clip_factor = jnp.minimum(1.0, jnp.sqrt(F32(PARAMS)) / (gradient_norm + 1e-06))

    def whole(own):
        ring = jnp.stack(gather_line(own))
        ring = jnp.concatenate([ring, ring])
        ordered = lax.dynamic_slice_in_dim(ring, 4 - line, 4, 0)
        other = swap_core(ordered)
        first = jnp.where(core == 0, ordered, other)
        second = jnp.where(core == 0, other, ordered)
        return jnp.stack([first, second])

    attention_whole = jnp.transpose(whole(all_own), (0, 2, 1, 3)).reshape(shard, 4 * quarter)
    gu_whole = whole(gu_mine)
    piece_width = gu_whole.shape[-1]
    gu_whole = jnp.transpose(
        gu_whole.reshape(2, 2, 2, 4, half, piece_width), (1, 0, 4, 3, 2, 5)
    ).reshape(2, shard, 8 * piece_width)
    down_whole = whole(down_own).reshape(hidden_own, width)
    own_gains = lax.dynamic_slice_in_dim(grad_gains, me * shard, shard, 1)
    gradients = (
        attention_whole[:, :width],
        attention_whole[:, width : width + kv_width],
        attention_whole[:, width + kv_width : width + 2 * kv_width],
        attention_whole[:, width + 2 * kv_width :],
        gu_whole[0],
        gu_whole[1],
        down_whole,
        own_gains[0],
        own_gains[1],
    )
    momenta = [
        momentum_beta * moment + clip_factor * gradient
        for moment, gradient in zip(moments, gradients)
    ]
    updated = [
        master * (1.0 - learning_rate * weight_decay) - learning_rate * momentum
        for master, momentum in zip(masters, momenta)
    ]
    return (output, input_grad, *momenta, *updated, gradient_norm)


def solution(mesh):
    fits = mesh.shape["seq"] == 4 and mesh.shape["dp"] == 8
    body = fast_device if fits else per_device
    return jax.shard_map(
        body,
        mesh=mesh,
        in_specs=(
            P("dp", "seq", None),
            P("dp", "seq", None),
            P("dp", None),
            P("seq", None),
            P("seq", None),
            P("seq", None),
            P("seq", None),
            P("seq", None),
            P("seq", None),
            P("seq", None),
            P("seq"),
            P("seq"),
            P("seq", None),
            P("seq", None),
            P("seq", None),
            P("seq", None),
            P("seq", None),
            P("seq", None),
            P("seq", None),
            P("seq"),
            P("seq"),
        ),
        out_specs=(
            P("dp", "seq", None),
            P("dp", "seq", None),
            P("seq", None),
            P("seq", None),
            P("seq", None),
            P("seq", None),
            P("seq", None),
            P("seq", None),
            P("seq", None),
            P("seq"),
            P("seq"),
            P("seq", None),
            P("seq", None),
            P("seq", None),
            P("seq", None),
            P("seq", None),
            P("seq", None),
            P("seq", None),
            P("seq"),
            P("seq"),
            P(),
        ),
        check_vma=False,
    )
```

```python
from functools import partial
import math

import jax
import jax.numpy as jnp
from jax import lax
from jax.experimental import pallas as pl
from jax.experimental.pallas import tpu as pltpu
from jax.sharding import PartitionSpec as P

QUERY_HEAD_COUNT = 18
KEY_VALUE_HEADS = 6
HEAD_SIZE = 64
PIECE = 256
PARAMS = 14158080


learning_rate = 0.25
weight_decay = 0.1
momentum_beta = 0.5


def rms_scale(values, scaling):
    return values * lax.rsqrt(jnp.mean(values * values, axis=-1, keepdims=True) + 1e-05) * scaling


def apply_rotary(values, token_positions):
    half_width = values.shape[-1] // 2
    frequency = 10000.0 ** (-jnp.arange(half_width, dtype=jnp.float32) / half_width)
    angles = token_positions.astype(jnp.float32)[:, None] * frequency[None, :]
    cosine = jnp.cos(angles)[:, None, :]
    sine_part = jnp.sin(angles)[:, None, :]
    leading = values[..., :half_width]
    trailing = values[..., half_width:]
    return jnp.concatenate(
        [leading * cosine - trailing * sine_part, trailing * cosine + leading * sine_part], axis=-1
    )


def swiglu(gate_values, up_values):
    return jax.nn.silu(gate_values) * up_values


def piece_number(token_positions, starts):
    inside = (token_positions[:, None] >= starts[None, :]) & (
        token_positions[:, None] < starts[None, :] + PIECE
    )
    numbers = jnp.arange(starts.shape[0], dtype=jnp.int32) + 1
    return jnp.sum(jnp.where(inside, numbers[None, :], 0), axis=1) - 1


def visible(query_position, query_piece, key_position, key_piece):
    earlier = key_position[None, :] <= query_position[:, None]
    same_piece = (query_piece[:, None] == key_piece[None, :]) & (query_piece[:, None] >= 0)
    return earlier | same_piece


def per_device(
    tokens,
    cotangent,
    picture_starts,
    query_weight,
    key_matrix,
    value_matrix,
    out_weight,
    gate_weight,
    up_weight,
    down_weight,
    attention_gain,
    feed_gain,
    query_moment,
    key_velocity,
    value_velocity,
    out_moment,
    gate_moment,
    up_moment,
    down_moment,
    attention_moment,
    feed_moment,
):
    masters = (
        query_weight,
        key_matrix,
        value_matrix,
        out_weight,
        gate_weight,
        up_weight,
        down_weight,
        attention_gain,
        feed_gain,
    )
    moments = (
        query_moment,
        key_velocity,
        value_velocity,
        out_moment,
        gate_moment,
        up_moment,
        down_moment,
        attention_moment,
        feed_moment,
    )
    shard_query = query_weight.astype(jnp.bfloat16)
    shard_key = key_matrix.astype(jnp.bfloat16)
    shard_value = value_matrix.astype(jnp.bfloat16)
    shard_out = out_weight.astype(jnp.bfloat16)
    shard_gate = gate_weight.astype(jnp.bfloat16)
    shard_up = up_weight.astype(jnp.bfloat16)
    shard_down = down_weight.astype(jnp.bfloat16)
    shard_gain_one = attention_gain.astype(jnp.bfloat16)
    shard_gain_two = feed_gain.astype(jnp.bfloat16)
    gathered = (
        lax.all_gather(shard_query, "seq", axis=0, tiled=True),
        lax.all_gather(shard_key, "seq", axis=0, tiled=True),
        lax.all_gather(shard_value, "seq", axis=0, tiled=True),
        lax.all_gather(shard_out, "seq", axis=0, tiled=True),
        lax.all_gather(shard_gate, "seq", axis=0, tiled=True),
        lax.all_gather(shard_up, "seq", axis=0, tiled=True),
        lax.all_gather(shard_down, "seq", axis=0, tiled=True),
        lax.all_gather(shard_gain_one, "seq", axis=0, tiled=True),
        lax.all_gather(shard_gain_two, "seq", axis=0, tiled=True),
    )
    full_query, complete_key, complete_value, full_out, full_gate, full_up, full_down = gathered[:7]
    gain_one = gathered[7].astype(jnp.float32)
    gain_two = gathered[8].astype(jnp.float32)
    group_size = lax.axis_size("seq")
    local_rows = tokens.shape[1]
    sequence_length = local_rows * group_size
    heads_per_group = QUERY_HEAD_COUNT // KEY_VALUE_HEADS
    token_positions = lax.axis_index("seq") * local_rows + jnp.arange(local_rows, dtype=jnp.int32)
    starts = picture_starts[0]
    query_piece = piece_number(token_positions, starts)
    key_positions = jnp.arange(sequence_length, dtype=jnp.int32)
    key_pieces = piece_number(key_positions, starts)
    layer_input = tokens[0].astype(jnp.float32)
    normed_one, pull_norm_one = jax.vjp(rms_scale, layer_input, gain_one)
    first_activation = normed_one.astype(jnp.bfloat16)
    rotation = partial(apply_rotary, token_positions=token_positions)
    query_linear = jnp.dot(
        first_activation, full_query, preferred_element_type=jnp.float32
    ).reshape(local_rows, QUERY_HEAD_COUNT, HEAD_SIZE)
    rotated_query, pull_query = jax.vjp(rotation, query_linear)
    query_reduced = rotated_query.astype(jnp.bfloat16).reshape(
        local_rows, KEY_VALUE_HEADS, heads_per_group, HEAD_SIZE
    )
    key_linear = jnp.dot(
        first_activation, complete_key, preferred_element_type=jnp.float32
    ).reshape(local_rows, KEY_VALUE_HEADS, HEAD_SIZE)
    rotated_key, key_pullback = jax.vjp(rotation, key_linear)
    key_reduced = rotated_key.astype(jnp.bfloat16).reshape(local_rows, KEY_VALUE_HEADS * HEAD_SIZE)
    value_reduced = jnp.dot(
        first_activation, complete_value, preferred_element_type=jnp.float32
    ).astype(jnp.bfloat16)
    every_key_row, every_value_row = (
        lax.all_gather(key_reduced, "seq", axis=0, tiled=True),
        lax.all_gather(value_reduced, "seq", axis=0, tiled=True),
    )
    every_key_row = every_key_row.reshape(sequence_length, KEY_VALUE_HEADS, HEAD_SIZE)
    every_value_row = every_value_row.reshape(sequence_length, KEY_VALUE_HEADS, HEAD_SIZE)
    rows_per_block = math.gcd(512, sequence_length)
    count_of_blocks = sequence_length // rows_per_block
    last_position = token_positions[local_rows - 1]
    last_piece = query_piece[local_rows - 1]

    def needed(number):
        first_row = number * rows_per_block
        return (first_row <= last_position) | (last_piece >= 0) & (
            key_pieces[first_row] == last_piece
        )

    def block_scores(number):
        first_row = number * rows_per_block
        key_block = lax.dynamic_slice_in_dim(every_key_row, first_row, rows_per_block, 0)
        value_block = lax.dynamic_slice_in_dim(every_value_row, first_row, rows_per_block, 0)
        allowed = visible(
            token_positions,
            query_piece,
            lax.dynamic_slice_in_dim(key_positions, first_row, rows_per_block, 0),
            lax.dynamic_slice_in_dim(key_pieces, first_row, rows_per_block, 0),
        )
        raw_scores = jnp.einsum(
            "qhgd,khd->hgqk", query_reduced, key_block, preferred_element_type=jnp.float32
        )
        exponent = jnp.where(allowed[None, None], jnp.exp(raw_scores * 0.125), 0.0)
        return (key_block, value_block, exponent)

    def unchanged(current):
        return current

    def forward_step(number, running):

        def forward_compute(current):
            summed, totals = current
            key_block, value_block, exponent = block_scores(number)
            summed = summed + jnp.einsum(
                "hgqk,khd->hgqd",
                exponent.astype(jnp.bfloat16),
                value_block,
                preferred_element_type=jnp.float32,
            )
            return (summed, totals + jnp.sum(exponent, axis=-1))

        return lax.cond(needed(number), forward_compute, unchanged, running)

    initial_sum = jnp.zeros((KEY_VALUE_HEADS, heads_per_group, local_rows, HEAD_SIZE), jnp.float32)
    initial_total = jnp.zeros((KEY_VALUE_HEADS, heads_per_group, local_rows), jnp.float32)
    summed, totals = lax.fori_loop(0, count_of_blocks, forward_step, (initial_sum, initial_total))
    attended = summed / totals[..., None]
    attention = (
        jnp.transpose(attended, (2, 0, 1, 3))
        .reshape(local_rows, QUERY_HEAD_COUNT * HEAD_SIZE)
        .astype(jnp.bfloat16)
    )
    residual = layer_input + jnp.dot(attention, full_out, preferred_element_type=jnp.float32)
    normed_two, pull_norm_two = jax.vjp(rms_scale, residual, gain_two)
    act_two = normed_two.astype(jnp.bfloat16)
    gate_linear = jnp.dot(act_two, full_gate, preferred_element_type=jnp.float32)
    up_linear = jnp.dot(act_two, full_up, preferred_element_type=jnp.float32)
    hidden_full, pull_swiglu = jax.vjp(swiglu, gate_linear, up_linear)
    hidden = hidden_full.astype(jnp.bfloat16)
    layer_out = residual + jnp.dot(hidden, full_down, preferred_element_type=jnp.float32)
    output = layer_out.astype(jnp.bfloat16)[None]
    upstream = cotangent[0].astype(jnp.float32)
    upstream_low = upstream.astype(jnp.bfloat16)
    grad_down = jnp.einsum("nf,nd->fd", hidden, upstream_low, preferred_element_type=jnp.float32)
    grad_hidden = jnp.einsum(
        "nd,fd->nf", upstream_low, full_down, preferred_element_type=jnp.float32
    )
    grad_gate_full, grad_up_full = pull_swiglu(grad_hidden)
    gate_back = grad_gate_full.astype(jnp.bfloat16)
    up_back = grad_up_full.astype(jnp.bfloat16)
    grad_gate = jnp.einsum("nd,nf->df", act_two, gate_back, preferred_element_type=jnp.float32)
    grad_up = jnp.einsum("nd,nf->df", act_two, up_back, preferred_element_type=jnp.float32)
    grad_act_two = jnp.einsum(
        "nf,df->nd", gate_back, full_gate, preferred_element_type=jnp.float32
    ) + jnp.einsum("nf,df->nd", up_back, full_up, preferred_element_type=jnp.float32)
    residual_norm_grad, grad_gain_two = pull_norm_two(grad_act_two)
    grad_residual = upstream + residual_norm_grad
    residual_back = grad_residual.astype(jnp.bfloat16)
    grad_out = jnp.einsum("nk,nd->kd", attention, residual_back, preferred_element_type=jnp.float32)
    attention_pullback = jnp.einsum(
        "nd,kd->nk", residual_back, full_out, preferred_element_type=jnp.float32
    ).astype(jnp.bfloat16)
    attention_pullback = jnp.transpose(
        attention_pullback.reshape(local_rows, KEY_VALUE_HEADS, heads_per_group, HEAD_SIZE),
        (1, 2, 0, 3),
    )
    back_full = attention_pullback.astype(jnp.float32)
    scaled_back = (back_full / totals[..., None]).astype(jnp.bfloat16)
    total_back = -jnp.sum(back_full * attended, axis=-1) / totals
    query_heads = jnp.transpose(query_reduced, (1, 2, 0, 3))

    def backward_step(number, running):

        def backward_compute(current):
            grad_query_sum, key_gradient_rows, value_gradient_rows = current
            first_row = number * rows_per_block
            key_block, value_block, exponent = block_scores(number)
            through = jnp.einsum(
                "hgqd,khd->hgqk", scaled_back, value_block, preferred_element_type=jnp.float32
            )
            score_back = (exponent * (through + total_back[..., None])).astype(jnp.bfloat16)
            grad_query_sum = (
                grad_query_sum
                + jnp.einsum(
                    "hgqk,khd->hgqd", score_back, key_block, preferred_element_type=jnp.float32
                )
                * 0.125
            )
            key_part = (
                jnp.einsum(
                    "hgqk,hgqd->khd", score_back, query_heads, preferred_element_type=jnp.float32
                )
                * 0.125
            )
            value_part = jnp.einsum(
                "hgqk,hgqd->khd",
                exponent.astype(jnp.bfloat16),
                scaled_back,
                preferred_element_type=jnp.float32,
            )
            key_gradient_rows = lax.dynamic_update_slice_in_dim(
                key_gradient_rows, key_part, first_row, 0
            )
            value_gradient_rows = lax.dynamic_update_slice_in_dim(
                value_gradient_rows, value_part, first_row, 0
            )
            return (grad_query_sum, key_gradient_rows, value_gradient_rows)

        return lax.cond(needed(number), backward_compute, unchanged, running)

    initial_query = jnp.zeros(
        (KEY_VALUE_HEADS, heads_per_group, local_rows, HEAD_SIZE), jnp.float32
    )
    initial_keys = jnp.zeros((sequence_length, KEY_VALUE_HEADS, HEAD_SIZE), jnp.float32)
    grad_query_sum, key_gradient_rows, value_gradient_rows = lax.fori_loop(
        0, count_of_blocks, backward_step, (initial_query, initial_keys, initial_keys)
    )
    local_key_rows, value_own = (
        lax.psum_scatter(
            key_gradient_rows.reshape(sequence_length, KEY_VALUE_HEADS * HEAD_SIZE),
            "seq",
            scatter_dimension=0,
            tiled=True,
        ),
        lax.psum_scatter(
            value_gradient_rows.reshape(sequence_length, KEY_VALUE_HEADS * HEAD_SIZE),
            "seq",
            scatter_dimension=0,
            tiled=True,
        ),
    )
    key_back = (
        key_pullback(local_key_rows.reshape(local_rows, KEY_VALUE_HEADS, HEAD_SIZE))[0]
        .reshape(local_rows, KEY_VALUE_HEADS * HEAD_SIZE)
        .astype(jnp.bfloat16)
    )
    query_rot_grad = jnp.transpose(grad_query_sum, (2, 0, 1, 3)).reshape(
        local_rows, QUERY_HEAD_COUNT, HEAD_SIZE
    )
    query_back = (
        pull_query(query_rot_grad)[0]
        .reshape(local_rows, QUERY_HEAD_COUNT * HEAD_SIZE)
        .astype(jnp.bfloat16)
    )
    value_back = value_own.astype(jnp.bfloat16)
    grad_query = jnp.einsum(
        "nd,nk->dk", first_activation, query_back, preferred_element_type=jnp.float32
    )
    grad_key = jnp.einsum(
        "nd,nk->dk", first_activation, key_back, preferred_element_type=jnp.float32
    )
    grad_value = jnp.einsum(
        "nd,nk->dk", first_activation, value_back, preferred_element_type=jnp.float32
    )
    grad_act_one = jnp.einsum(
        "nk,dk->nd", query_back, full_query, preferred_element_type=jnp.float32
    )
    grad_act_one = grad_act_one + jnp.einsum(
        "nk,dk->nd", key_back, complete_key, preferred_element_type=jnp.float32
    )
    grad_act_one = grad_act_one + jnp.einsum(
        "nk,dk->nd", value_back, complete_value, preferred_element_type=jnp.float32
    )
    input_norm_grad, grad_gain_one = pull_norm_one(grad_act_one)
    input_grad = (grad_residual + input_norm_grad)[None]
    shard_grads = (
        lax.psum_scatter(grad_query, "seq", scatter_dimension=0, tiled=True),
        lax.psum_scatter(grad_key, "seq", scatter_dimension=0, tiled=True),
        lax.psum_scatter(grad_value, "seq", scatter_dimension=0, tiled=True),
        lax.psum_scatter(grad_out, "seq", scatter_dimension=0, tiled=True),
        lax.psum_scatter(grad_gate, "seq", scatter_dimension=0, tiled=True),
        lax.psum_scatter(grad_up, "seq", scatter_dimension=0, tiled=True),
        lax.psum_scatter(grad_down, "seq", scatter_dimension=0, tiled=True),
        lax.psum_scatter(grad_gain_one, "seq", scatter_dimension=0, tiled=True),
        lax.psum_scatter(grad_gain_two, "seq", scatter_dimension=0, tiled=True),
    )
    gradients = lax.psum(
        (
            shard_grads[0],
            shard_grads[1],
            shard_grads[2],
            shard_grads[3],
            shard_grads[4],
            shard_grads[5],
            shard_grads[6],
            shard_grads[7],
            shard_grads[8],
        ),
        "dp",
    )
    squares = jnp.float32(0.0)
    for gradient in gradients:
        squares = squares + jnp.sum(gradient * gradient)
    gradient_norm = jnp.sqrt(lax.psum(squares, "seq"))
    clip_factor = jnp.minimum(1.0, jnp.sqrt(jnp.float32(PARAMS)) / (gradient_norm + 1e-06))
    momenta = [
        momentum_beta * moment + clip_factor * gradient
        for moment, gradient in zip(moments, gradients)
    ]
    updated = [
        master * (1.0 - learning_rate * weight_decay) - learning_rate * momentum
        for master, momentum in zip(masters, momenta)
    ]
    return (
        output,
        input_grad,
        momenta[0],
        momenta[1],
        momenta[2],
        momenta[3],
        momenta[4],
        momenta[5],
        momenta[6],
        momenta[7],
        momenta[8],
        updated[0],
        updated[1],
        updated[2],
        updated[3],
        updated[4],
        updated[5],
        updated[6],
        updated[7],
        updated[8],
        gradient_norm,
    )


BF = jnp.bfloat16
F32 = jnp.float32


def swap_x(value):
    return lax.ppermute(value, "seq", [(i, i ^ 1) for i in range(4)])


def swap_y(value):
    return lax.ppermute(value, "seq", [(i, i ^ 2) for i in range(4)])


def swap_diagonal(value):
    return lax.ppermute(value, "seq", [(i, i ^ 3) for i in range(4)])


def swap_core(value):
    return lax.ppermute(value, "dp", [(i, i ^ 1) for i in range(8)])


def move_up(value):
    return lax.ppermute(value, "dp", [(i, i + 2) for i in range(6)])


def move_down(value):
    return lax.ppermute(value, "dp", [(i + 2, i) for i in range(6)])


def gather_plane(value):
    middle = value.shape[0] // 2
    from_x = swap_x(value)
    from_y = swap_y(value)
    from_d = jnp.concatenate([swap_x(from_y[:middle]), swap_y(from_x[middle:])])
    return from_x, from_y, from_d


def scatter_plane(own, for_x, for_y, for_d):
    from_x = swap_x(for_x.astype(BF))
    from_y = swap_y(for_y.astype(BF))
    from_d = swap_diagonal(for_d.astype(BF))
    return own.astype(F32) + from_x + from_y + from_d


def swap_near(value):
    return lax.ppermute(value, "dp", [(i, i ^ 2) for i in range(8)])


def swap_far(value):
    return lax.ppermute(value, "dp", [(i, i ^ 4) for i in range(8)])


def after(value, other):
    return lax.optimization_barrier((value, other))


def index_array(*numbers):
    return jnp.stack([jnp.asarray(number, jnp.int32) for number in numbers])


VMEM_LIMIT = 50 * 1024 * 1024
COLUMNS = 384


def whole(shape):
    return pl.BlockSpec(shape, lambda *_: (0,) * len(shape))


ANY = pl.BlockSpec(memory_space=pl.ANY)
SCALARS = pl.BlockSpec(memory_space=pltpu.SMEM)


def params():
    return pltpu.CompilerParams(vmem_limit_bytes=VMEM_LIMIT)


def cost(flops, transferred):
    return pl.CostEstimate(flops=flops // 1000, bytes_accessed=transferred // 1000, transcendentals=0)


def start_rows(target, blocks, info, semaphores):
    own, fetched, other = blocks[0], blocks[1:4], blocks[4:7]
    shard, half = own.shape[0], own.shape[0] // 2
    copies = [(own, info[0] * shard, shard)]
    for j in range(3):
        first = (info[0] ^ (j + 1)) * shard
        copies.append((fetched[j], first + info[2] * half, half))
        copies.append((other[j], first + (1 - info[2]) * half, half))
    started = []
    for j, (source, row, count) in enumerate(copies):
        row = pl.multiple_of(row, 16)
        copy = pltpu.make_async_copy(source, target.at[pl.ds(row, count)], semaphores.at[j])
        copy.start()
        started.append(copy)
    return started


def partners(value):
    lanes = value.shape[1]
    low = lax.broadcasted_iota(jnp.int32, value.shape, 1) % HEAD_SIZE < HEAD_SIZE // 2
    return jnp.where(low, pltpu.roll(value, lanes - 32, 1), pltpu.roll(value, 32, 1))


def rotate(value, cosine, sine):
    return value * cosine + partners(value) * sine


def transposed(left, right):
    return lax.dot_general(left, right, (((1,), (1,)), ((), ())), preferred_element_type=F32)


def row_mean(value):
    return jnp.mean(value, axis=-1, keepdims=True)


def project_kernel(info, x, gain, cosine, sine, *refs):
    blocks, (query, key_value, act), (weight, semaphores) = refs[:7], refs[7:10], refs[10:]
    copies = start_rows(weight, blocks, info, semaphores)
    values = x[...].astype(F32)
    normed = values * lax.rsqrt(row_mean(values * values) + 1e-05) * gain[...]
    low = normed.astype(BF)
    act[...] = low
    cos = jnp.concatenate([cosine[...]] * 3, axis=1)
    sin = jnp.concatenate([sine[...]] * 3, axis=1)
    for copy in copies:
        copy.wait()
    for j in range(5):
        part = jnp.dot(
            low, weight[:, j * COLUMNS : (j + 1) * COLUMNS], preferred_element_type=F32
        )
        if j < 4:
            part = rotate(part, cos, sin)
        part = part.astype(BF)
        if j < 3:
            query[:, j * COLUMNS : (j + 1) * COLUMNS] = part * 0.125
        else:
            key_value[:, (j - 3) * COLUMNS : (j - 2) * COLUMNS] = part


def project(info, x, gain, cosine, sine, blocks):
    rows, width = x.shape
    columns = blocks[0].shape[1]
    return pl.pallas_call(
        project_kernel,
        in_specs=[SCALARS, *[whole(a.shape) for a in (x, gain, cosine, sine)]] + [ANY] * 7,
        out_specs=[whole((rows, width)), whole((rows, 2 * COLUMNS)), whole((rows, width))],
        out_shape=[
            jax.ShapeDtypeStruct((rows, width), BF),
            jax.ShapeDtypeStruct((rows, 2 * COLUMNS), BF),
            jax.ShapeDtypeStruct((rows, width), BF),
        ],
        scratch_shapes=[pltpu.VMEM((width, columns), BF), pltpu.SemaphoreType.DMA((7,))],
        compiler_params=params(),
        cost_estimate=cost(2 * rows * width * columns, 8_000_000),
        name="project",
    )(info, x, gain, cosine, sine, *blocks)


def piece_of(positions, starts, count):
    piece = jnp.full(positions.shape, -1, jnp.int32)
    for j in range(count):
        first = starts[j]
        piece = jnp.where((positions >= first) & (positions < first + PIECE), j, piece)
    return piece


def visibility(info, starts, count, rows, keys_first):
    axis = 1 if keys_first else 0
    query_shape = (1, rows) if keys_first else (rows, 1)
    query_at = info[0] * rows + lax.broadcasted_iota(jnp.int32, query_shape, axis)
    query_piece = piece_of(query_at, starts, count)
    biases = []
    for j in range(4):
        key_shape = query_shape[::-1]
        key_at = (info[0] ^ j) * rows + lax.broadcasted_iota(jnp.int32, key_shape, 1 - axis)
        key_piece = piece_of(key_at, starts, count)
        seen = (key_at <= query_at) | ((key_piece == query_piece) & (query_piece >= 0))
        biases.append(jnp.where(seen, 0.0, -1e30).astype(F32))
    return jnp.concatenate(biases, axis=1 - axis)


def attend_kernel(info, starts, query, kv0, kv1, kv2, kv3, x, gain, *refs):
    blocks, outs = refs[:7], refs[7:11]
    attended, attention, residual, act = outs
    weight, every, semaphores = refs[11:]
    rows = x.shape[0]
    copies = start_rows(weight, blocks, info, semaphores)
    for j, block in enumerate((kv0, kv1, kv2, kv3)):
        every[j * rows : (j + 1) * rows, :] = block[...]
    bias = visibility(info, starts, starts.shape[0], rows, False)

    def pair(p, carry):
        at = pl.multiple_of(p * 128, 128)
        keys = every[:, pl.ds(at, 128)]
        values = every[:, pl.ds(COLUMNS + at, 128)]
        queries = query[:, pl.ds(pl.multiple_of(p * COLUMNS, 128), COLUMNS)]
        results = []
        for k in range(2):
            key = keys[:, k * 64 : (k + 1) * 64]
            value = values[:, k * 64 : (k + 1) * 64]
            for h in range(3):
                at = (k * 3 + h) * 64
                scores = transposed(queries[:, at : at + 64], key)
                exponent = jnp.exp(scores + bias)
                total = jnp.sum(exponent, axis=-1, keepdims=True)
                summed = jnp.dot(exponent.astype(BF), value, preferred_element_type=F32)
                results.append(summed / total)
        attended[:, pl.ds(pl.multiple_of(p * COLUMNS, 128), COLUMNS)] = jnp.concatenate(
            results, axis=1
        )
        return carry

    lax.fori_loop(0, 3, pair, 0)
    low = attended[...].astype(BF)
    attention[...] = low
    for copy in copies:
        copy.wait()
    summed = x[...].astype(F32) + jnp.dot(low, weight[...], preferred_element_type=F32)
    residual[...] = summed
    act[...] = (summed * lax.rsqrt(row_mean(summed * summed) + 1e-05) * gain[...]).astype(BF)


def attend(info, starts, query, key_values, x, gain, blocks):
    rows, width = x.shape
    square = whole((rows, width))
    return pl.pallas_call(
        attend_kernel,
        in_specs=[SCALARS, SCALARS, square]
        + [whole(a.shape) for a in key_values]
        + [square, whole(gain.shape)]
        + [ANY] * 7,
        out_specs=[square] * 4,
        out_shape=[jax.ShapeDtypeStruct((rows, width), t) for t in (F32, BF, F32, BF)],
        scratch_shapes=[
            pltpu.VMEM((width, width), BF),
            pltpu.VMEM((4 * rows, 2 * COLUMNS), BF),
            pltpu.SemaphoreType.DMA((7,)),
        ],
        compiler_params=params(),
        cost_estimate=cost(4 * rows * 4 * rows * width * 4, 10_000_000),
        name="attend",
    )(info, starts, query, *key_values, x, gain, *blocks)


def feed_kernel(info, *refs):
    acts, ups, blocks, down = refs[:4], refs[4:8], refs[8:15], refs[15]
    hidden, back, outs = refs[16], refs[17], refs[18:22]
    weight, semaphores = refs[22:]
    rows = acts[0].shape[0]
    units = down.shape[0]
    for copy in start_rows(weight, blocks, info, semaphores):
        copy.wait()
    for j in range(4):
        span = slice(j * rows, (j + 1) * rows)
        both = jnp.dot(acts[j][...], weight[...], preferred_element_type=F32)
        gate, up = both[:, :units], both[:, units:]
        grad = transposed(ups[j][...], down[...])
        logistic = 1.0 / (1.0 + jnp.exp(-gate))
        smooth = gate * logistic
        hidden[span, :] = (smooth * up).astype(BF)
        slope = logistic * (1.0 + gate * (1.0 - logistic))
        back[span, :units] = (grad * up * slope).astype(BF)
        back[span, units:] = (grad * smooth).astype(BF)
        outs[j][...] = transposed(back[span, :], weight[...]).astype(outs[j].dtype)


def feed(info, acts, ups, blocks, down):
    rows, width = acts[0].shape
    units = down.shape[0]
    square = whole((rows, width))
    return pl.pallas_call(
        feed_kernel,
        in_specs=[SCALARS] + [square] * 8 + [ANY] * 7 + [whole(down.shape)],
        out_specs=[whole((4 * rows, units)), whole((4 * rows, 2 * units))] + [square] * 4,
        out_shape=[
            jax.ShapeDtypeStruct((4 * rows, units), BF),
            jax.ShapeDtypeStruct((4 * rows, 2 * units), BF),
            jax.ShapeDtypeStruct((rows, width), F32),
        ]
        + [jax.ShapeDtypeStruct((rows, width), BF)] * 3,
        scratch_shapes=[pltpu.VMEM((width, 2 * units), BF), pltpu.SemaphoreType.DMA((7,))],
        compiler_params=params(),
        cost_estimate=cost(10 * 4 * rows * width * units, 20_000_000),
        name="feed",
    )(info, *acts, *ups, *blocks, down)


def layer_parts_kernel(hidden, down, *outs):
    rows = outs[0].shape[0]
    for j in range(4):
        outs[j][...] = jnp.dot(
            hidden[j * rows : (j + 1) * rows, :], down[...], preferred_element_type=F32
        ).astype(outs[j].dtype)


def layer_parts(hidden, down):
    tokens, units = hidden.shape
    rows, width = tokens // 4, down.shape[1]
    return pl.pallas_call(
        layer_parts_kernel,
        in_specs=[whole(hidden.shape), whole(down.shape)],
        out_specs=[whole((rows, width))] * 4,
        out_shape=[jax.ShapeDtypeStruct((rows, width), t) for t in (F32, BF, BF, BF)],
        compiler_params=params(),
        cost_estimate=cost(2 * tokens * units * width, 8_000_000),
        name="layer_parts",
    )(hidden, down)


def attend_back_kernel(info, starts, g0, g1, g2, g3, upstream, residual, gain, query, *refs):
    kvs, attended, cosine, sine, blocks = refs[:4], refs[4], refs[5], refs[6], refs[7:14]
    grad_residual, grad_low, query_back, outs = refs[14], refs[15], refs[16], refs[17:21]
    weight, every, back, semaphores = refs[21:]
    rows = query.shape[0]
    copies = start_rows(weight, blocks, info, semaphores)
    for j, block in enumerate(kvs):
        every[j * rows : (j + 1) * rows, :] = block[...]
    act_back = g0[...] + g1[...].astype(F32) + g2[...].astype(F32) + g3[...].astype(F32)
    values = residual[...]
    scale = lax.rsqrt(row_mean(values * values) + 1e-05)
    weighted = act_back * gain[...]
    grad = upstream[...].astype(F32) + scale * (
        weighted - values * (scale * scale * row_mean(weighted * values))
    )
    grad_residual[...] = grad
    low = grad.astype(BF)
    grad_low[...] = low
    for copy in copies:
        copy.wait()
    back[...] = transposed(low, weight[...]).astype(BF)
    bias = visibility(info, starts, starts.shape[0], rows, True)
    cos = jnp.concatenate([cosine[...]] * 3, axis=1)
    sin = jnp.concatenate([sine[...]] * 3, axis=1)

    def pair(p, carry):
        at = pl.multiple_of(p * 128, 128)
        wide = pl.ds(pl.multiple_of(p * COLUMNS, 128), COLUMNS)
        keys = every[:, pl.ds(at, 128)]
        values = every[:, pl.ds(COLUMNS + at, 128)]
        queries = query[:, wide]
        backs = back[:, wide].astype(F32).T
        products = backs * attended[:, wide].T
        query_parts, key_parts, value_parts = [], [], []
        for k in range(2):
            key = keys[:, k * 64 : (k + 1) * 64]
            value = values[:, k * 64 : (k + 1) * 64]
            key_t = key.T
            key_sum = value_sum = None
            for h in range(3):
                at = (k * 3 + h) * 64
                one = queries[:, at : at + 64]
                exponent = jnp.exp(transposed(key, one) + bias)
                total = jnp.sum(exponent, axis=0, keepdims=True)
                scaled = (backs[at : at + 64] / total).astype(BF)
                shift = -jnp.sum(products[at : at + 64], axis=0, keepdims=True) / total
                through = jnp.dot(value, scaled, preferred_element_type=F32)
                score = (exponent * (through + shift)).astype(BF)
                query_parts.append(jnp.dot(key_t, score, preferred_element_type=F32))
                key_part = jnp.dot(score, one, preferred_element_type=F32)
                value_part = transposed(exponent.astype(BF), scaled)
                key_sum = key_part if key_sum is None else key_sum + key_part
                value_sum = value_part if value_sum is None else value_sum + value_part
            key_parts.append(key_sum)
            value_parts.append(value_sum)
        turned = jnp.concatenate(query_parts, axis=0).T * 0.125
        query_back[:, wide] = rotate(turned, cos, -sin).astype(BF)
        key_pair = jnp.concatenate(key_parts, axis=1)
        value_pair = jnp.concatenate(value_parts, axis=1)
        for j in range(4):
            span = slice(j * rows, (j + 1) * rows)
            kind = outs[j].dtype
            at = pl.multiple_of(p * 128, 128)
            outs[j][:, pl.ds(at, 128)] = key_pair[span].astype(kind)
            outs[j][:, pl.ds(COLUMNS + at, 128)] = value_pair[span].astype(kind)
        return carry

    lax.fori_loop(0, 3, pair, 0)


def attend_back(info, starts, grads, upstream, residual, gain, query, kvs, attended, trig, blocks):
    rows, width = query.shape
    square = whole((rows, width))
    table = whole(trig[0].shape)
    pair = whole((rows, 2 * COLUMNS))
    return pl.pallas_call(
        attend_back_kernel,
        in_specs=[SCALARS, SCALARS]
        + [square] * 6
        + [whole(gain.shape), square]
        + [pair] * 4
        + [square, table, table]
        + [ANY] * 7,
        out_specs=[square] * 3 + [pair] * 4,
        out_shape=[jax.ShapeDtypeStruct((rows, width), t) for t in (F32, BF, BF)]
        + [jax.ShapeDtypeStruct((rows, 2 * COLUMNS), t) for t in (F32, BF, BF, BF)],
        scratch_shapes=[
            pltpu.VMEM((width, width), BF),
            pltpu.VMEM((4 * rows, 2 * COLUMNS), BF),
            pltpu.VMEM((rows, width), BF),
            pltpu.SemaphoreType.DMA((7,)),
        ],
        compiler_params=params(),
        cost_estimate=cost(10 * rows * 4 * rows * width * 4, 15_000_000),
        name="attend_back",
    )(info, starts, *grads, upstream, residual, gain, query, *kvs, attended, *trig, *blocks)


def split_rows(info, product, keep, send, columns):
    half = keep.shape[1]
    for sr in range(4):
        row = (info[0] ^ sr) * (2 * half)
        kept = pl.multiple_of(row + info[2] * half, 16)
        sent = pl.multiple_of(row + (1 - info[2]) * half, 16)
        keep[sr, :, columns] = product[pl.ds(kept, half), :].astype(BF)
        send[sr, :, columns] = product[pl.ds(sent, half), :].astype(BF)


def query_gradients_kernel(info, act, att, query_back, grad_low, keep, send, product):
    for first, (left, right) in enumerate(((act, query_back), (att, grad_low))):
        left_t = left[...].T
        for j in range(3):
            columns = slice(j * COLUMNS, (j + 1) * COLUMNS)
            product[...] = jnp.dot(left_t, right[:, columns], preferred_element_type=F32)
            at = (first * 3 + j) * COLUMNS
            split_rows(info, product, keep, send, slice(at, at + COLUMNS))


def query_gradients(info, act, att, query_back, grad_low):
    rows, width = act.shape
    half = width // 8
    square = whole((rows, width))
    out = (4, half, 2 * width)
    return pl.pallas_call(
        query_gradients_kernel,
        in_specs=[SCALARS] + [square] * 4,
        out_specs=[whole(out)] * 2,
        out_shape=[jax.ShapeDtypeStruct(out, BF)] * 2,
        scratch_shapes=[pltpu.VMEM((width, COLUMNS), F32)],
        compiler_params=params(),
        cost_estimate=cost(4 * rows * width * width, 9_000_000),
        name="query_gradients",
    )(info, act, att, query_back, grad_low)


def key_gradients_kernel(info, act, p0, p1, p2, p3, cosine, sine, back, keep, send, product):
    summed = p0[...] + p1[...].astype(F32) + p2[...].astype(F32) + p3[...].astype(F32)
    cos = jnp.concatenate([cosine[...]] * 3, axis=1)
    sin = jnp.concatenate([sine[...]] * 3, axis=1)
    back[:, :COLUMNS] = rotate(summed[:, :COLUMNS], cos, -sin).astype(BF)
    back[:, COLUMNS:] = summed[:, COLUMNS:].astype(BF)
    left_t = act[...].T
    for j in range(2):
        columns = slice(j * COLUMNS, (j + 1) * COLUMNS)
        product[...] = jnp.dot(left_t, back[:, columns], preferred_element_type=F32)
        split_rows(info, product, keep, send, columns)


def key_gradients(info, act, parts, trig):
    rows, width = act.shape
    half = width // 8
    out = (4, half, 2 * COLUMNS)
    pair = whole((rows, 2 * COLUMNS))
    table = whole(trig[0].shape)
    return pl.pallas_call(
        key_gradients_kernel,
        in_specs=[SCALARS, whole((rows, width))] + [pair] * 4 + [table, table],
        out_specs=[pair, whole(out), whole(out)],
        out_shape=[jax.ShapeDtypeStruct((rows, 2 * COLUMNS), BF)]
        + [jax.ShapeDtypeStruct(out, BF)] * 2,
        scratch_shapes=[pltpu.VMEM((width, COLUMNS), F32)],
        compiler_params=params(),
        cost_estimate=cost(4 * rows * width * COLUMNS, 5_000_000),
        name="key_gradients",
    )(info, act, *parts, *trig)


def input_back_kernel(info, query_back, key_back, x, gain, grad_residual, *refs):
    blocks, out, (weight, semaphores) = refs[:7], refs[7], refs[8:]
    width = x.shape[1]
    for copy in start_rows(weight, blocks, info, semaphores):
        copy.wait()
    act_back = transposed(query_back[...], weight[:, :width])
    act_back = act_back + transposed(key_back[...], weight[:, width:])
    values = x[...].astype(F32)
    scale = lax.rsqrt(row_mean(values * values) + 1e-05)
    weighted = act_back * gain[...]
    out[...] = grad_residual[...] + scale * (
        weighted - values * (scale * scale * row_mean(weighted * values))
    )


def input_back(info, query_back, key_back, x, gain, grad_residual, blocks):
    rows, width = x.shape
    square = whole((rows, width))
    columns = blocks[0].shape[1]
    return pl.pallas_call(
        input_back_kernel,
        in_specs=[SCALARS, square, whole(key_back.shape), square, whole(gain.shape), square]
        + [ANY] * 7,
        out_specs=square,
        out_shape=jax.ShapeDtypeStruct((rows, width), F32),
        scratch_shapes=[pltpu.VMEM((width, columns), BF), pltpu.SemaphoreType.DMA((7,))],
        compiler_params=params(),
        cost_estimate=cost(2 * rows * width * columns, 9_000_000),
        name="input_back",
    )(info, query_back, key_back, x, gain, grad_residual, *blocks)


def feed_gradients_kernel(info, a0, a1, a2, a3, back, hidden, u0, u1, u2, u3, out, act_t, hid_t, acc):
    rows = a0.shape[0]
    half = a0.shape[1] // 8
    z = pl.program_id(0)

    @pl.when(z == 0)
    def _():
        for j, block in enumerate((a0, a1, a2, a3)):
            act_t[:, j * rows : (j + 1) * rows] = block[...].T
            hid_t[:, j * rows : (j + 1) * rows] = hidden[j * rows : (j + 1) * rows, :].T

    acc[...] = jnp.dot(act_t[...], back[...], preferred_element_type=F32)
    for c in range(2):
        for sr in range(4):
            row = pl.multiple_of((info[0] ^ sr) * (2 * half) + c * half, 16)
            out[c, sr * half : (sr + 1) * half, :] = acc[pl.ds(row, half), :].astype(BF)
    left = jnp.concatenate(
        [hid_t[pl.ds(pl.multiple_of(i * 128 + z * 32, 32), 32), :] for i in range(6)]
    )
    down = jnp.zeros((192, u0.shape[1]), F32)
    for j, block in enumerate((u0, u1, u2, u3)):
        down = down + jnp.dot(
            left[:, j * rows : (j + 1) * rows], block[...], preferred_element_type=F32
        )
    for c in range(2):
        rows_of_c = jnp.concatenate(
            [down[i * 32 + c * 16 : i * 32 + (c + 1) * 16] for i in range(6)]
        ).astype(BF)
        for cb in range(3):
            first = 4 * half + cb * 96
            out[c, first : first + 96, :] = rows_of_c[:, cb * COLUMNS : (cb + 1) * COLUMNS]


def feed_gradients(info, acts, back, hidden, ups):
    rows, width = acts[0].shape
    units = hidden.shape[1]
    return pl.pallas_call(
        feed_gradients_kernel,
        grid=(4,),
        in_specs=[SCALARS]
        + [whole((rows, width))] * 4
        + [pl.BlockSpec((4 * rows, COLUMNS), lambda z: (0, z)), whole((4 * rows, units))]
        + [whole((rows, width))] * 4,
        out_specs=pl.BlockSpec((2, 864, COLUMNS), lambda z: (z, 0, 0)),
        scratch_shapes=[
            pltpu.VMEM((width, 4 * rows), BF),
            pltpu.VMEM((units, 4 * rows), BF),
            pltpu.VMEM((width, COLUMNS), F32),
        ],
        out_shape=jax.ShapeDtypeStruct((8, 864, COLUMNS), BF),
        compiler_params=params(),
        cost_estimate=cost(2 * 4 * rows * width * 3 * units, 20_000_000),
        name="feed_gradients",
    )(info, *acts, back, hidden, *ups)


STEPS = 6


def gradient_block(info, attention, feed_sum, step, number):
    c = step // 3
    row = pl.multiple_of((step % 3) * 48, 16)
    if number < 8:
        place = (number // 2) ^ info[1]
        at = (c ^ info[2]) * 4 + (place % 2) * 2 + place // 2
        first = (number % 2) * COLUMNS
        return attention[at, pl.ds(row, 48), first : first + COLUMNS]
    which, rest = divmod(number - 8, 8)
    t, sub = divmod(rest, 2)
    row = pl.multiple_of((info[0] ^ t) * 144 + row, 16)
    return feed_sum[(which * 2 + sub) * 2 + c, pl.ds(row, 48), :]


def lanes_sum(value):
    return sum(value[:, j * 128 : (j + 1) * 128] for j in range(value.shape[1] // 128))


def totals_kernel(info, attention, feed_sum, query, key, value, gate, up, first, second, squares):
    step = pl.program_id(0)
    wide = []
    for group in (
        ((query, 0, 3), (key, 6, 1), (value, 7, 1)),
        ((gate, 8, 8), (up, 16, 8)),
    ):
        total = jnp.zeros((48, 128), F32)
        for master, number, count in group:
            for j in range(count):
                block = gradient_block(info, attention, feed_sum, step, number + j).astype(F32)
                weight = master[:, j * COLUMNS : (j + 1) * COLUMNS].astype(BF).astype(F32)
                total = total + lanes_sum(weight * block)
                wide.append(block)
        (first if group[0][1] == 0 else second)[...] = total
    for j in range(3):
        wide.append(gradient_block(info, attention, feed_sum, step, 3 + j).astype(F32))
    total = sum(lanes_sum(block * block) for block in wide)
    row = pl.multiple_of(step * 16, 16)
    for e in range(8):
        for cb in range(3):
            block = feed_sum[e, pl.ds(576 + cb * 96 + row, 16), :].astype(F32)
            part = lanes_sum(block * block)
            total = total + jnp.concatenate([part, jnp.zeros((32, 128), F32)])
    squares[...] = total


def totals(info, attention, feed_sum, query, key, value, gate, up):
    rows = query.shape[0]
    blocks = [
        pl.BlockSpec((rows // STEPS, a.shape[1]), lambda i: (i, 0)) for a in (query, key, value, gate, up)
    ]
    narrow = pl.BlockSpec((rows // STEPS, 128), lambda i: (i, 0))
    return pl.pallas_call(
        totals_kernel,
        grid=(STEPS,),
        in_specs=[SCALARS, whole(attention.shape), whole(feed_sum.shape)] + blocks,
        out_specs=[narrow] * 3,
        out_shape=[jax.ShapeDtypeStruct((rows, 128), F32)] * 3,
        compiler_params=params(),
        cost_estimate=cost(30_000_000, 18_000_000),
        name="totals",
    )(info, attention, feed_sum, query, key, value, gate, up)


def update_kernel(info, clip, attention, feed_sum, *refs):
    moments, masters, new_moments, updates = refs[:7], refs[7:14], refs[14:21], refs[21:]
    step = pl.program_id(0)

    def renew(k, rows, columns, block):
        momentum = momentum_beta * moments[k][rows, columns] + clip[0] * block.astype(F32)
        new_moments[k][rows, columns] = momentum
        updates[k][rows, columns] = (
            masters[k][rows, columns] * (1.0 - learning_rate * weight_decay)
            - learning_rate * momentum
        )

    for k, number, count in ((0, 0, 3), (1, 6, 1), (2, 7, 1), (3, 3, 3), (4, 8, 8), (5, 16, 8)):
        for j in range(count):
            block = gradient_block(info, attention, feed_sum, step, number + j)
            renew(k, slice(0, 48), slice(j * COLUMNS, (j + 1) * COLUMNS), block)
    row = pl.multiple_of(step * 16, 16)
    for e in range(8):
        for cb in range(3):
            block = feed_sum[e, pl.ds(576 + cb * 96 + row, 16), :]
            renew(6, slice(e * 16, (e + 1) * 16), slice(cb * COLUMNS, (cb + 1) * COLUMNS), block)


def update(info, clip, attention, feed_sum, moments, masters):
    blocks = [
        pl.BlockSpec((a.shape[0] // STEPS, a.shape[1]), lambda i: (i, 0)) for a in masters
    ]
    shapes = [jax.ShapeDtypeStruct(a.shape, F32) for a in masters]
    return pl.pallas_call(
        update_kernel,
        grid=(STEPS,),
        in_specs=[SCALARS, SCALARS, whole(attention.shape), whole(feed_sum.shape)] + blocks * 2,
        out_specs=blocks * 2,
        out_shape=shapes * 2,
        compiler_params=params(),
        cost_estimate=cost(20_000_000, 64_000_000),
        name="update",
    )(info, clip, attention, feed_sum, *moments, *masters)


def natural(blocks, own_place):
    result = jnp.stack(blocks)
    order = jnp.arange(4, dtype=jnp.int32) ^ own_place
    return result[order]


def fast_device(
    tokens,
    cotangent,
    picture_starts,
    query_weight,
    key_matrix,
    value_matrix,
    out_weight,
    gate_weight,
    up_weight,
    down_weight,
    attention_gain,
    feed_gain,
    query_moment,
    key_velocity,
    value_velocity,
    out_moment,
    gate_moment,
    up_moment,
    down_moment,
    attention_moment,
    feed_moment,
):
    masters = (
        query_weight,
        key_matrix,
        value_matrix,
        out_weight,
        gate_weight,
        up_weight,
        down_weight,
        attention_gain,
        feed_gain,
    )
    moments = (
        query_moment,
        key_velocity,
        value_velocity,
        out_moment,
        gate_moment,
        up_moment,
        down_moment,
        attention_moment,
        feed_moment,
    )
    me = lax.axis_index("seq")
    line = lax.axis_index("dp") // 2
    core = lax.axis_index("dp") % 2
    rows = tokens.shape[1]
    width = tokens.shape[2]
    shard = query_weight.shape[0]
    half = shard // 2
    hidden_own = down_weight.shape[0]
    places = [me, me ^ 1, me ^ 2, me ^ 3]

    gains = jnp.stack([attention_gain, feed_gain]).astype(BF)
    gains_x = swap_x(gains)
    gains_y = swap_y(gains)
    gains_d = swap_x(gains_y)
    all_gains = natural([gains, gains_x, gains_y, gains_d], me)
    gain_one = all_gains[:, 0].reshape(width).astype(F32)
    gain_two = all_gains[:, 1].reshape(width).astype(F32)

    info = index_array(me, line, core)

    def fetch_rows(own, mine):
        fetched = gather_plane(mine)
        return [own, *fetched, *[swap_core(block) for block in fetched]]

    def core_half(own):
        return lax.dynamic_slice_in_dim(own, core * half, half, 0)

    own_qkv = jnp.concatenate([query_weight, key_matrix, value_matrix], axis=1).astype(BF)
    qkv = fetch_rows(own_qkv, core_half(own_qkv))
    own_out = out_weight.astype(BF)
    mine_out, _ = after(core_half(own_out), qkv[3])
    out_rows = fetch_rows(own_out, mine_out)

    def columns_for(place, first, count):
        at = (first, place * hidden_own)
        size = (count, hidden_own)
        return jnp.concatenate(
            [lax.dynamic_slice(gate_weight, at, size), lax.dynamic_slice(up_weight, at, size)],
            axis=1,
        ).astype(BF)

    sent = [columns_for(place, core * half, half) for place in places[1:]]
    sent, _ = after(sent, qkv[3])
    fetched = [swap_x(sent[0]), swap_y(sent[1]), swap_diagonal(sent[2])]
    gate_up = [
        columns_for(me, jnp.int32(0), shard),
        *fetched,
        *[swap_core(block) for block in fetched],
    ]
    own_down = down_weight.astype(BF)

    upstream_low = cotangent[0]
    upstream_sent, _ = after(upstream_low, out_rows[3])
    upstreams = [upstream_low, *gather_plane(upstream_sent)]

    token_positions = me * rows + jnp.arange(rows, dtype=jnp.int32)
    frequency = 10000.0 ** (-jnp.arange(HEAD_SIZE // 2, dtype=F32) / (HEAD_SIZE // 2))
    angles = token_positions.astype(F32)[:, None] * frequency[None, :]
    cosine, sine = jnp.cos(angles), jnp.sin(angles)
    trig = (
        jnp.concatenate([cosine] * 4, axis=1),
        jnp.concatenate([-sine, sine, -sine, sine], axis=1),
    )

    x = tokens[0]
    starts = picture_starts[0]
    query, key_value, act_one = project(info, x, gain_one[None], *trig, qkv)
    key_values = [key_value, *gather_plane(key_value)]
    attended, attention, residual, act_two = attend(
        info, starts, query, key_values, x, gain_two[None], out_rows
    )
    acts = [act_two, *gather_plane(act_two)]
    hidden, both_back, *act_parts = feed(info, acts, upstreams, gate_up, own_down)
    act_grads = [
        act_parts[0],
        swap_x(act_parts[1]),
        swap_y(act_parts[2]),
        swap_diagonal(act_parts[3]),
    ]
    layer_blocks = layer_parts(hidden, own_down)
    parts = feed_gradients(info, acts, both_back, hidden, upstreams)
    act_grads[0], (parts, layer_blocks) = after(act_grads[0], (parts, layer_blocks))
    output = (residual + scatter_plane(*layer_blocks)).astype(BF)[None]

    grad_residual, grad_low, query_back, *kv_parts = attend_back(
        info,
        starts,
        act_grads,
        upstream_low,
        residual,
        gain_two[None],
        query,
        key_values,
        attended,
        trig,
        out_rows,
    )
    feed_own = lax.psum_scatter(parts, "dp", scatter_dimension=0, tiled=True)[0]
    feed_own, query_back = after(feed_own, query_back)
    feed_own = jnp.concatenate(
        [
            feed_own[:half],
            swap_x(feed_own[half : 2 * half]),
            swap_y(feed_own[2 * half : 3 * half]),
            swap_diagonal(feed_own[3 * half : 4 * half]),
            feed_own[4 * half :],
        ]
    )
    feed_whole = lax.all_gather(feed_own, "dp", axis=0)

    kv_sums = [
        kv_parts[0],
        swap_x(kv_parts[1]),
        swap_y(kv_parts[2]),
        swap_diagonal(kv_parts[3]),
    ]

    def reduce_rows(keep, send):
        received = swap_core(send)
        return scatter_plane(*[keep[j].astype(F32) + received[j] for j in range(4)])

    first_sum = reduce_rows(*query_gradients(info, act_one, attention, query_back, grad_low))
    key_back, keep, send = key_gradients(info, act_one, kv_sums, trig)
    second_sum = reduce_rows(keep, send)
    input_grad = input_back(
        info, query_back, key_back, x, gain_one[None], grad_residual, qkv
    )[None]
    second_sum, input_grad = after(second_sum, input_grad)
    plane_sum = jnp.concatenate([first_sum, second_sum], axis=1)
    quarter = plane_sum.shape[1] // 4

    def chunk(number):
        return lax.dynamic_slice_in_dim(plane_sum, number * quarter, quarter, 1)

    near = swap_near(jnp.stack([chunk(line ^ 1), chunk(line ^ 3)]).astype(BF))
    far = swap_far((chunk(line ^ 2) + near[1]).astype(BF))
    line_own = (chunk(line) + near[0] + far).astype(BF)
    pair_own = jnp.stack([line_own, swap_far(line_own)])
    quad_own = jnp.concatenate([pair_own, swap_near(pair_own)])
    attention_whole = jnp.concatenate([quad_own, swap_core(quad_own)])

    first, second, squares = totals(
        info, attention_whole, feed_whole, query_weight, key_matrix, value_matrix, gate_weight, up_weight
    )
    own_gain_grads = (
        jnp.sum(first, axis=1) / attention_gain.astype(BF).astype(F32),
        jnp.sum(second, axis=1) / feed_gain.astype(BF).astype(F32),
    )
    squares = (
        jnp.sum(squares)
        + jnp.sum(jnp.square(own_gain_grads[0]))
        + jnp.sum(jnp.square(own_gain_grads[1]))
    )
    squares = jnp.broadcast_to(squares, (8, 128))
    squares = squares + swap_x(squares)
    squares = squares + swap_y(squares)
    gradient_norm = jnp.sqrt(squares[0, 0])
    clip_factor = jnp.minimum(1.0, jnp.sqrt(F32(PARAMS)) / (gradient_norm + 1e-06))
    renewed = update(
        info, clip_factor[None], attention_whole, feed_whole, moments[:7], masters[:7]
    )
    momenta, updated = list(renewed[:7]), list(renewed[7:])
    for k in (7, 8):
        momenta.append(momentum_beta * moments[k] + clip_factor * own_gain_grads[k - 7])
        updated.append(
            masters[k] * (1.0 - learning_rate * weight_decay) - learning_rate * momenta[k]
        )
    return (output, input_grad, *momenta, *updated, gradient_norm)


def solution(mesh):
    fits = mesh.shape["seq"] == 4 and mesh.shape["dp"] == 8
    body = fast_device if fits else per_device
    return jax.shard_map(
        body,
        mesh=mesh,
        in_specs=(
            P("dp", "seq", None),
            P("dp", "seq", None),
            P("dp", None),
            P("seq", None),
            P("seq", None),
            P("seq", None),
            P("seq", None),
            P("seq", None),
            P("seq", None),
            P("seq", None),
            P("seq"),
            P("seq"),
            P("seq", None),
            P("seq", None),
            P("seq", None),
            P("seq", None),
            P("seq", None),
            P("seq", None),
            P("seq", None),
            P("seq"),
            P("seq"),
        ),
        out_specs=(
            P("dp", "seq", None),
            P("dp", "seq", None),
            P("seq", None),
            P("seq", None),
            P("seq", None),
            P("seq", None),
            P("seq", None),
            P("seq", None),
            P("seq", None),
            P("seq"),
            P("seq"),
            P("seq", None),
            P("seq", None),
            P("seq", None),
            P("seq", None),
            P("seq", None),
            P("seq", None),
            P("seq", None),
            P("seq"),
            P("seq"),
            P(),
        ),
        check_vma=False,
    )
```

```python
from functools import partial
import math

import jax
import jax.numpy as jnp
from jax import lax
from jax.experimental import pallas as pl
from jax.experimental.pallas import tpu as pltpu
from jax.sharding import PartitionSpec as P

QUERY_HEAD_COUNT = 18
KEY_VALUE_HEADS = 6
HEAD_SIZE = 64
PIECE = 256
PARAMS = 14158080


learning_rate = 0.25
weight_decay = 0.1
momentum_beta = 0.5


def rms_scale(values, scaling):
    return values * lax.rsqrt(jnp.mean(values * values, axis=-1, keepdims=True) + 1e-05) * scaling


def apply_rotary(values, token_positions):
    half_width = values.shape[-1] // 2
    frequency = 10000.0 ** (-jnp.arange(half_width, dtype=jnp.float32) / half_width)
    angles = token_positions.astype(jnp.float32)[:, None] * frequency[None, :]
    cosine = jnp.cos(angles)[:, None, :]
    sine_part = jnp.sin(angles)[:, None, :]
    leading = values[..., :half_width]
    trailing = values[..., half_width:]
    return jnp.concatenate(
        [leading * cosine - trailing * sine_part, trailing * cosine + leading * sine_part], axis=-1
    )


def swiglu(gate_values, up_values):
    return jax.nn.silu(gate_values) * up_values


def piece_number(token_positions, starts):
    inside = (token_positions[:, None] >= starts[None, :]) & (
        token_positions[:, None] < starts[None, :] + PIECE
    )
    numbers = jnp.arange(starts.shape[0], dtype=jnp.int32) + 1
    return jnp.sum(jnp.where(inside, numbers[None, :], 0), axis=1) - 1


def visible(query_position, query_piece, key_position, key_piece):
    earlier = key_position[None, :] <= query_position[:, None]
    same_piece = (query_piece[:, None] == key_piece[None, :]) & (query_piece[:, None] >= 0)
    return earlier | same_piece


def per_device(
    tokens,
    cotangent,
    picture_starts,
    query_weight,
    key_matrix,
    value_matrix,
    out_weight,
    gate_weight,
    up_weight,
    down_weight,
    attention_gain,
    feed_gain,
    query_moment,
    key_velocity,
    value_velocity,
    out_moment,
    gate_moment,
    up_moment,
    down_moment,
    attention_moment,
    feed_moment,
):
    masters = (
        query_weight,
        key_matrix,
        value_matrix,
        out_weight,
        gate_weight,
        up_weight,
        down_weight,
        attention_gain,
        feed_gain,
    )
    moments = (
        query_moment,
        key_velocity,
        value_velocity,
        out_moment,
        gate_moment,
        up_moment,
        down_moment,
        attention_moment,
        feed_moment,
    )
    shard_query = query_weight.astype(jnp.bfloat16)
    shard_key = key_matrix.astype(jnp.bfloat16)
    shard_value = value_matrix.astype(jnp.bfloat16)
    shard_out = out_weight.astype(jnp.bfloat16)
    shard_gate = gate_weight.astype(jnp.bfloat16)
    shard_up = up_weight.astype(jnp.bfloat16)
    shard_down = down_weight.astype(jnp.bfloat16)
    shard_gain_one = attention_gain.astype(jnp.bfloat16)
    shard_gain_two = feed_gain.astype(jnp.bfloat16)
    gathered = (
        lax.all_gather(shard_query, "seq", axis=0, tiled=True),
        lax.all_gather(shard_key, "seq", axis=0, tiled=True),
        lax.all_gather(shard_value, "seq", axis=0, tiled=True),
        lax.all_gather(shard_out, "seq", axis=0, tiled=True),
        lax.all_gather(shard_gate, "seq", axis=0, tiled=True),
        lax.all_gather(shard_up, "seq", axis=0, tiled=True),
        lax.all_gather(shard_down, "seq", axis=0, tiled=True),
        lax.all_gather(shard_gain_one, "seq", axis=0, tiled=True),
        lax.all_gather(shard_gain_two, "seq", axis=0, tiled=True),
    )
    full_query, complete_key, complete_value, full_out, full_gate, full_up, full_down = gathered[:7]
    gain_one = gathered[7].astype(jnp.float32)
    gain_two = gathered[8].astype(jnp.float32)
    group_size = lax.axis_size("seq")
    local_rows = tokens.shape[1]
    sequence_length = local_rows * group_size
    heads_per_group = QUERY_HEAD_COUNT // KEY_VALUE_HEADS
    token_positions = lax.axis_index("seq") * local_rows + jnp.arange(local_rows, dtype=jnp.int32)
    starts = picture_starts[0]
    query_piece = piece_number(token_positions, starts)
    key_positions = jnp.arange(sequence_length, dtype=jnp.int32)
    key_pieces = piece_number(key_positions, starts)
    layer_input = tokens[0].astype(jnp.float32)
    normed_one, pull_norm_one = jax.vjp(rms_scale, layer_input, gain_one)
    first_activation = normed_one.astype(jnp.bfloat16)
    rotation = partial(apply_rotary, token_positions=token_positions)
    query_linear = jnp.dot(
        first_activation, full_query, preferred_element_type=jnp.float32
    ).reshape(local_rows, QUERY_HEAD_COUNT, HEAD_SIZE)
    rotated_query, pull_query = jax.vjp(rotation, query_linear)
    query_reduced = rotated_query.astype(jnp.bfloat16).reshape(
        local_rows, KEY_VALUE_HEADS, heads_per_group, HEAD_SIZE
    )
    key_linear = jnp.dot(
        first_activation, complete_key, preferred_element_type=jnp.float32
    ).reshape(local_rows, KEY_VALUE_HEADS, HEAD_SIZE)
    rotated_key, key_pullback = jax.vjp(rotation, key_linear)
    key_reduced = rotated_key.astype(jnp.bfloat16).reshape(local_rows, KEY_VALUE_HEADS * HEAD_SIZE)
    value_reduced = jnp.dot(
        first_activation, complete_value, preferred_element_type=jnp.float32
    ).astype(jnp.bfloat16)
    every_key_row, every_value_row = (
        lax.all_gather(key_reduced, "seq", axis=0, tiled=True),
        lax.all_gather(value_reduced, "seq", axis=0, tiled=True),
    )
    every_key_row = every_key_row.reshape(sequence_length, KEY_VALUE_HEADS, HEAD_SIZE)
    every_value_row = every_value_row.reshape(sequence_length, KEY_VALUE_HEADS, HEAD_SIZE)
    rows_per_block = math.gcd(512, sequence_length)
    count_of_blocks = sequence_length // rows_per_block
    last_position = token_positions[local_rows - 1]
    last_piece = query_piece[local_rows - 1]

    def needed(number):
        first_row = number * rows_per_block
        return (first_row <= last_position) | (last_piece >= 0) & (
            key_pieces[first_row] == last_piece
        )

    def block_scores(number):
        first_row = number * rows_per_block
        key_block = lax.dynamic_slice_in_dim(every_key_row, first_row, rows_per_block, 0)
        value_block = lax.dynamic_slice_in_dim(every_value_row, first_row, rows_per_block, 0)
        allowed = visible(
            token_positions,
            query_piece,
            lax.dynamic_slice_in_dim(key_positions, first_row, rows_per_block, 0),
            lax.dynamic_slice_in_dim(key_pieces, first_row, rows_per_block, 0),
        )
        raw_scores = jnp.einsum(
            "qhgd,khd->hgqk", query_reduced, key_block, preferred_element_type=jnp.float32
        )
        exponent = jnp.where(allowed[None, None], jnp.exp(raw_scores * 0.125), 0.0)
        return (key_block, value_block, exponent)

    def unchanged(current):
        return current

    def forward_step(number, running):

        def forward_compute(current):
            summed, totals = current
            key_block, value_block, exponent = block_scores(number)
            summed = summed + jnp.einsum(
                "hgqk,khd->hgqd",
                exponent.astype(jnp.bfloat16),
                value_block,
                preferred_element_type=jnp.float32,
            )
            return (summed, totals + jnp.sum(exponent, axis=-1))

        return lax.cond(needed(number), forward_compute, unchanged, running)

    initial_sum = jnp.zeros((KEY_VALUE_HEADS, heads_per_group, local_rows, HEAD_SIZE), jnp.float32)
    initial_total = jnp.zeros((KEY_VALUE_HEADS, heads_per_group, local_rows), jnp.float32)
    summed, totals = lax.fori_loop(0, count_of_blocks, forward_step, (initial_sum, initial_total))
    attended = summed / totals[..., None]
    attention = (
        jnp.transpose(attended, (2, 0, 1, 3))
        .reshape(local_rows, QUERY_HEAD_COUNT * HEAD_SIZE)
        .astype(jnp.bfloat16)
    )
    residual = layer_input + jnp.dot(attention, full_out, preferred_element_type=jnp.float32)
    normed_two, pull_norm_two = jax.vjp(rms_scale, residual, gain_two)
    act_two = normed_two.astype(jnp.bfloat16)
    gate_linear = jnp.dot(act_two, full_gate, preferred_element_type=jnp.float32)
    up_linear = jnp.dot(act_two, full_up, preferred_element_type=jnp.float32)
    hidden_full, pull_swiglu = jax.vjp(swiglu, gate_linear, up_linear)
    hidden = hidden_full.astype(jnp.bfloat16)
    layer_out = residual + jnp.dot(hidden, full_down, preferred_element_type=jnp.float32)
    output = layer_out.astype(jnp.bfloat16)[None]
    upstream = cotangent[0].astype(jnp.float32)
    upstream_low = upstream.astype(jnp.bfloat16)
    grad_down = jnp.einsum("nf,nd->fd", hidden, upstream_low, preferred_element_type=jnp.float32)
    grad_hidden = jnp.einsum(
        "nd,fd->nf", upstream_low, full_down, preferred_element_type=jnp.float32
    )
    grad_gate_full, grad_up_full = pull_swiglu(grad_hidden)
    gate_back = grad_gate_full.astype(jnp.bfloat16)
    up_back = grad_up_full.astype(jnp.bfloat16)
    grad_gate = jnp.einsum("nd,nf->df", act_two, gate_back, preferred_element_type=jnp.float32)
    grad_up = jnp.einsum("nd,nf->df", act_two, up_back, preferred_element_type=jnp.float32)
    grad_act_two = jnp.einsum(
        "nf,df->nd", gate_back, full_gate, preferred_element_type=jnp.float32
    ) + jnp.einsum("nf,df->nd", up_back, full_up, preferred_element_type=jnp.float32)
    residual_norm_grad, grad_gain_two = pull_norm_two(grad_act_two)
    grad_residual = upstream + residual_norm_grad
    residual_back = grad_residual.astype(jnp.bfloat16)
    grad_out = jnp.einsum("nk,nd->kd", attention, residual_back, preferred_element_type=jnp.float32)
    attention_pullback = jnp.einsum(
        "nd,kd->nk", residual_back, full_out, preferred_element_type=jnp.float32
    ).astype(jnp.bfloat16)
    attention_pullback = jnp.transpose(
        attention_pullback.reshape(local_rows, KEY_VALUE_HEADS, heads_per_group, HEAD_SIZE),
        (1, 2, 0, 3),
    )
    back_full = attention_pullback.astype(jnp.float32)
    scaled_back = (back_full / totals[..., None]).astype(jnp.bfloat16)
    total_back = -jnp.sum(back_full * attended, axis=-1) / totals
    query_heads = jnp.transpose(query_reduced, (1, 2, 0, 3))

    def backward_step(number, running):

        def backward_compute(current):
            grad_query_sum, key_gradient_rows, value_gradient_rows = current
            first_row = number * rows_per_block
            key_block, value_block, exponent = block_scores(number)
            through = jnp.einsum(
                "hgqd,khd->hgqk", scaled_back, value_block, preferred_element_type=jnp.float32
            )
            score_back = (exponent * (through + total_back[..., None])).astype(jnp.bfloat16)
            grad_query_sum = (
                grad_query_sum
                + jnp.einsum(
                    "hgqk,khd->hgqd", score_back, key_block, preferred_element_type=jnp.float32
                )
                * 0.125
            )
            key_part = (
                jnp.einsum(
                    "hgqk,hgqd->khd", score_back, query_heads, preferred_element_type=jnp.float32
                )
                * 0.125
            )
            value_part = jnp.einsum(
                "hgqk,hgqd->khd",
                exponent.astype(jnp.bfloat16),
                scaled_back,
                preferred_element_type=jnp.float32,
            )
            key_gradient_rows = lax.dynamic_update_slice_in_dim(
                key_gradient_rows, key_part, first_row, 0
            )
            value_gradient_rows = lax.dynamic_update_slice_in_dim(
                value_gradient_rows, value_part, first_row, 0
            )
            return (grad_query_sum, key_gradient_rows, value_gradient_rows)

        return lax.cond(needed(number), backward_compute, unchanged, running)

    initial_query = jnp.zeros(
        (KEY_VALUE_HEADS, heads_per_group, local_rows, HEAD_SIZE), jnp.float32
    )
    initial_keys = jnp.zeros((sequence_length, KEY_VALUE_HEADS, HEAD_SIZE), jnp.float32)
    grad_query_sum, key_gradient_rows, value_gradient_rows = lax.fori_loop(
        0, count_of_blocks, backward_step, (initial_query, initial_keys, initial_keys)
    )
    local_key_rows, value_own = (
        lax.psum_scatter(
            key_gradient_rows.reshape(sequence_length, KEY_VALUE_HEADS * HEAD_SIZE),
            "seq",
            scatter_dimension=0,
            tiled=True,
        ),
        lax.psum_scatter(
            value_gradient_rows.reshape(sequence_length, KEY_VALUE_HEADS * HEAD_SIZE),
            "seq",
            scatter_dimension=0,
            tiled=True,
        ),
    )
    key_back = (
        key_pullback(local_key_rows.reshape(local_rows, KEY_VALUE_HEADS, HEAD_SIZE))[0]
        .reshape(local_rows, KEY_VALUE_HEADS * HEAD_SIZE)
        .astype(jnp.bfloat16)
    )
    query_rot_grad = jnp.transpose(grad_query_sum, (2, 0, 1, 3)).reshape(
        local_rows, QUERY_HEAD_COUNT, HEAD_SIZE
    )
    query_back = (
        pull_query(query_rot_grad)[0]
        .reshape(local_rows, QUERY_HEAD_COUNT * HEAD_SIZE)
        .astype(jnp.bfloat16)
    )
    value_back = value_own.astype(jnp.bfloat16)
    grad_query = jnp.einsum(
        "nd,nk->dk", first_activation, query_back, preferred_element_type=jnp.float32
    )
    grad_key = jnp.einsum(
        "nd,nk->dk", first_activation, key_back, preferred_element_type=jnp.float32
    )
    grad_value = jnp.einsum(
        "nd,nk->dk", first_activation, value_back, preferred_element_type=jnp.float32
    )
    grad_act_one = jnp.einsum(
        "nk,dk->nd", query_back, full_query, preferred_element_type=jnp.float32
    )
    grad_act_one = grad_act_one + jnp.einsum(
        "nk,dk->nd", key_back, complete_key, preferred_element_type=jnp.float32
    )
    grad_act_one = grad_act_one + jnp.einsum(
        "nk,dk->nd", value_back, complete_value, preferred_element_type=jnp.float32
    )
    input_norm_grad, grad_gain_one = pull_norm_one(grad_act_one)
    input_grad = (grad_residual + input_norm_grad)[None]
    shard_grads = (
        lax.psum_scatter(grad_query, "seq", scatter_dimension=0, tiled=True),
        lax.psum_scatter(grad_key, "seq", scatter_dimension=0, tiled=True),
        lax.psum_scatter(grad_value, "seq", scatter_dimension=0, tiled=True),
        lax.psum_scatter(grad_out, "seq", scatter_dimension=0, tiled=True),
        lax.psum_scatter(grad_gate, "seq", scatter_dimension=0, tiled=True),
        lax.psum_scatter(grad_up, "seq", scatter_dimension=0, tiled=True),
        lax.psum_scatter(grad_down, "seq", scatter_dimension=0, tiled=True),
        lax.psum_scatter(grad_gain_one, "seq", scatter_dimension=0, tiled=True),
        lax.psum_scatter(grad_gain_two, "seq", scatter_dimension=0, tiled=True),
    )
    gradients = lax.psum(
        (
            shard_grads[0],
            shard_grads[1],
            shard_grads[2],
            shard_grads[3],
            shard_grads[4],
            shard_grads[5],
            shard_grads[6],
            shard_grads[7],
            shard_grads[8],
        ),
        "dp",
    )
    squares = jnp.float32(0.0)
    for gradient in gradients:
        squares = squares + jnp.sum(gradient * gradient)
    gradient_norm = jnp.sqrt(lax.psum(squares, "seq"))
    clip_factor = jnp.minimum(1.0, jnp.sqrt(jnp.float32(PARAMS)) / (gradient_norm + 1e-06))
    momenta = [
        momentum_beta * moment + clip_factor * gradient
        for moment, gradient in zip(moments, gradients)
    ]
    updated = [
        master * (1.0 - learning_rate * weight_decay) - learning_rate * momentum
        for master, momentum in zip(masters, momenta)
    ]
    return (
        output,
        input_grad,
        momenta[0],
        momenta[1],
        momenta[2],
        momenta[3],
        momenta[4],
        momenta[5],
        momenta[6],
        momenta[7],
        momenta[8],
        updated[0],
        updated[1],
        updated[2],
        updated[3],
        updated[4],
        updated[5],
        updated[6],
        updated[7],
        updated[8],
        gradient_norm,
    )


BF = jnp.bfloat16
F32 = jnp.float32


def swap_x(value):
    return lax.ppermute(value, "seq", [(i, i ^ 1) for i in range(4)])


def swap_y(value):
    return lax.ppermute(value, "seq", [(i, i ^ 2) for i in range(4)])


def swap_diagonal(value):
    return lax.ppermute(value, "seq", [(i, i ^ 3) for i in range(4)])


def swap_core(value):
    return lax.ppermute(value, "dp", [(i, i ^ 1) for i in range(8)])


def move_up(value):
    return lax.ppermute(value, "dp", [(i, i + 2) for i in range(6)])


def move_down(value):
    return lax.ppermute(value, "dp", [(i + 2, i) for i in range(6)])


def gather_parts(value):
    middle = value.shape[0] // 2
    from_x = swap_x(value)
    from_y = swap_y(value)
    return from_x, from_y, (swap_x(from_y[:middle]), swap_y(from_x[middle:]))


def relay(from_x, from_y):
    middle = from_x.shape[0] // 2
    return jnp.concatenate([swap_x(from_y[:middle]), swap_y(from_x[middle:])])


def gather_plane(value):
    from_x, from_y, from_d = gather_parts(value)
    return from_x, from_y, jnp.concatenate(from_d)


def scatter_plane(own, for_x, for_y, for_d):
    from_x = swap_x(for_x.astype(BF))
    from_y = swap_y(for_y.astype(BF))
    from_d = swap_diagonal(for_d.astype(BF))
    return own.astype(F32) + from_x + from_y + from_d


def swap_near(value):
    return lax.ppermute(value, "dp", [(i, i ^ 2) for i in range(8)])


def swap_far(value):
    return lax.ppermute(value, "dp", [(i, i ^ 4) for i in range(8)])


def after(value, other):
    return lax.optimization_barrier((value, other))


def index_array(*numbers):
    return jnp.stack([jnp.asarray(number, jnp.int32) for number in numbers])


COLUMNS = 384


def whole(shape):
    return pl.BlockSpec(shape, lambda *_: (0,) * len(shape))


def once(shape):
    return pl.BlockSpec(shape, lambda *_: (0,) * len(shape), pipeline_mode=pl.Buffered(1))


ANY = pl.BlockSpec(memory_space=pl.ANY)
SCALARS = pl.BlockSpec(memory_space=pltpu.SMEM)


def params(mebibytes):
    return pltpu.CompilerParams(vmem_limit_bytes=mebibytes * 1024 * 1024)


def cost(flops, transferred):
    return pl.CostEstimate(flops=flops // 1000, bytes_accessed=transferred // 1000, transcendentals=0)


def start_rows(target, blocks, info, semaphores):
    own, fetched, other = blocks[0], blocks[1:4], blocks[4:7]
    shard, half = own.shape[0], own.shape[0] // 2
    copies = [(own, info[0] * shard, shard)]
    for j in range(3):
        first = (info[0] ^ (j + 1)) * shard
        copies.append((fetched[j], first + info[2] * half, half))
        copies.append((other[j], first + (1 - info[2]) * half, half))
    started = []
    for j, (source, row, count) in enumerate(copies):
        row = pl.multiple_of(row, 16)
        copy = pltpu.make_async_copy(source, target.at[pl.ds(row, count)], semaphores.at[j])
        copy.start()
        started.append(copy)
    return started


def partners(value):
    lanes = value.shape[1]
    low = lax.broadcasted_iota(jnp.int32, value.shape, 1) % HEAD_SIZE < HEAD_SIZE // 2
    return jnp.where(low, pltpu.roll(value, lanes - 32, 1), pltpu.roll(value, 32, 1))


def rotate(value, cosine, sine):
    return value * cosine + partners(value) * sine


def transposed(left, right):
    return lax.dot_general(left, right, (((1,), (1,)), ((), ())), preferred_element_type=F32)


def row_mean(value):
    return jnp.mean(value, axis=-1, keepdims=True)


def project_kernel(info, x, cosine, sine, *refs):
    blocks, outs, semaphores = refs[:7], refs[7:12], refs[12]
    query, key_value, act, gains, weight = outs
    copies = start_rows(weight, blocks, info, semaphores)
    values = x[...].astype(F32)
    normed = values * lax.rsqrt(row_mean(values * values) + 1e-05)
    cos = jnp.concatenate([cosine[...]] * 3, axis=1)
    sin = jnp.concatenate([sine[...]] * 3, axis=1)
    for copy in copies:
        copy.wait()
    gains[...] = weight[:, 5 * COLUMNS :].astype(F32).T[:8]
    low = (normed * gains[0:1, :]).astype(BF)
    act[...] = low
    for j in range(5):
        part = jnp.dot(
            low, weight[:, j * COLUMNS : (j + 1) * COLUMNS], preferred_element_type=F32
        )
        if j < 4:
            part = rotate(part, cos, sin)
        part = part.astype(BF)
        if j < 3:
            query[:, j * COLUMNS : (j + 1) * COLUMNS] = part * 0.125
        else:
            key_value[:, (j - 3) * COLUMNS : (j - 2) * COLUMNS] = part


def project(info, x, cosine, sine, blocks):
    rows, width = x.shape
    columns = blocks[0].shape[1]
    shapes = [
        ((rows, width), BF),
        ((rows, 2 * COLUMNS), BF),
        ((rows, width), BF),
        ((8, width), F32),
        ((width, columns), BF),
    ]
    return pl.pallas_call(
        project_kernel,
        in_specs=[SCALARS, *[whole(a.shape) for a in (x, cosine, sine)]] + [ANY] * 7,
        out_specs=[whole(shape) for shape, _ in shapes],
        out_shape=[jax.ShapeDtypeStruct(shape, kind) for shape, kind in shapes],
        scratch_shapes=[pltpu.SemaphoreType.DMA((7,))],
        compiler_params=params(24),
        cost_estimate=cost(2 * rows * width * columns, 8_000_000),
        name="project",
    )(info, x, cosine, sine, *blocks)


def piece_of(positions, starts, count):
    piece = jnp.full(positions.shape, -1, jnp.int32)
    for j in range(count):
        first = starts[j]
        piece = jnp.where((positions >= first) & (positions < first + PIECE), j, piece)
    return piece


def visibility(info, starts, count, rows, keys_first):
    axis = 1 if keys_first else 0
    query_shape = (1, rows) if keys_first else (rows, 1)
    query_at = info[0] * rows + lax.broadcasted_iota(jnp.int32, query_shape, axis)
    query_piece = piece_of(query_at, starts, count)
    biases = []
    for j in range(4):
        key_shape = query_shape[::-1]
        key_at = (info[0] ^ j) * rows + lax.broadcasted_iota(jnp.int32, key_shape, 1 - axis)
        key_piece = piece_of(key_at, starts, count)
        seen = (key_at <= query_at) | ((key_piece == query_piece) & (query_piece >= 0))
        biases.append(jnp.where(seen, 0.0, -1e30).astype(F32))
    return jnp.concatenate(biases, axis=1 - axis)


def attend_kernel(info, starts, query, kv0, kv1, kv2, kv3, attended, every):
    rows = query.shape[0]
    for j, block in enumerate((kv0, kv1, kv2, kv3)):
        every[j * rows : (j + 1) * rows, :] = block[...]
    bias = visibility(info, starts, starts.shape[0], rows, False)

    def pair(p, carry):
        at = pl.multiple_of(p * 128, 128)
        keys = every[:, pl.ds(at, 128)]
        values = every[:, pl.ds(COLUMNS + at, 128)]
        queries = query[:, pl.ds(pl.multiple_of(p * COLUMNS, 128), COLUMNS)]
        results = []
        for k in range(2):
            key = keys[:, k * 64 : (k + 1) * 64]
            value = values[:, k * 64 : (k + 1) * 64]
            for h in range(3):
                at = (k * 3 + h) * 64
                scores = transposed(queries[:, at : at + 64], key)
                exponent = jnp.exp(scores + bias)
                total = jnp.sum(exponent, axis=-1, keepdims=True)
                summed = jnp.dot(exponent.astype(BF), value, preferred_element_type=F32)
                results.append(summed / total)
        attended[:, pl.ds(pl.multiple_of(p * COLUMNS, 128), COLUMNS)] = jnp.concatenate(
            results, axis=1
        )
        return carry

    lax.fori_loop(0, 3, pair, 0)


def attend(info, starts, query, key_values):
    rows, width = query.shape
    square = whole((rows, width))
    return pl.pallas_call(
        attend_kernel,
        in_specs=[SCALARS, SCALARS, square] + [whole(a.shape) for a in key_values],
        out_specs=square,
        out_shape=jax.ShapeDtypeStruct((rows, width), F32),
        scratch_shapes=[pltpu.VMEM((4 * rows, 2 * COLUMNS), BF)],
        compiler_params=params(20),
        cost_estimate=cost(4 * rows * 4 * rows * width * 4, 10_000_000),
        name="attend",
    )(info, starts, query, *key_values)


def out_project_kernel(info, attended, x, gains, *refs):
    blocks, (attention, residual, act, weight), semaphores = refs[:7], refs[7:11], refs[11]
    copies = start_rows(weight, blocks, info, semaphores)
    low = attended[...].astype(BF)
    attention[...] = low
    for copy in copies:
        copy.wait()
    summed = x[...].astype(F32) + jnp.dot(low, weight[...], preferred_element_type=F32)
    residual[...] = summed
    scale = lax.rsqrt(row_mean(summed * summed) + 1e-05)
    act[...] = (summed * scale * gains[1:2, :]).astype(BF)


def out_project(info, attended, x, gains, blocks):
    rows, width = x.shape
    square = whole((rows, width))
    return pl.pallas_call(
        out_project_kernel,
        in_specs=[SCALARS, square, square, whole(gains.shape)] + [ANY] * 7,
        out_specs=[square] * 3 + [whole((width, width))],
        out_shape=[jax.ShapeDtypeStruct((rows, width), t) for t in (BF, F32, BF)]
        + [jax.ShapeDtypeStruct((width, width), BF)],
        scratch_shapes=[pltpu.SemaphoreType.DMA((7,))],
        compiler_params=params(18),
        cost_estimate=cost(2 * rows * width * width, 6_000_000),
        name="out_project",
    )(info, attended, x, gains, *blocks)


def feed_blocks(acts, ups, weight, down, hidden, back, outs):
    rows = acts[0].shape[0]
    units = down.shape[0]
    for j in range(len(acts)):
        span = slice(j * rows, (j + 1) * rows)
        both = jnp.dot(acts[j][...], weight[...], preferred_element_type=F32)
        gate, up = both[:, :units], both[:, units:]
        grad = transposed(ups[j][...], down[...])
        logistic = 1.0 / (1.0 + jnp.exp(-gate))
        smooth = gate * logistic
        hidden[span, :] = (smooth * up).astype(BF)
        slope = logistic * (1.0 + gate * (1.0 - logistic))
        back[span, :units] = (grad * up * slope).astype(BF)
        back[span, units:] = (grad * smooth).astype(BF)
        outs[j][...] = transposed(back[span, :], weight[...]).astype(outs[j].dtype)


def feed_first_kernel(info, *refs):
    acts, ups, refs = refs[:3], refs[3:6], refs[6:]
    own, fetched, near, other, down = refs[0], refs[1:4], refs[4], refs[5], refs[6]
    hidden, back, outs, weight, semaphores = refs[7], refs[8], refs[9:12], refs[12], refs[13]
    units = down.shape[0]
    shard, half = own.shape[0], own.shape[0] // 2
    bit = info[1] % 2
    copies = [(own, weight.at[pl.ds(pl.multiple_of(info[0] * shard, 16), shard)])]
    for j in range(3):
        first = (info[0] ^ (j + 1)) * shard
        mine = pl.ds(pl.multiple_of(first + info[2] * half, 16), half)
        theirs = pl.ds(pl.multiple_of(first + (1 - info[2]) * half, 16), half)
        same = pl.ds(pl.multiple_of(bit * units, 128), units)
        opposite = pl.ds(pl.multiple_of((1 - bit) * units, 128), units)
        copies.append((fetched[j], weight.at[mine, same]))
        copies.append((near.at[j], weight.at[mine, opposite]))
        copies.append((other.at[j], weight.at[theirs, same]))
        copies.append((other.at[3 + j], weight.at[theirs, opposite]))
    started = []
    for j, (source, target) in enumerate(copies):
        copy = pltpu.make_async_copy(source, target, semaphores.at[j])
        copy.start()
        started.append(copy)
    for copy in started:
        copy.wait()
    feed_blocks(acts, ups, weight, down, hidden, back, outs)


def feed_last_kernel(act, up, weight, down, hidden, back, out):
    feed_blocks([act], [up], weight, down, hidden, back, [out])


def feed(kernel, info, acts, ups, weights, specs, down, kinds, extra, scratch):
    count = len(acts)
    rows, width = acts[0].shape
    units = down.shape[0]
    square = whole((rows, width))
    shapes = [((count * rows, units), BF), ((count * rows, 2 * units), BF)]
    shapes += [((rows, width), kind) for kind in kinds] + extra
    return pl.pallas_call(
        kernel,
        in_specs=[SCALARS] * len(info) + [square] * (2 * count) + specs + [whole(down.shape)],
        out_specs=[whole(shape) for shape, _ in shapes],
        out_shape=[jax.ShapeDtypeStruct(shape, kind) for shape, kind in shapes],
        scratch_shapes=scratch,
        compiler_params=params(28 if count == 3 else 20),
        cost_estimate=cost(10 * count * rows * width * units, 20_000_000),
        name="feed",
    )(*info, *acts, *ups, *weights, down)


def feed_first(info, acts, ups, blocks, down):
    full = (acts[0].shape[1], 2 * down.shape[0])
    return feed(
        feed_first_kernel,
        [info],
        acts,
        ups,
        blocks,
        [ANY] * 6,
        down,
        (F32, BF, BF),
        [(full, BF)],
        [pltpu.SemaphoreType.DMA((13,))],
    )


def feed_last(act, up, weight, down):
    return feed(
        feed_last_kernel, [], [act], [up], [weight], [whole(weight.shape)], down, (BF,), [], []
    )


def layer_parts_kernel(hidden, last, down, *outs):
    rows = last.shape[0]
    for j in range(4):
        left = last[...] if j == 3 else hidden[j * rows : (j + 1) * rows, :]
        outs[j][...] = jnp.dot(left, down[...], preferred_element_type=F32).astype(outs[j].dtype)


def layer_parts(hidden, last, down):
    rows, units = last.shape
    width = down.shape[1]
    return pl.pallas_call(
        layer_parts_kernel,
        in_specs=[whole(hidden.shape), whole(last.shape), whole(down.shape)],
        out_specs=[whole((rows, width))] * 4,
        out_shape=[jax.ShapeDtypeStruct((rows, width), t) for t in (F32, BF, BF, BF)],
        compiler_params=params(14),
        cost_estimate=cost(8 * rows * units * width, 8_000_000),
        name="layer_parts",
    )(hidden, last, down)


def attend_back_kernel(info, starts, g0, g1, g2, g3, upstream, residual, gains, query, *refs):
    kvs, attended, cosine, sine, weight = refs[:4], refs[4], refs[5], refs[6], refs[7]
    grad_residual, grad_low, query_back, outs = refs[8], refs[9], refs[10], refs[11:15]
    every, back = refs[15:]
    rows = query.shape[0]
    for j, block in enumerate(kvs):
        every[j * rows : (j + 1) * rows, :] = block[...]
    act_back = g0[...] + g1[...].astype(F32) + g2[...].astype(F32) + g3[...].astype(F32)
    weighted = act_back * gains[1:2, :]
    values = residual[...]
    scale = lax.rsqrt(row_mean(values * values) + 1e-05)
    grad = upstream[...].astype(F32) + scale * (
        weighted - values * (scale * scale * row_mean(weighted * values))
    )
    grad_residual[...] = grad
    low = grad.astype(BF)
    grad_low[...] = low
    back[...] = transposed(low, weight[...]).astype(BF)
    bias = visibility(info, starts, starts.shape[0], rows, True)
    cos = jnp.concatenate([cosine[...]] * 3, axis=1)
    sin = jnp.concatenate([sine[...]] * 3, axis=1)

    def pair(p, carry):
        at = pl.multiple_of(p * 128, 128)
        wide = pl.ds(pl.multiple_of(p * COLUMNS, 128), COLUMNS)
        keys = every[:, pl.ds(at, 128)]
        values = every[:, pl.ds(COLUMNS + at, 128)]
        queries = query[:, wide]
        backs = back[:, wide].astype(F32).T
        products = backs * attended[:, wide].T
        query_parts, key_parts, value_parts = [], [], []
        for k in range(2):
            key = keys[:, k * 64 : (k + 1) * 64]
            value = values[:, k * 64 : (k + 1) * 64]
            key_t = key.T
            key_sum = value_sum = None
            for h in range(3):
                at = (k * 3 + h) * 64
                one = queries[:, at : at + 64]
                exponent = jnp.exp(transposed(key, one) + bias)
                total = jnp.sum(exponent, axis=0, keepdims=True)
                scaled = (backs[at : at + 64] / total).astype(BF)
                shift = -jnp.sum(products[at : at + 64], axis=0, keepdims=True) / total
                through = jnp.dot(value, scaled, preferred_element_type=F32)
                score = (exponent * (through + shift)).astype(BF)
                query_parts.append(jnp.dot(key_t, score, preferred_element_type=F32))
                key_part = jnp.dot(score, one, preferred_element_type=F32)
                value_part = transposed(exponent.astype(BF), scaled)
                key_sum = key_part if key_sum is None else key_sum + key_part
                value_sum = value_part if value_sum is None else value_sum + value_part
            key_parts.append(key_sum)
            value_parts.append(value_sum)
        turned = jnp.concatenate(query_parts, axis=0).T * 0.125
        query_back[:, wide] = rotate(turned, cos, -sin).astype(BF)
        key_pair = jnp.concatenate(key_parts, axis=1)
        value_pair = jnp.concatenate(value_parts, axis=1)
        for j in range(4):
            span = slice(j * rows, (j + 1) * rows)
            kind = outs[j].dtype
            at = pl.multiple_of(p * 128, 128)
            outs[j][:, pl.ds(at, 128)] = key_pair[span].astype(kind)
            outs[j][:, pl.ds(COLUMNS + at, 128)] = value_pair[span].astype(kind)
        return carry

    lax.fori_loop(0, 3, pair, 0)


def attend_back(info, starts, grads, upstream, residual, gains, query, kvs, attended, trig, weight):
    rows, width = query.shape
    square = whole((rows, width))
    table = whole(trig[0].shape)
    pair = whole((rows, 2 * COLUMNS))
    return pl.pallas_call(
        attend_back_kernel,
        in_specs=[SCALARS, SCALARS]
        + [square] * 6
        + [whole(gains.shape), square]
        + [pair] * 4
        + [square, table, table, whole(weight.shape)],
        out_specs=[square] * 3 + [pair] * 4,
        out_shape=[jax.ShapeDtypeStruct((rows, width), t) for t in (F32, BF, BF)]
        + [jax.ShapeDtypeStruct((rows, 2 * COLUMNS), t) for t in (F32, BF, BF, BF)],
        scratch_shapes=[
            pltpu.VMEM((4 * rows, 2 * COLUMNS), BF),
            pltpu.VMEM((rows, width), BF),
        ],
        compiler_params=params(28),
        cost_estimate=cost(10 * rows * 4 * rows * width * 4, 15_000_000),
        name="attend_back",
    )(info, starts, *grads, upstream, residual, gains, query, *kvs, attended, *trig, weight)


def split_rows(info, product, keep, send, columns):
    half = keep.shape[1]
    for sr in range(4):
        row = (info[0] ^ sr) * (2 * half)
        kept = pl.multiple_of(row + info[2] * half, 16)
        sent = pl.multiple_of(row + (1 - info[2]) * half, 16)
        keep[sr, :, columns] = product[pl.ds(kept, half), :].astype(BF)
        send[sr, :, columns] = product[pl.ds(sent, half), :].astype(BF)


def query_gradients_kernel(info, act, att, query_back, grad_low, keep, send, product):
    for first, (left, right) in enumerate(((act, query_back), (att, grad_low))):
        left_t = left[...].T
        for j in range(3):
            columns = slice(j * COLUMNS, (j + 1) * COLUMNS)
            product[...] = jnp.dot(left_t, right[:, columns], preferred_element_type=F32)
            at = (first * 3 + j) * COLUMNS
            split_rows(info, product, keep, send, slice(at, at + COLUMNS))


def query_gradients(info, act, att, query_back, grad_low):
    rows, width = act.shape
    half = width // 8
    square = whole((rows, width))
    out = (4, half, 2 * width)
    return pl.pallas_call(
        query_gradients_kernel,
        in_specs=[SCALARS] + [square] * 4,
        out_specs=[whole(out)] * 2,
        out_shape=[jax.ShapeDtypeStruct(out, BF)] * 2,
        scratch_shapes=[pltpu.VMEM((width, COLUMNS), F32)],
        compiler_params=params(20),
        cost_estimate=cost(4 * rows * width * width, 9_000_000),
        name="query_gradients",
    )(info, act, att, query_back, grad_low)


def key_gradients_kernel(info, act, p0, p1, p2, p3, cosine, sine, back, keep, send, product):
    summed = p0[...] + p1[...].astype(F32) + p2[...].astype(F32) + p3[...].astype(F32)
    cos = jnp.concatenate([cosine[...]] * 3, axis=1)
    sin = jnp.concatenate([sine[...]] * 3, axis=1)
    back[:, :COLUMNS] = rotate(summed[:, :COLUMNS], cos, -sin).astype(BF)
    back[:, COLUMNS:] = summed[:, COLUMNS:].astype(BF)
    left_t = act[...].T
    for j in range(2):
        columns = slice(j * COLUMNS, (j + 1) * COLUMNS)
        product[...] = jnp.dot(left_t, back[:, columns], preferred_element_type=F32)
        split_rows(info, product, keep, send, columns)


def key_gradients(info, act, parts, trig):
    rows, width = act.shape
    half = width // 8
    out = (4, half, 2 * COLUMNS)
    pair = whole((rows, 2 * COLUMNS))
    table = whole(trig[0].shape)
    return pl.pallas_call(
        key_gradients_kernel,
        in_specs=[SCALARS, whole((rows, width))] + [pair] * 4 + [table, table],
        out_specs=[pair, whole(out), whole(out)],
        out_shape=[jax.ShapeDtypeStruct((rows, 2 * COLUMNS), BF)]
        + [jax.ShapeDtypeStruct(out, BF)] * 2,
        scratch_shapes=[pltpu.VMEM((width, COLUMNS), F32)],
        compiler_params=params(14),
        cost_estimate=cost(4 * rows * width * COLUMNS, 5_000_000),
        name="key_gradients",
    )(info, act, *parts, *trig)


def input_back_kernel(query_back, key_back, x, gains, grad_residual, weight, out):
    width = x.shape[1]
    act_back = transposed(query_back[...], weight[:, :width])
    act_back = act_back + transposed(key_back[...], weight[:, width : width + 2 * COLUMNS])
    values = x[...].astype(F32)
    scale = lax.rsqrt(row_mean(values * values) + 1e-05)
    weighted = act_back * gains[0:1, :]
    out[...] = grad_residual[...] + scale * (
        weighted - values * (scale * scale * row_mean(weighted * values))
    )


def input_back(*operands):
    rows, width = operands[0].shape
    return pl.pallas_call(
        input_back_kernel,
        in_specs=[whole(a.shape) for a in operands],
        out_specs=whole((rows, width)),
        out_shape=jax.ShapeDtypeStruct((rows, width), F32),
        compiler_params=params(20),
        cost_estimate=cost(10 * rows * width * COLUMNS, 9_000_000),
        name="input_back",
    )(*operands)


def feed_gradients_kernel(
    info, a0, a1, a2, a3, back, back_last, hidden, last, u0, u1, u2, u3, out, act_t, hid_t, acc
):
    rows = a0.shape[0]
    half = a0.shape[1] // 8
    z = pl.program_id(0)

    @pl.when(z == 0)
    def _():
        for j, block in enumerate((a0, a1, a2, a3)):
            act_t[:, j * rows : (j + 1) * rows] = block[...].T
            block = last[...] if j == 3 else hidden[j * rows : (j + 1) * rows, :]
            hid_t[:, j * rows : (j + 1) * rows] = block.T

    acc[...] = jnp.dot(
        act_t[:, : 3 * rows], back[...], preferred_element_type=F32
    ) + jnp.dot(act_t[:, 3 * rows :], back_last[...], preferred_element_type=F32)
    for c in range(2):
        for sr in range(4):
            row = pl.multiple_of((info[0] ^ sr) * (2 * half) + c * half, 16)
            out[c, sr * half : (sr + 1) * half, :] = acc[pl.ds(row, half), :].astype(BF)
    left = jnp.concatenate(
        [hid_t[pl.ds(pl.multiple_of(i * 128 + z * 32, 32), 32), :] for i in range(6)]
    )
    down = jnp.zeros((192, u0.shape[1]), F32)
    for j, block in enumerate((u0, u1, u2, u3)):
        down = down + jnp.dot(
            left[:, j * rows : (j + 1) * rows], block[...], preferred_element_type=F32
        )
    for c in range(2):
        rows_of_c = jnp.concatenate(
            [down[i * 32 + c * 16 : i * 32 + (c + 1) * 16] for i in range(6)]
        ).astype(BF)
        for cb in range(3):
            first = 4 * half + cb * 96
            out[c, first : first + 96, :] = rows_of_c[:, cb * COLUMNS : (cb + 1) * COLUMNS]


def feed_gradients(info, acts, back, back_last, hidden, last, ups):
    rows, width = acts[0].shape
    units = hidden.shape[1]
    return pl.pallas_call(
        feed_gradients_kernel,
        grid=(4,),
        in_specs=[SCALARS]
        + [once((rows, width))] * 4
        + [
            pl.BlockSpec((3 * rows, COLUMNS), lambda z: (0, z)),
            pl.BlockSpec((rows, COLUMNS), lambda z: (0, z)),
            once(hidden.shape),
            once(last.shape),
        ]
        + [once((rows, width))] * 4,
        out_specs=pl.BlockSpec((2, 864, COLUMNS), lambda z: (z, 0, 0)),
        scratch_shapes=[
            pltpu.VMEM((width, 4 * rows), BF),
            pltpu.VMEM((units, 4 * rows), BF),
            pltpu.VMEM((width, COLUMNS), F32),
        ],
        out_shape=jax.ShapeDtypeStruct((8, 864, COLUMNS), BF),
        compiler_params=params(26),
        cost_estimate=cost(2 * 4 * rows * width * 3 * units, 20_000_000),
        name="feed_gradients",
    )(info, *acts, back, back_last, hidden, last, *ups)


def pair_sum_kernel(keep, received, second_keep, second_received, *outs):
    columns = keep.shape[2]
    for j in range(4):
        for span, one, other in (
            (slice(0, columns), keep, received),
            (slice(columns, None), second_keep, second_received),
        ):
            outs[j][:, span] = (one[j].astype(F32) + other[j].astype(F32)).astype(outs[j].dtype)


def pair_sum(*parts):
    shape = (parts[0].shape[1], parts[0].shape[2] + parts[2].shape[2])
    return pl.pallas_call(
        pair_sum_kernel,
        in_specs=[whole(a.shape) for a in parts],
        out_specs=[whole(shape)] * 4,
        out_shape=[jax.ShapeDtypeStruct(shape, t) for t in (F32, BF, BF, BF)],
        compiler_params=params(18),
        cost_estimate=cost(10_000_000, 5_000_000),
        name="pair_sum",
    )(*parts)


def plane_sum_kernel(info, own, from_x, from_y, from_d, near, keep):
    quarter = near.shape[2]
    for j, (target, place) in enumerate(((keep, 0), (near, 1), (keep, 2), (near, 3))):
        span = pl.ds(pl.multiple_of((info[1] ^ place) * quarter, 128), quarter)
        summed = own[:, span]
        for part in (from_x, from_y, from_d):
            summed = summed + part[:, span].astype(F32)
        target[j // 2] = summed.astype(target.dtype)


def plane_sum(info, parts):
    rows, columns = parts[0].shape
    shape = (2, rows, columns // 4)
    return pl.pallas_call(
        plane_sum_kernel,
        in_specs=[SCALARS] + [whole(a.shape) for a in parts],
        out_specs=[whole(shape)] * 2,
        out_shape=[jax.ShapeDtypeStruct(shape, t) for t in (BF, F32)],
        compiler_params=params(16),
        cost_estimate=cost(10_000_000, 5_000_000),
        name="plane_sum",
    )(info, *parts)


STEPS = 6


def attention_block(attention, step, number):
    row = pl.multiple_of((step % 3) * 48, 16)
    first = (number % 2) * COLUMNS
    return attention[(step // 3) * 4 + number // 2, pl.ds(row, 48), first : first + COLUMNS]


def feed_block(info, feed_sum, step, number):
    which, rest = divmod(number, 8)
    t, sub = divmod(rest, 2)
    row = pl.multiple_of((info[0] ^ t) * 144 + (step % 3) * 48, 16)
    return feed_sum[(which * 2 + sub) * 2 + step // 3, pl.ds(row, 48), :]


def lanes_sum(value):
    return sum(value[:, j * 128 : (j + 1) * 128] for j in range(value.shape[1] // 128))


def start_attention(info, pieces, target, semaphores):
    copies = []
    for j, piece in enumerate(pieces):
        core = info[2] if j < 2 else 1 - info[2]
        for k in range(2):
            place = core * 4 + (info[1] ^ (2 * k + j % 2))
            copy = pltpu.make_async_copy(piece.at[k], target.at[place], semaphores.at[2 * j + k])
            copy.start()
            copies.append(copy)
    return copies


def attention_scratch(pieces):
    return [pltpu.VMEM((8, *pieces[0].shape[1:]), BF), pltpu.SemaphoreType.DMA((8,))]


def feed_totals_kernel(info, feed_sum, gate, up, gain, gain_grad, squares):
    step = pl.program_id(0)
    total = jnp.zeros((48, 128), F32)
    square = jnp.zeros((48, 128), F32)
    for master, number in ((gate, 0), (up, 8)):
        for j in range(8):
            block = feed_block(info, feed_sum, step, number + j).astype(F32)
            weight = master[:, j * COLUMNS : (j + 1) * COLUMNS].astype(BF).astype(F32)
            total = total + lanes_sum(weight * block)
            square = square + lanes_sum(block * block)
    grad = jnp.sum(total, axis=1, keepdims=True) / gain[...]
    gain_grad[...] = grad
    result = jnp.sum(square.reshape(6, 8, 128), axis=0)
    result = result + jnp.sum(jnp.square(grad)) * (1.0 / 1024)
    row = pl.multiple_of(step * 16, 16)
    for e in range(8):
        for cb in range(3):
            block = feed_sum[e, pl.ds(576 + cb * 96 + row, 16), :].astype(F32)
            part = lanes_sum(block * block)
            result = result + part[:8] + part[8:]

    @pl.when(step == 0)
    def _():
        squares[...] = result

    @pl.when(step > 0)
    def _():
        squares[...] += result


def feed_totals(info, feed_sum, gate, up, gain):
    rows, columns = gate.shape
    wide = pl.BlockSpec((rows // STEPS, columns), lambda i: (i, 0))
    narrow = pl.BlockSpec((rows // STEPS, 1), lambda i: (i, 0))
    return pl.pallas_call(
        feed_totals_kernel,
        grid=(STEPS,),
        in_specs=[SCALARS, once(feed_sum.shape), wide, wide, narrow],
        out_specs=[narrow, whole((8, 128))],
        out_shape=[jax.ShapeDtypeStruct((rows, 1), F32), jax.ShapeDtypeStruct((8, 128), F32)],
        compiler_params=params(20),
        cost_estimate=cost(30_000_000, 13_000_000),
        name="feed_totals",
    )(info, feed_sum, gate, up, gain)


def attention_totals_kernel(info, *refs):
    pieces, (query, key, value, gain, before) = refs[:4], refs[4:9]
    gain_grad, squares, attention, semaphores = refs[9:]
    for copy in start_attention(info, pieces, attention, semaphores):
        copy.wait()
    result = before[...]
    for step in range(STEPS):
        rows = slice(step * 48, (step + 1) * 48)
        total = jnp.zeros((48, 128), F32)
        square = jnp.zeros((48, 128), F32)
        for master, number, count in ((query, 0, 3), (key, 6, 1), (value, 7, 1)):
            for j in range(count):
                block = attention_block(attention, step, number + j).astype(F32)
                square = square + lanes_sum(block * block)
                weight = master[rows, j * COLUMNS : (j + 1) * COLUMNS].astype(BF).astype(F32)
                total = total + lanes_sum(weight * block)
        for j in range(3):
            block = attention_block(attention, step, 3 + j).astype(F32)
            square = square + lanes_sum(block * block)
        grad = jnp.sum(total, axis=1, keepdims=True) / gain[rows, :]
        gain_grad[rows, :] = grad
        result = result + jnp.sum(square.reshape(6, 8, 128), axis=0)
        result = result + jnp.sum(jnp.square(grad)) * (1.0 / 1024)
    squares[...] = result


def attention_totals(info, pieces, query, key, value, gain, before):
    rows = query.shape[0]
    return pl.pallas_call(
        attention_totals_kernel,
        in_specs=[SCALARS]
        + [ANY] * 4
        + [whole(a.shape) for a in (query, key, value, gain, before)],
        out_specs=[whole((rows, 1)), whole((8, 128))],
        out_shape=[jax.ShapeDtypeStruct((rows, 1), F32), jax.ShapeDtypeStruct((8, 128), F32)],
        scratch_shapes=attention_scratch(pieces),
        compiler_params=params(12),
        cost_estimate=cost(10_000_000, 4_000_000),
        name="attention_totals",
    )(info, *pieces, query, key, value, gain, before)


def update_kernel(info, s0, s1, s2, s3, feed_sum, *refs):
    pieces, moments, masters = refs[:4], refs[4:11], refs[11:18]
    new_moments, updates, norm, attention, semaphores = (
        refs[18:25],
        refs[25:32],
        refs[32],
        refs[33],
        refs[34],
    )
    step = pl.program_id(0)

    @pl.when(step == 0)
    def _():
        for copy in start_attention(info, pieces, attention, semaphores):
            copy.wait()

    squares = (s0[...] + s1[...]) + (s2[...] + s3[...])
    length = jnp.sqrt(jnp.sum(squares, keepdims=True))
    norm[...] = length
    clip = jnp.minimum(1.0, jnp.sqrt(F32(PARAMS)) / (length + 1e-06))

    def renew(k, rows, columns, block):
        momentum = momentum_beta * moments[k][rows, columns] + clip * block.astype(F32)
        new_moments[k][rows, columns] = momentum
        updates[k][rows, columns] = (
            masters[k][rows, columns] * (1.0 - learning_rate * weight_decay)
            - learning_rate * momentum
        )

    for k, number, count in ((0, 0, 3), (1, 6, 1), (2, 7, 1), (3, 3, 3)):
        for j in range(count):
            block = attention_block(attention, step, number + j)
            renew(k, slice(0, 48), slice(j * COLUMNS, (j + 1) * COLUMNS), block)
    for k, number in ((4, 0), (5, 8)):
        for j in range(8):
            block = feed_block(info, feed_sum, step, number + j)
            renew(k, slice(0, 48), slice(j * COLUMNS, (j + 1) * COLUMNS), block)
    row = pl.multiple_of(step * 16, 16)
    for e in range(8):
        for cb in range(3):
            block = feed_sum[e, pl.ds(576 + cb * 96 + row, 16), :]
            renew(6, slice(e * 16, (e + 1) * 16), slice(cb * COLUMNS, (cb + 1) * COLUMNS), block)


def update(info, squares, pieces, feed_sum, moments, masters):
    blocks = [
        pl.BlockSpec((a.shape[0] // STEPS, a.shape[1]), lambda i: (i, 0)) for a in masters
    ]
    shapes = [jax.ShapeDtypeStruct(a.shape, F32) for a in masters]
    return pl.pallas_call(
        update_kernel,
        grid=(STEPS,),
        in_specs=[SCALARS]
        + [whole((8, 128))] * 4
        + [once(feed_sum.shape)]
        + [ANY] * 4
        + blocks * 2,
        out_specs=blocks * 2 + [whole((1, 1))],
        out_shape=shapes * 2 + [jax.ShapeDtypeStruct((1, 1), F32)],
        scratch_shapes=attention_scratch(pieces),
        compiler_params=params(36),
        cost_estimate=cost(20_000_000, 64_000_000),
        name="update",
    )(info, *squares, feed_sum, *pieces, *moments, *masters)


def fast_device(
    tokens,
    cotangent,
    picture_starts,
    query_weight,
    key_matrix,
    value_matrix,
    out_weight,
    gate_weight,
    up_weight,
    down_weight,
    attention_gain,
    feed_gain,
    query_moment,
    key_velocity,
    value_velocity,
    out_moment,
    gate_moment,
    up_moment,
    down_moment,
    attention_moment,
    feed_moment,
):
    masters = (
        query_weight,
        key_matrix,
        value_matrix,
        out_weight,
        gate_weight,
        up_weight,
        down_weight,
        attention_gain,
        feed_gain,
    )
    moments = (
        query_moment,
        key_velocity,
        value_velocity,
        out_moment,
        gate_moment,
        up_moment,
        down_moment,
        attention_moment,
        feed_moment,
    )
    me = lax.axis_index("seq")
    line = lax.axis_index("dp") // 2
    core = lax.axis_index("dp") % 2
    rows = tokens.shape[1]
    width = tokens.shape[2]
    shard = query_weight.shape[0]
    half = shard // 2
    hidden_own = down_weight.shape[0]
    places = [me, me ^ 1, me ^ 2, me ^ 3]

    gain_columns = [
        gain.astype(BF).astype(F32)[:, None] for gain in (attention_gain, feed_gain)
    ]
    info = index_array(me, line, core)

    def fetch_rows(own, mine):
        fetched = gather_plane(mine)
        return [own, *fetched, *[swap_core(block) for block in fetched]]

    def core_half(own):
        return lax.dynamic_slice_in_dim(own, core * half, half, 0)

    wide_gains = jnp.pad(jnp.concatenate(gain_columns, axis=1), ((0, 0), (0, 126)))
    projections = (query_weight, key_matrix, value_matrix, wide_gains)
    mine_qkv = jnp.concatenate([core_half(weight) for weight in projections], axis=1).astype(BF)
    own_qkv = jnp.concatenate(projections, axis=1).astype(BF)
    qkv = fetch_rows(own_qkv, mine_qkv)
    own_out = out_weight.astype(BF)
    mine_out = core_half(own_out)

    own_down = down_weight.astype(BF)

    token_positions = me * rows + jnp.arange(rows, dtype=jnp.int32)
    frequency = 10000.0 ** (-jnp.arange(HEAD_SIZE // 2, dtype=F32) / (HEAD_SIZE // 2))
    angles = token_positions.astype(F32)[:, None] * frequency[None, :]
    cosine, sine = jnp.cos(angles), jnp.sin(angles)
    trig = (
        jnp.concatenate([cosine] * 4, axis=1),
        jnp.concatenate([-sine, sine, -sine, sine], axis=1),
    )

    x = tokens[0]
    starts = picture_starts[0]
    bit = line % 2

    def columns_for(place):
        at = (core * half, place * hidden_own)
        size = (half, hidden_own)
        return jnp.where(
            bit == 0, lax.dynamic_slice(gate_weight, at, size), lax.dynamic_slice(up_weight, at, size)
        ).astype(BF)

    sent = [columns_for(place) for place in places[1:]]
    sent, _ = after(sent, qkv[1:3])
    fetched = [swap_x(sent[0]), swap_y(sent[1]), swap_diagonal(sent[2])]
    query, key_value, act_one, gains, full_qkv = project(info, x, *trig, qkv)
    key_sent, fetched = after(key_value, fetched)
    key_x, key_y = swap_x(key_sent), swap_y(key_sent)
    mine_out, _ = after(mine_out, (key_x, key_y))
    out_x, out_y = swap_x(mine_out), swap_y(mine_out)
    key_values = [key_value, key_x, key_y, relay(key_x, key_y)]
    attended = attend(info, starts, query, key_values)
    (out_x, out_y), attended = after((out_x, out_y), attended)
    fetched_out = [out_x, out_y, relay(out_x, out_y)]
    out_rows = [own_out, *fetched_out, *[swap_core(block) for block in fetched_out]]

    near_columns = swap_near(jnp.stack(fetched))
    other_columns = swap_core(jnp.concatenate([jnp.stack(fetched), near_columns]))
    own_columns = [
        lax.dynamic_slice_in_dim(weight, me * hidden_own, hidden_own, 1)
        for weight in (gate_weight, up_weight)
    ]
    gate_up = [
        jnp.concatenate(own_columns, axis=1).astype(BF),
        *fetched,
        near_columns,
        other_columns,
    ]

    upstream_low = cotangent[0]
    upstream_sent, _ = after(upstream_low, attended)
    upstreams = [upstream_low, *gather_plane(upstream_sent)]
    attention, residual, act_two, full_out = out_project(info, attended, x, gains, out_rows)
    act_x, act_y, act_d = gather_parts(act_two)
    acts = [act_two, act_x, act_y]
    hidden, both_back, *act_parts, full_gu = feed_first(
        info, acts, upstreams[:3], gate_up, own_down
    )
    act_d, hidden = after(act_d, hidden)
    acts.append(jnp.concatenate(act_d))
    last_hidden, last_back, act_part = feed_last(acts[3], upstreams[3], full_gu, own_down)
    act_grads = [
        act_parts[0],
        swap_x(act_parts[1]),
        swap_y(act_parts[2]),
        swap_diagonal(act_part),
    ]
    layer_blocks = layer_parts(hidden, last_hidden, own_down)
    parts = feed_gradients(
        info, acts, both_back, last_back, hidden, last_hidden, upstreams
    )
    act_grads, (parts, layer_blocks) = after(act_grads, (parts, layer_blocks))
    output = (residual + scatter_plane(*layer_blocks)).astype(BF)[None]

    grad_residual, grad_low, query_back, *kv_parts = attend_back(
        info,
        starts,
        act_grads,
        upstream_low,
        residual,
        gains,
        query,
        key_values,
        attended,
        trig,
        full_out,
    )
    kv_sums = [
        kv_parts[0],
        swap_x(kv_parts[1]),
        swap_y(kv_parts[2]),
        swap_diagonal(kv_parts[3]),
    ]

    def across(own, for_x, for_y, for_d):
        return [own, swap_x(for_x), swap_y(for_y), swap_diagonal(for_d)]

    act_sent, output = after(act_one, output)
    keep, send = query_gradients(info, act_sent, attention, query_back, grad_low)
    feed_own = lax.psum_scatter(parts, "dp", scatter_dimension=0, tiled=True)[0]
    feed_own, _ = after(feed_own, (keep, send))
    feed_own = jnp.concatenate(
        [
            feed_own[:half],
            swap_x(feed_own[half : 2 * half]),
            swap_y(feed_own[2 * half : 3 * half]),
            swap_diagonal(feed_own[3 * half : 4 * half]),
            feed_own[4 * half :],
        ]
    )
    kv_sums[0], (keep, send, feed_own) = after(kv_sums[0], (keep, send, feed_own))
    received = swap_core(send)
    key_back, second_keep, second_send = key_gradients(info, act_one, kv_sums, trig)
    pair = pair_sum(keep, received, second_keep, swap_core(second_send))
    plane_parts = across(*pair)

    feed_whole = lax.all_gather(feed_own, "dp", axis=0)

    input_grad = input_back(query_back, key_back, x, gains, grad_residual, full_qkv)[None]
    plane_parts, input_grad = after(plane_parts, input_grad)
    near_sent, keep = plane_sum(info, plane_parts)
    near = swap_near(near_sent)
    far = swap_far((keep[1] + near[1]).astype(BF))
    line_own = (keep[0] + near[0] + far).astype(BF)
    pair_own = jnp.stack([line_own, swap_far(line_own)])
    near_own = swap_near(pair_own)

    feed_gain_grad, feed_squares = feed_totals(
        info, feed_whole, gate_weight, up_weight, gain_columns[1]
    )
    near_own, feed_squares = after(near_own, feed_squares)
    pieces = [pair_own, near_own, swap_core(pair_own), swap_core(near_own)]
    attention_gain_grad, squares = attention_totals(
        info, pieces, query_weight, key_matrix, value_matrix, gain_columns[0], feed_squares
    )
    *renewed, norm = update(
        info,
        across(squares, squares, squares, squares),
        pieces,
        feed_whole,
        moments[:7],
        masters[:7],
    )
    gradient_norm = norm[0, 0]
    clip_factor = jnp.minimum(1.0, jnp.sqrt(F32(PARAMS)) / (gradient_norm + 1e-06))
    momenta, updated = list(renewed[:7]), list(renewed[7:])
    for k, gradient in ((7, attention_gain_grad[:, 0]), (8, feed_gain_grad[:, 0])):
        momenta.append(momentum_beta * moments[k] + clip_factor * gradient)
        updated.append(
            masters[k] * (1.0 - learning_rate * weight_decay) - learning_rate * momenta[k]
        )
    return (output, input_grad, *momenta, *updated, gradient_norm)


def solution(mesh):
    fits = mesh.shape["seq"] == 4 and mesh.shape["dp"] == 8
    body = fast_device if fits else per_device
    return jax.shard_map(
        body,
        mesh=mesh,
        in_specs=(
            P("dp", "seq", None),
            P("dp", "seq", None),
            P("dp", None),
            P("seq", None),
            P("seq", None),
            P("seq", None),
            P("seq", None),
            P("seq", None),
            P("seq", None),
            P("seq", None),
            P("seq"),
            P("seq"),
            P("seq", None),
            P("seq", None),
            P("seq", None),
            P("seq", None),
            P("seq", None),
            P("seq", None),
            P("seq", None),
            P("seq"),
            P("seq"),
        ),
        out_specs=(
            P("dp", "seq", None),
            P("dp", "seq", None),
            P("seq", None),
            P("seq", None),
            P("seq", None),
            P("seq", None),
            P("seq", None),
            P("seq", None),
            P("seq", None),
            P("seq"),
            P("seq"),
            P("seq", None),
            P("seq", None),
            P("seq", None),
            P("seq", None),
            P("seq", None),
            P("seq", None),
            P("seq", None),
            P("seq"),
            P("seq"),
            P(),
        ),
        check_vma=False,
    )
```

```python
from functools import partial
import math

import jax
import jax.numpy as jnp
from jax import lax
from jax.experimental import pallas as pl
from jax.experimental.pallas import tpu as pltpu
from jax.sharding import PartitionSpec as P

QUERY_HEAD_COUNT = 18
KEY_VALUE_HEADS = 6
HEAD_SIZE = 64
PIECE = 256
PARAMS = 14158080


learning_rate = 0.25
weight_decay = 0.1
momentum_beta = 0.5


def rms_scale(values, scaling):
    return values * lax.rsqrt(jnp.mean(values * values, axis=-1, keepdims=True) + 1e-05) * scaling


def apply_rotary(values, token_positions):
    half_width = values.shape[-1] // 2
    frequency = 10000.0 ** (-jnp.arange(half_width, dtype=jnp.float32) / half_width)
    angles = token_positions.astype(jnp.float32)[:, None] * frequency[None, :]
    cosine = jnp.cos(angles)[:, None, :]
    sine_part = jnp.sin(angles)[:, None, :]
    leading = values[..., :half_width]
    trailing = values[..., half_width:]
    return jnp.concatenate(
        [leading * cosine - trailing * sine_part, trailing * cosine + leading * sine_part], axis=-1
    )


def swiglu(gate_values, up_values):
    return jax.nn.silu(gate_values) * up_values


def piece_number(token_positions, starts):
    inside = (token_positions[:, None] >= starts[None, :]) & (
        token_positions[:, None] < starts[None, :] + PIECE
    )
    numbers = jnp.arange(starts.shape[0], dtype=jnp.int32) + 1
    return jnp.sum(jnp.where(inside, numbers[None, :], 0), axis=1) - 1


def visible(query_position, query_piece, key_position, key_piece):
    earlier = key_position[None, :] <= query_position[:, None]
    same_piece = (query_piece[:, None] == key_piece[None, :]) & (query_piece[:, None] >= 0)
    return earlier | same_piece


def per_device(
    tokens,
    cotangent,
    picture_starts,
    query_weight,
    key_matrix,
    value_matrix,
    out_weight,
    gate_weight,
    up_weight,
    down_weight,
    attention_gain,
    feed_gain,
    query_moment,
    key_velocity,
    value_velocity,
    out_moment,
    gate_moment,
    up_moment,
    down_moment,
    attention_moment,
    feed_moment,
):
    masters = (
        query_weight,
        key_matrix,
        value_matrix,
        out_weight,
        gate_weight,
        up_weight,
        down_weight,
        attention_gain,
        feed_gain,
    )
    moments = (
        query_moment,
        key_velocity,
        value_velocity,
        out_moment,
        gate_moment,
        up_moment,
        down_moment,
        attention_moment,
        feed_moment,
    )
    shard_query = query_weight.astype(jnp.bfloat16)
    shard_key = key_matrix.astype(jnp.bfloat16)
    shard_value = value_matrix.astype(jnp.bfloat16)
    shard_out = out_weight.astype(jnp.bfloat16)
    shard_gate = gate_weight.astype(jnp.bfloat16)
    shard_up = up_weight.astype(jnp.bfloat16)
    shard_down = down_weight.astype(jnp.bfloat16)
    shard_gain_one = attention_gain.astype(jnp.bfloat16)
    shard_gain_two = feed_gain.astype(jnp.bfloat16)
    gathered = (
        lax.all_gather(shard_query, "seq", axis=0, tiled=True),
        lax.all_gather(shard_key, "seq", axis=0, tiled=True),
        lax.all_gather(shard_value, "seq", axis=0, tiled=True),
        lax.all_gather(shard_out, "seq", axis=0, tiled=True),
        lax.all_gather(shard_gate, "seq", axis=0, tiled=True),
        lax.all_gather(shard_up, "seq", axis=0, tiled=True),
        lax.all_gather(shard_down, "seq", axis=0, tiled=True),
        lax.all_gather(shard_gain_one, "seq", axis=0, tiled=True),
        lax.all_gather(shard_gain_two, "seq", axis=0, tiled=True),
    )
    full_query, complete_key, complete_value, full_out, full_gate, full_up, full_down = gathered[:7]
    gain_one = gathered[7].astype(jnp.float32)
    gain_two = gathered[8].astype(jnp.float32)
    group_size = lax.axis_size("seq")
    local_rows = tokens.shape[1]
    sequence_length = local_rows * group_size
    heads_per_group = QUERY_HEAD_COUNT // KEY_VALUE_HEADS
    token_positions = lax.axis_index("seq") * local_rows + jnp.arange(local_rows, dtype=jnp.int32)
    starts = picture_starts[0]
    query_piece = piece_number(token_positions, starts)
    key_positions = jnp.arange(sequence_length, dtype=jnp.int32)
    key_pieces = piece_number(key_positions, starts)
    layer_input = tokens[0].astype(jnp.float32)
    normed_one, pull_norm_one = jax.vjp(rms_scale, layer_input, gain_one)
    first_activation = normed_one.astype(jnp.bfloat16)
    rotation = partial(apply_rotary, token_positions=token_positions)
    query_linear = jnp.dot(
        first_activation, full_query, preferred_element_type=jnp.float32
    ).reshape(local_rows, QUERY_HEAD_COUNT, HEAD_SIZE)
    rotated_query, pull_query = jax.vjp(rotation, query_linear)
    query_reduced = rotated_query.astype(jnp.bfloat16).reshape(
        local_rows, KEY_VALUE_HEADS, heads_per_group, HEAD_SIZE
    )
    key_linear = jnp.dot(
        first_activation, complete_key, preferred_element_type=jnp.float32
    ).reshape(local_rows, KEY_VALUE_HEADS, HEAD_SIZE)
    rotated_key, key_pullback = jax.vjp(rotation, key_linear)
    key_reduced = rotated_key.astype(jnp.bfloat16).reshape(local_rows, KEY_VALUE_HEADS * HEAD_SIZE)
    value_reduced = jnp.dot(
        first_activation, complete_value, preferred_element_type=jnp.float32
    ).astype(jnp.bfloat16)
    every_key_row, every_value_row = (
        lax.all_gather(key_reduced, "seq", axis=0, tiled=True),
        lax.all_gather(value_reduced, "seq", axis=0, tiled=True),
    )
    every_key_row = every_key_row.reshape(sequence_length, KEY_VALUE_HEADS, HEAD_SIZE)
    every_value_row = every_value_row.reshape(sequence_length, KEY_VALUE_HEADS, HEAD_SIZE)
    rows_per_block = math.gcd(512, sequence_length)
    count_of_blocks = sequence_length // rows_per_block
    last_position = token_positions[local_rows - 1]
    last_piece = query_piece[local_rows - 1]

    def needed(number):
        first_row = number * rows_per_block
        return (first_row <= last_position) | (last_piece >= 0) & (
            key_pieces[first_row] == last_piece
        )

    def block_scores(number):
        first_row = number * rows_per_block
        key_block = lax.dynamic_slice_in_dim(every_key_row, first_row, rows_per_block, 0)
        value_block = lax.dynamic_slice_in_dim(every_value_row, first_row, rows_per_block, 0)
        allowed = visible(
            token_positions,
            query_piece,
            lax.dynamic_slice_in_dim(key_positions, first_row, rows_per_block, 0),
            lax.dynamic_slice_in_dim(key_pieces, first_row, rows_per_block, 0),
        )
        raw_scores = jnp.einsum(
            "qhgd,khd->hgqk", query_reduced, key_block, preferred_element_type=jnp.float32
        )
        exponent = jnp.where(allowed[None, None], jnp.exp(raw_scores * 0.125), 0.0)
        return (key_block, value_block, exponent)

    def unchanged(current):
        return current

    def forward_step(number, running):

        def forward_compute(current):
            summed, totals = current
            key_block, value_block, exponent = block_scores(number)
            summed = summed + jnp.einsum(
                "hgqk,khd->hgqd",
                exponent.astype(jnp.bfloat16),
                value_block,
                preferred_element_type=jnp.float32,
            )
            return (summed, totals + jnp.sum(exponent, axis=-1))

        return lax.cond(needed(number), forward_compute, unchanged, running)

    initial_sum = jnp.zeros((KEY_VALUE_HEADS, heads_per_group, local_rows, HEAD_SIZE), jnp.float32)
    initial_total = jnp.zeros((KEY_VALUE_HEADS, heads_per_group, local_rows), jnp.float32)
    summed, totals = lax.fori_loop(0, count_of_blocks, forward_step, (initial_sum, initial_total))
    attended = summed / totals[..., None]
    attention = (
        jnp.transpose(attended, (2, 0, 1, 3))
        .reshape(local_rows, QUERY_HEAD_COUNT * HEAD_SIZE)
        .astype(jnp.bfloat16)
    )
    residual = layer_input + jnp.dot(attention, full_out, preferred_element_type=jnp.float32)
    normed_two, pull_norm_two = jax.vjp(rms_scale, residual, gain_two)
    act_two = normed_two.astype(jnp.bfloat16)
    gate_linear = jnp.dot(act_two, full_gate, preferred_element_type=jnp.float32)
    up_linear = jnp.dot(act_two, full_up, preferred_element_type=jnp.float32)
    hidden_full, pull_swiglu = jax.vjp(swiglu, gate_linear, up_linear)
    hidden = hidden_full.astype(jnp.bfloat16)
    layer_out = residual + jnp.dot(hidden, full_down, preferred_element_type=jnp.float32)
    output = layer_out.astype(jnp.bfloat16)[None]
    upstream = cotangent[0].astype(jnp.float32)
    upstream_low = upstream.astype(jnp.bfloat16)
    grad_down = jnp.einsum("nf,nd->fd", hidden, upstream_low, preferred_element_type=jnp.float32)
    grad_hidden = jnp.einsum(
        "nd,fd->nf", upstream_low, full_down, preferred_element_type=jnp.float32
    )
    grad_gate_full, grad_up_full = pull_swiglu(grad_hidden)
    gate_back = grad_gate_full.astype(jnp.bfloat16)
    up_back = grad_up_full.astype(jnp.bfloat16)
    grad_gate = jnp.einsum("nd,nf->df", act_two, gate_back, preferred_element_type=jnp.float32)
    grad_up = jnp.einsum("nd,nf->df", act_two, up_back, preferred_element_type=jnp.float32)
    grad_act_two = jnp.einsum(
        "nf,df->nd", gate_back, full_gate, preferred_element_type=jnp.float32
    ) + jnp.einsum("nf,df->nd", up_back, full_up, preferred_element_type=jnp.float32)
    residual_norm_grad, grad_gain_two = pull_norm_two(grad_act_two)
    grad_residual = upstream + residual_norm_grad
    residual_back = grad_residual.astype(jnp.bfloat16)
    grad_out = jnp.einsum("nk,nd->kd", attention, residual_back, preferred_element_type=jnp.float32)
    attention_pullback = jnp.einsum(
        "nd,kd->nk", residual_back, full_out, preferred_element_type=jnp.float32
    ).astype(jnp.bfloat16)
    attention_pullback = jnp.transpose(
        attention_pullback.reshape(local_rows, KEY_VALUE_HEADS, heads_per_group, HEAD_SIZE),
        (1, 2, 0, 3),
    )
    back_full = attention_pullback.astype(jnp.float32)
    scaled_back = (back_full / totals[..., None]).astype(jnp.bfloat16)
    total_back = -jnp.sum(back_full * attended, axis=-1) / totals
    query_heads = jnp.transpose(query_reduced, (1, 2, 0, 3))

    def backward_step(number, running):

        def backward_compute(current):
            grad_query_sum, key_gradient_rows, value_gradient_rows = current
            first_row = number * rows_per_block
            key_block, value_block, exponent = block_scores(number)
            through = jnp.einsum(
                "hgqd,khd->hgqk", scaled_back, value_block, preferred_element_type=jnp.float32
            )
            score_back = (exponent * (through + total_back[..., None])).astype(jnp.bfloat16)
            grad_query_sum = (
                grad_query_sum
                + jnp.einsum(
                    "hgqk,khd->hgqd", score_back, key_block, preferred_element_type=jnp.float32
                )
                * 0.125
            )
            key_part = (
                jnp.einsum(
                    "hgqk,hgqd->khd", score_back, query_heads, preferred_element_type=jnp.float32
                )
                * 0.125
            )
            value_part = jnp.einsum(
                "hgqk,hgqd->khd",
                exponent.astype(jnp.bfloat16),
                scaled_back,
                preferred_element_type=jnp.float32,
            )
            key_gradient_rows = lax.dynamic_update_slice_in_dim(
                key_gradient_rows, key_part, first_row, 0
            )
            value_gradient_rows = lax.dynamic_update_slice_in_dim(
                value_gradient_rows, value_part, first_row, 0
            )
            return (grad_query_sum, key_gradient_rows, value_gradient_rows)

        return lax.cond(needed(number), backward_compute, unchanged, running)

    initial_query = jnp.zeros(
        (KEY_VALUE_HEADS, heads_per_group, local_rows, HEAD_SIZE), jnp.float32
    )
    initial_keys = jnp.zeros((sequence_length, KEY_VALUE_HEADS, HEAD_SIZE), jnp.float32)
    grad_query_sum, key_gradient_rows, value_gradient_rows = lax.fori_loop(
        0, count_of_blocks, backward_step, (initial_query, initial_keys, initial_keys)
    )
    local_key_rows, value_own = (
        lax.psum_scatter(
            key_gradient_rows.reshape(sequence_length, KEY_VALUE_HEADS * HEAD_SIZE),
            "seq",
            scatter_dimension=0,
            tiled=True,
        ),
        lax.psum_scatter(
            value_gradient_rows.reshape(sequence_length, KEY_VALUE_HEADS * HEAD_SIZE),
            "seq",
            scatter_dimension=0,
            tiled=True,
        ),
    )
    key_back = (
        key_pullback(local_key_rows.reshape(local_rows, KEY_VALUE_HEADS, HEAD_SIZE))[0]
        .reshape(local_rows, KEY_VALUE_HEADS * HEAD_SIZE)
        .astype(jnp.bfloat16)
    )
    query_rot_grad = jnp.transpose(grad_query_sum, (2, 0, 1, 3)).reshape(
        local_rows, QUERY_HEAD_COUNT, HEAD_SIZE
    )
    query_back = (
        pull_query(query_rot_grad)[0]
        .reshape(local_rows, QUERY_HEAD_COUNT * HEAD_SIZE)
        .astype(jnp.bfloat16)
    )
    value_back = value_own.astype(jnp.bfloat16)
    grad_query = jnp.einsum(
        "nd,nk->dk", first_activation, query_back, preferred_element_type=jnp.float32
    )
    grad_key = jnp.einsum(
        "nd,nk->dk", first_activation, key_back, preferred_element_type=jnp.float32
    )
    grad_value = jnp.einsum(
        "nd,nk->dk", first_activation, value_back, preferred_element_type=jnp.float32
    )
    grad_act_one = jnp.einsum(
        "nk,dk->nd", query_back, full_query, preferred_element_type=jnp.float32
    )
    grad_act_one = grad_act_one + jnp.einsum(
        "nk,dk->nd", key_back, complete_key, preferred_element_type=jnp.float32
    )
    grad_act_one = grad_act_one + jnp.einsum(
        "nk,dk->nd", value_back, complete_value, preferred_element_type=jnp.float32
    )
    input_norm_grad, grad_gain_one = pull_norm_one(grad_act_one)
    input_grad = (grad_residual + input_norm_grad)[None]
    shard_grads = (
        lax.psum_scatter(grad_query, "seq", scatter_dimension=0, tiled=True),
        lax.psum_scatter(grad_key, "seq", scatter_dimension=0, tiled=True),
        lax.psum_scatter(grad_value, "seq", scatter_dimension=0, tiled=True),
        lax.psum_scatter(grad_out, "seq", scatter_dimension=0, tiled=True),
        lax.psum_scatter(grad_gate, "seq", scatter_dimension=0, tiled=True),
        lax.psum_scatter(grad_up, "seq", scatter_dimension=0, tiled=True),
        lax.psum_scatter(grad_down, "seq", scatter_dimension=0, tiled=True),
        lax.psum_scatter(grad_gain_one, "seq", scatter_dimension=0, tiled=True),
        lax.psum_scatter(grad_gain_two, "seq", scatter_dimension=0, tiled=True),
    )
    gradients = lax.psum(
        (
            shard_grads[0],
            shard_grads[1],
            shard_grads[2],
            shard_grads[3],
            shard_grads[4],
            shard_grads[5],
            shard_grads[6],
            shard_grads[7],
            shard_grads[8],
        ),
        "dp",
    )
    squares = jnp.float32(0.0)
    for gradient in gradients:
        squares = squares + jnp.sum(gradient * gradient)
    gradient_norm = jnp.sqrt(lax.psum(squares, "seq"))
    clip_factor = jnp.minimum(1.0, jnp.sqrt(jnp.float32(PARAMS)) / (gradient_norm + 1e-06))
    momenta = [
        momentum_beta * moment + clip_factor * gradient
        for moment, gradient in zip(moments, gradients)
    ]
    updated = [
        master * (1.0 - learning_rate * weight_decay) - learning_rate * momentum
        for master, momentum in zip(masters, momenta)
    ]
    return (
        output,
        input_grad,
        momenta[0],
        momenta[1],
        momenta[2],
        momenta[3],
        momenta[4],
        momenta[5],
        momenta[6],
        momenta[7],
        momenta[8],
        updated[0],
        updated[1],
        updated[2],
        updated[3],
        updated[4],
        updated[5],
        updated[6],
        updated[7],
        updated[8],
        gradient_norm,
    )


BF = jnp.bfloat16
F32 = jnp.float32


def swap_x(value):
    return lax.ppermute(value, "seq", [(i, i ^ 1) for i in range(4)])


def swap_y(value):
    return lax.ppermute(value, "seq", [(i, i ^ 2) for i in range(4)])


def swap_diagonal(value):
    return lax.ppermute(value, "seq", [(i, i ^ 3) for i in range(4)])


def swap_core(value):
    return lax.ppermute(value, "dp", [(i, i ^ 1) for i in range(8)])


def move_up(value):
    return lax.ppermute(value, "dp", [(i, i + 2) for i in range(6)])


def move_down(value):
    return lax.ppermute(value, "dp", [(i + 2, i) for i in range(6)])


def gather_parts(value):
    middle = value.shape[0] // 2
    from_x = swap_x(value)
    from_y = swap_y(value)
    return from_x, from_y, (swap_x(from_y[:middle]), swap_y(from_x[middle:]))


def relay(from_x, from_y):
    middle = from_x.shape[0] // 2
    return jnp.concatenate([swap_x(from_y[:middle]), swap_y(from_x[middle:])])


def gather_plane(value):
    from_x, from_y, from_d = gather_parts(value)
    return from_x, from_y, jnp.concatenate(from_d)


def scatter_plane(own, for_x, for_y, for_d):
    from_x = swap_x(for_x.astype(BF))
    from_y = swap_y(for_y.astype(BF))
    from_d = swap_diagonal(for_d.astype(BF))
    return own.astype(F32) + from_x + from_y + from_d


def swap_near(value):
    return lax.ppermute(value, "dp", [(i, i ^ 2) for i in range(8)])


def swap_far(value):
    return lax.ppermute(value, "dp", [(i, i ^ 4) for i in range(8)])


def after(value, other):
    return lax.optimization_barrier((value, other))


def index_array(*numbers):
    return jnp.stack([jnp.asarray(number, jnp.int32) for number in numbers])


COLUMNS = 384


def whole(shape):
    return pl.BlockSpec(shape, lambda *_: (0,) * len(shape))


def once(shape):
    return pl.BlockSpec(shape, lambda *_: (0,) * len(shape), pipeline_mode=pl.Buffered(1))


ANY = pl.BlockSpec(memory_space=pl.ANY)
SCALARS = pl.BlockSpec(memory_space=pltpu.SMEM)


def params(mebibytes):
    return pltpu.CompilerParams(vmem_limit_bytes=mebibytes * 1024 * 1024)


def cost(flops, transferred):
    return pl.CostEstimate(flops=flops // 1000, bytes_accessed=transferred // 1000, transcendentals=0)


def start_rows(target, blocks, info, semaphores):
    own, fetched, other = blocks[0], blocks[1:4], blocks[4:7]
    shard, half = own.shape[0], own.shape[0] // 2
    copies = [(own, info[0] * shard, shard)]
    for j in range(3):
        first = (info[0] ^ (j + 1)) * shard
        copies.append((fetched[j], first + info[2] * half, half))
        copies.append((other[j], first + (1 - info[2]) * half, half))
    started = []
    for j, (source, row, count) in enumerate(copies):
        row = pl.multiple_of(row, 16)
        copy = pltpu.make_async_copy(source, target.at[pl.ds(row, count)], semaphores.at[j])
        copy.start()
        started.append(copy)
    return started


def partners(value):
    lanes = value.shape[1]
    low = lax.broadcasted_iota(jnp.int32, value.shape, 1) % HEAD_SIZE < HEAD_SIZE // 2
    return jnp.where(low, pltpu.roll(value, lanes - 32, 1), pltpu.roll(value, 32, 1))


def rotate(value, cosine, sine):
    return value * cosine + partners(value) * sine


def transposed(left, right):
    return lax.dot_general(left, right, (((1,), (1,)), ((), ())), preferred_element_type=F32)


def row_mean(value):
    return jnp.mean(value, axis=-1, keepdims=True)


def project_kernel(info, x, cosine, sine, *refs):
    blocks, outs, semaphores = refs[:7], refs[7:12], refs[12]
    query, key_value, act, gains, weight = outs
    copies = start_rows(weight, blocks, info, semaphores)
    values = x[...].astype(F32)
    normed = values * lax.rsqrt(row_mean(values * values) + 1e-05)
    cos = jnp.concatenate([cosine[...]] * 3, axis=1)
    sin = jnp.concatenate([sine[...]] * 3, axis=1)
    for copy in copies:
        copy.wait()
    gains[...] = weight[:, 5 * COLUMNS :].astype(F32).T[:8]
    low = (normed * gains[0:1, :]).astype(BF)
    act[...] = low
    for j in range(5):
        part = jnp.dot(
            low, weight[:, j * COLUMNS : (j + 1) * COLUMNS], preferred_element_type=F32
        )
        if j < 4:
            part = rotate(part, cos, sin)
        part = part.astype(BF)
        if j < 3:
            query[:, j * COLUMNS : (j + 1) * COLUMNS] = part * 0.125
        else:
            key_value[:, (j - 3) * COLUMNS : (j - 2) * COLUMNS] = part


def project(info, x, cosine, sine, blocks):
    rows, width = x.shape
    columns = blocks[0].shape[1]
    shapes = [
        ((rows, width), BF),
        ((rows, 2 * COLUMNS), BF),
        ((rows, width), BF),
        ((8, width), F32),
        ((width, columns), BF),
    ]
    return pl.pallas_call(
        project_kernel,
        in_specs=[SCALARS, *[whole(a.shape) for a in (x, cosine, sine)]] + [ANY] * 7,
        out_specs=[whole(shape) for shape, _ in shapes],
        out_shape=[jax.ShapeDtypeStruct(shape, kind) for shape, kind in shapes],
        scratch_shapes=[pltpu.SemaphoreType.DMA((7,))],
        compiler_params=params(24),
        cost_estimate=cost(2 * rows * width * columns, 8_000_000),
        name="project",
    )(info, x, cosine, sine, *blocks)


def piece_of(positions, starts, count):
    piece = jnp.full(positions.shape, -1, jnp.int32)
    for j in range(count):
        first = starts[j]
        piece = jnp.where((positions >= first) & (positions < first + PIECE), j, piece)
    return piece


def visibility(info, starts, count, rows, keys_first):
    axis = 1 if keys_first else 0
    query_shape = (1, rows) if keys_first else (rows, 1)
    query_at = info[0] * rows + lax.broadcasted_iota(jnp.int32, query_shape, axis)
    query_piece = piece_of(query_at, starts, count)
    biases = []
    for j in range(4):
        key_shape = query_shape[::-1]
        key_at = (info[0] ^ j) * rows + lax.broadcasted_iota(jnp.int32, key_shape, 1 - axis)
        key_piece = piece_of(key_at, starts, count)
        seen = (key_at <= query_at) | ((key_piece == query_piece) & (query_piece >= 0))
        biases.append(jnp.where(seen, 0.0, -1e30).astype(F32))
    return jnp.concatenate(biases, axis=1 - axis)


def attend_kernel(info, starts, query, kv0, kv1, kv2, kv3, attended, every):
    rows = query.shape[0]
    for j, block in enumerate((kv0, kv1, kv2, kv3)):
        every[j * rows : (j + 1) * rows, :] = block[...]
    bias = visibility(info, starts, starts.shape[0], rows, False)

    def pair(p, carry):
        at = pl.multiple_of(p * 128, 128)
        keys = every[:, pl.ds(at, 128)]
        values = every[:, pl.ds(COLUMNS + at, 128)]
        queries = query[:, pl.ds(pl.multiple_of(p * COLUMNS, 128), COLUMNS)]
        results = []
        for k in range(2):
            key = keys[:, k * 64 : (k + 1) * 64]
            value = values[:, k * 64 : (k + 1) * 64]
            for h in range(3):
                at = (k * 3 + h) * 64
                scores = transposed(queries[:, at : at + 64], key)
                exponent = jnp.exp(scores + bias)
                total = jnp.sum(exponent, axis=-1, keepdims=True)
                summed = jnp.dot(exponent.astype(BF), value, preferred_element_type=F32)
                results.append(summed / total)
        attended[:, pl.ds(pl.multiple_of(p * COLUMNS, 128), COLUMNS)] = jnp.concatenate(
            results, axis=1
        )
        return carry

    lax.fori_loop(0, 3, pair, 0)


def attend(info, starts, query, key_values):
    rows, width = query.shape
    square = whole((rows, width))
    return pl.pallas_call(
        attend_kernel,
        in_specs=[SCALARS, SCALARS, square] + [whole(a.shape) for a in key_values],
        out_specs=square,
        out_shape=jax.ShapeDtypeStruct((rows, width), F32),
        scratch_shapes=[pltpu.VMEM((4 * rows, 2 * COLUMNS), BF)],
        compiler_params=params(20),
        cost_estimate=cost(4 * rows * 4 * rows * width * 4, 10_000_000),
        name="attend",
    )(info, starts, query, *key_values)


def out_project_kernel(info, attended, x, gains, *refs):
    blocks, (attention, residual, act, weight), semaphores = refs[:7], refs[7:11], refs[11]
    copies = start_rows(weight, blocks, info, semaphores)
    low = attended[...].astype(BF)
    attention[...] = low
    for copy in copies:
        copy.wait()
    summed = x[...].astype(F32) + jnp.dot(low, weight[...], preferred_element_type=F32)
    residual[...] = summed
    scale = lax.rsqrt(row_mean(summed * summed) + 1e-05)
    act[...] = (summed * scale * gains[1:2, :]).astype(BF)


def out_project(info, attended, x, gains, blocks):
    rows, width = x.shape
    square = whole((rows, width))
    return pl.pallas_call(
        out_project_kernel,
        in_specs=[SCALARS, square, square, whole(gains.shape)] + [ANY] * 7,
        out_specs=[square] * 3 + [whole((width, width))],
        out_shape=[jax.ShapeDtypeStruct((rows, width), t) for t in (BF, F32, BF)]
        + [jax.ShapeDtypeStruct((width, width), BF)],
        scratch_shapes=[pltpu.SemaphoreType.DMA((7,))],
        compiler_params=params(18),
        cost_estimate=cost(2 * rows * width * width, 6_000_000),
        name="out_project",
    )(info, attended, x, gains, *blocks)


def feed_blocks(acts, ups, weight, down, hidden, back, outs):
    rows = acts[0].shape[0]
    units = down.shape[0]
    for j in range(len(acts)):
        span = slice(j * rows, (j + 1) * rows)
        both = jnp.dot(acts[j][...], weight[...], preferred_element_type=F32)
        gate, up = both[:, :units], both[:, units:]
        grad = transposed(ups[j][...], down[...])
        logistic = 1.0 / (1.0 + jnp.exp(-gate))
        smooth = gate * logistic
        hidden[span, :] = (smooth * up).astype(BF)
        slope = logistic * (1.0 + gate * (1.0 - logistic))
        back[span, :units] = (grad * up * slope).astype(BF)
        back[span, units:] = (grad * smooth).astype(BF)
        outs[j][...] = transposed(back[span, :], weight[...]).astype(outs[j].dtype)


def feed_first_kernel(info, *refs):
    acts, ups, refs = refs[:3], refs[3:6], refs[6:]
    own, fetched, near, other, down = refs[0], refs[1:4], refs[4], refs[5], refs[6]
    hidden, back, outs, weight, semaphores = refs[7], refs[8], refs[9:12], refs[12], refs[13]
    units = down.shape[0]
    shard, half = own.shape[0], own.shape[0] // 2
    bit = info[1] % 2
    copies = [(own, weight.at[pl.ds(pl.multiple_of(info[0] * shard, 16), shard)])]
    for j in range(3):
        first = (info[0] ^ (j + 1)) * shard
        mine = pl.ds(pl.multiple_of(first + info[2] * half, 16), half)
        theirs = pl.ds(pl.multiple_of(first + (1 - info[2]) * half, 16), half)
        same = pl.ds(pl.multiple_of(bit * units, 128), units)
        opposite = pl.ds(pl.multiple_of((1 - bit) * units, 128), units)
        copies.append((fetched[j], weight.at[mine, same]))
        copies.append((near.at[j], weight.at[mine, opposite]))
        copies.append((other.at[j], weight.at[theirs, same]))
        copies.append((other.at[3 + j], weight.at[theirs, opposite]))
    started = []
    for j, (source, target) in enumerate(copies):
        copy = pltpu.make_async_copy(source, target, semaphores.at[j])
        copy.start()
        started.append(copy)
    for copy in started:
        copy.wait()
    feed_blocks(acts, ups, weight, down, hidden, back, outs)


def feed_last_kernel(act, up, weight, down, hidden, back, out):
    feed_blocks([act], [up], weight, down, hidden, back, [out])


def feed(kernel, info, acts, ups, weights, specs, down, kinds, extra, scratch):
    count = len(acts)
    rows, width = acts[0].shape
    units = down.shape[0]
    square = whole((rows, width))
    shapes = [((count * rows, units), BF), ((count * rows, 2 * units), BF)]
    shapes += [((rows, width), kind) for kind in kinds] + extra
    return pl.pallas_call(
        kernel,
        in_specs=[SCALARS] * len(info) + [square] * (2 * count) + specs + [whole(down.shape)],
        out_specs=[whole(shape) for shape, _ in shapes],
        out_shape=[jax.ShapeDtypeStruct(shape, kind) for shape, kind in shapes],
        scratch_shapes=scratch,
        compiler_params=params(28 if count == 3 else 20),
        cost_estimate=cost(10 * count * rows * width * units, 20_000_000),
        name="feed",
    )(*info, *acts, *ups, *weights, down)


def feed_first(info, acts, ups, blocks, down):
    full = (acts[0].shape[1], 2 * down.shape[0])
    return feed(
        feed_first_kernel,
        [info],
        acts,
        ups,
        blocks,
        [ANY] * 6,
        down,
        (F32, BF, BF),
        [(full, BF)],
        [pltpu.SemaphoreType.DMA((13,))],
    )


def feed_last(act, up, weight, down):
    return feed(
        feed_last_kernel, [], [act], [up], [weight], [whole(weight.shape)], down, (BF,), [], []
    )


def layer_parts_kernel(hidden, last, down, *outs):
    rows = last.shape[0]
    for j in range(4):
        left = last[...] if j == 3 else hidden[j * rows : (j + 1) * rows, :]
        outs[j][...] = jnp.dot(left, down[...], preferred_element_type=F32).astype(outs[j].dtype)


def layer_parts(hidden, last, down):
    rows, units = last.shape
    width = down.shape[1]
    return pl.pallas_call(
        layer_parts_kernel,
        in_specs=[whole(hidden.shape), whole(last.shape), whole(down.shape)],
        out_specs=[whole((rows, width))] * 4,
        out_shape=[jax.ShapeDtypeStruct((rows, width), t) for t in (F32, BF, BF, BF)],
        compiler_params=params(14),
        cost_estimate=cost(8 * rows * units * width, 8_000_000),
        name="layer_parts",
    )(hidden, last, down)


def attend_back_kernel(info, starts, g0, g1, g2, g3, upstream, residual, gains, query, *refs):
    kvs, attended, cosine, sine, weight = refs[:4], refs[4], refs[5], refs[6], refs[7]
    grad_residual, grad_low, query_back, outs = refs[8], refs[9], refs[10], refs[11:15]
    every, back = refs[15:]
    rows = query.shape[0]
    for j, block in enumerate(kvs):
        every[j * rows : (j + 1) * rows, :] = block[...]
    act_back = g0[...] + g1[...].astype(F32) + g2[...].astype(F32) + g3[...].astype(F32)
    weighted = act_back * gains[1:2, :]
    values = residual[...]
    scale = lax.rsqrt(row_mean(values * values) + 1e-05)
    grad = upstream[...].astype(F32) + scale * (
        weighted - values * (scale * scale * row_mean(weighted * values))
    )
    grad_residual[...] = grad
    low = grad.astype(BF)
    grad_low[...] = low
    back[...] = transposed(low, weight[...]).astype(BF)
    bias = visibility(info, starts, starts.shape[0], rows, True)
    cos = jnp.concatenate([cosine[...]] * 3, axis=1)
    sin = jnp.concatenate([sine[...]] * 3, axis=1)

    def pair(p, carry):
        at = pl.multiple_of(p * 128, 128)
        wide = pl.ds(pl.multiple_of(p * COLUMNS, 128), COLUMNS)
        keys = every[:, pl.ds(at, 128)]
        values = every[:, pl.ds(COLUMNS + at, 128)]
        queries = query[:, wide]
        backs = back[:, wide].astype(F32).T
        products = backs * attended[:, wide].T
        query_parts, key_parts, value_parts = [], [], []
        for k in range(2):
            key = keys[:, k * 64 : (k + 1) * 64]
            value = values[:, k * 64 : (k + 1) * 64]
            key_t = key.T
            key_sum = value_sum = None
            for h in range(3):
                at = (k * 3 + h) * 64
                one = queries[:, at : at + 64]
                exponent = jnp.exp(transposed(key, one) + bias)
                total = jnp.sum(exponent, axis=0, keepdims=True)
                scaled = (backs[at : at + 64] / total).astype(BF)
                shift = -jnp.sum(products[at : at + 64], axis=0, keepdims=True) / total
                through = jnp.dot(value, scaled, preferred_element_type=F32)
                score = (exponent * (through + shift)).astype(BF)
                query_parts.append(jnp.dot(key_t, score, preferred_element_type=F32))
                key_part = jnp.dot(score, one, preferred_element_type=F32)
                value_part = transposed(exponent.astype(BF), scaled)
                key_sum = key_part if key_sum is None else key_sum + key_part
                value_sum = value_part if value_sum is None else value_sum + value_part
            key_parts.append(key_sum)
            value_parts.append(value_sum)
        turned = jnp.concatenate(query_parts, axis=0).T * 0.125
        query_back[:, wide] = rotate(turned, cos, -sin).astype(BF)
        key_pair = jnp.concatenate(key_parts, axis=1)
        value_pair = jnp.concatenate(value_parts, axis=1)
        for j in range(4):
            span = slice(j * rows, (j + 1) * rows)
            kind = outs[j].dtype
            at = pl.multiple_of(p * 128, 128)
            outs[j][:, pl.ds(at, 128)] = key_pair[span].astype(kind)
            outs[j][:, pl.ds(COLUMNS + at, 128)] = value_pair[span].astype(kind)
        return carry

    lax.fori_loop(0, 3, pair, 0)


def attend_back(info, starts, grads, upstream, residual, gains, query, kvs, attended, trig, weight):
    rows, width = query.shape
    square = whole((rows, width))
    table = whole(trig[0].shape)
    pair = whole((rows, 2 * COLUMNS))
    return pl.pallas_call(
        attend_back_kernel,
        in_specs=[SCALARS, SCALARS]
        + [square] * 6
        + [whole(gains.shape), square]
        + [pair] * 4
        + [square, table, table, whole(weight.shape)],
        out_specs=[square] * 3 + [pair] * 4,
        out_shape=[jax.ShapeDtypeStruct((rows, width), t) for t in (F32, BF, BF)]
        + [jax.ShapeDtypeStruct((rows, 2 * COLUMNS), t) for t in (F32, BF, BF, BF)],
        scratch_shapes=[
            pltpu.VMEM((4 * rows, 2 * COLUMNS), BF),
            pltpu.VMEM((rows, width), BF),
        ],
        compiler_params=params(60),
        cost_estimate=cost(10 * rows * 4 * rows * width * 4, 15_000_000),
        name="attend_back",
    )(info, starts, *grads, upstream, residual, gains, query, *kvs, attended, *trig, weight)


def split_rows(info, product, keep, send, columns):
    half = keep.shape[1]
    for sr in range(4):
        row = (info[0] ^ sr) * (2 * half)
        kept = pl.multiple_of(row + info[2] * half, 16)
        sent = pl.multiple_of(row + (1 - info[2]) * half, 16)
        keep[sr, :, columns] = product[pl.ds(kept, half), :].astype(BF)
        send[sr, :, columns] = product[pl.ds(sent, half), :].astype(BF)


def query_gradients_kernel(info, act, att, query_back, grad_low, keep, send, product):
    for first, (left, right) in enumerate(((act, query_back), (att, grad_low))):
        left_t = left[...].T
        for j in range(3):
            columns = slice(j * COLUMNS, (j + 1) * COLUMNS)
            product[...] = jnp.dot(left_t, right[:, columns], preferred_element_type=F32)
            at = (first * 3 + j) * COLUMNS
            split_rows(info, product, keep, send, slice(at, at + COLUMNS))


def query_gradients(info, act, att, query_back, grad_low):
    rows, width = act.shape
    half = width // 8
    square = whole((rows, width))
    out = (4, half, 2 * width)
    return pl.pallas_call(
        query_gradients_kernel,
        in_specs=[SCALARS] + [square] * 4,
        out_specs=[whole(out)] * 2,
        out_shape=[jax.ShapeDtypeStruct(out, BF)] * 2,
        scratch_shapes=[pltpu.VMEM((width, COLUMNS), F32)],
        compiler_params=params(20),
        cost_estimate=cost(4 * rows * width * width, 9_000_000),
        name="query_gradients",
    )(info, act, att, query_back, grad_low)


def key_gradients_kernel(info, act, p0, p1, p2, p3, cosine, sine, back, keep, send, product):
    summed = p0[...] + p1[...].astype(F32) + p2[...].astype(F32) + p3[...].astype(F32)
    cos = jnp.concatenate([cosine[...]] * 3, axis=1)
    sin = jnp.concatenate([sine[...]] * 3, axis=1)
    back[:, :COLUMNS] = rotate(summed[:, :COLUMNS], cos, -sin).astype(BF)
    back[:, COLUMNS:] = summed[:, COLUMNS:].astype(BF)
    left_t = act[...].T
    for j in range(2):
        columns = slice(j * COLUMNS, (j + 1) * COLUMNS)
        product[...] = jnp.dot(left_t, back[:, columns], preferred_element_type=F32)
        split_rows(info, product, keep, send, columns)


def key_gradients(info, act, parts, trig):
    rows, width = act.shape
    half = width // 8
    out = (4, half, 2 * COLUMNS)
    pair = whole((rows, 2 * COLUMNS))
    table = whole(trig[0].shape)
    return pl.pallas_call(
        key_gradients_kernel,
        in_specs=[SCALARS, whole((rows, width))] + [pair] * 4 + [table, table],
        out_specs=[pair, whole(out), whole(out)],
        out_shape=[jax.ShapeDtypeStruct((rows, 2 * COLUMNS), BF)]
        + [jax.ShapeDtypeStruct(out, BF)] * 2,
        scratch_shapes=[pltpu.VMEM((width, COLUMNS), F32)],
        compiler_params=params(14),
        cost_estimate=cost(4 * rows * width * COLUMNS, 5_000_000),
        name="key_gradients",
    )(info, act, *parts, *trig)


def input_back_kernel(query_back, key_back, x, gains, grad_residual, weight, out):
    width = x.shape[1]
    act_back = transposed(query_back[...], weight[:, :width])
    act_back = act_back + transposed(key_back[...], weight[:, width : width + 2 * COLUMNS])
    values = x[...].astype(F32)
    scale = lax.rsqrt(row_mean(values * values) + 1e-05)
    weighted = act_back * gains[0:1, :]
    out[...] = grad_residual[...] + scale * (
        weighted - values * (scale * scale * row_mean(weighted * values))
    )


def input_back(*operands):
    rows, width = operands[0].shape
    return pl.pallas_call(
        input_back_kernel,
        in_specs=[whole(a.shape) for a in operands],
        out_specs=whole((rows, width)),
        out_shape=jax.ShapeDtypeStruct((rows, width), F32),
        compiler_params=params(20),
        cost_estimate=cost(10 * rows * width * COLUMNS, 9_000_000),
        name="input_back",
    )(*operands)


def feed_gradients_kernel(
    info, a0, a1, a2, a3, back, back_last, hidden, last, u0, u1, u2, u3, out, act_t, hid_t, acc
):
    rows = a0.shape[0]
    half = a0.shape[1] // 8
    z = pl.program_id(0)

    @pl.when(z == 0)
    def _():
        for j, block in enumerate((a0, a1, a2, a3)):
            act_t[:, j * rows : (j + 1) * rows] = block[...].T
            block = last[...] if j == 3 else hidden[j * rows : (j + 1) * rows, :]
            hid_t[:, j * rows : (j + 1) * rows] = block.T

    acc[...] = jnp.dot(
        act_t[:, : 3 * rows], back[...], preferred_element_type=F32
    ) + jnp.dot(act_t[:, 3 * rows :], back_last[...], preferred_element_type=F32)
    for c in range(2):
        for sr in range(4):
            row = pl.multiple_of((info[0] ^ sr) * (2 * half) + c * half, 16)
            out[c, sr * half : (sr + 1) * half, :] = acc[pl.ds(row, half), :].astype(BF)
    left = jnp.concatenate(
        [hid_t[pl.ds(pl.multiple_of(i * 128 + z * 32, 32), 32), :] for i in range(6)]
    )
    down = jnp.zeros((192, u0.shape[1]), F32)
    for j, block in enumerate((u0, u1, u2, u3)):
        down = down + jnp.dot(
            left[:, j * rows : (j + 1) * rows], block[...], preferred_element_type=F32
        )
    for c in range(2):
        rows_of_c = jnp.concatenate(
            [down[i * 32 + c * 16 : i * 32 + (c + 1) * 16] for i in range(6)]
        ).astype(BF)
        for cb in range(3):
            first = 4 * half + cb * 96
            out[c, first : first + 96, :] = rows_of_c[:, cb * COLUMNS : (cb + 1) * COLUMNS]


def feed_gradients(info, acts, back, back_last, hidden, last, ups):
    rows, width = acts[0].shape
    units = hidden.shape[1]
    return pl.pallas_call(
        feed_gradients_kernel,
        grid=(4,),
        in_specs=[SCALARS]
        + [once((rows, width))] * 4
        + [
            pl.BlockSpec((3 * rows, COLUMNS), lambda z: (0, z)),
            pl.BlockSpec((rows, COLUMNS), lambda z: (0, z)),
            once(hidden.shape),
            once(last.shape),
        ]
        + [once((rows, width))] * 4,
        out_specs=pl.BlockSpec((2, 864, COLUMNS), lambda z: (z, 0, 0)),
        scratch_shapes=[
            pltpu.VMEM((width, 4 * rows), BF),
            pltpu.VMEM((units, 4 * rows), BF),
            pltpu.VMEM((width, COLUMNS), F32),
        ],
        out_shape=jax.ShapeDtypeStruct((8, 864, COLUMNS), BF),
        compiler_params=params(26),
        cost_estimate=cost(2 * 4 * rows * width * 3 * units, 20_000_000),
        name="feed_gradients",
    )(info, *acts, back, back_last, hidden, last, *ups)


def pair_sum_kernel(keep, received, second_keep, second_received, *outs):
    columns = keep.shape[2]
    for j in range(4):
        for span, one, other in (
            (slice(0, columns), keep, received),
            (slice(columns, None), second_keep, second_received),
        ):
            outs[j][:, span] = (one[j].astype(F32) + other[j].astype(F32)).astype(outs[j].dtype)


def pair_sum(*parts):
    shape = (parts[0].shape[1], parts[0].shape[2] + parts[2].shape[2])
    return pl.pallas_call(
        pair_sum_kernel,
        in_specs=[whole(a.shape) for a in parts],
        out_specs=[whole(shape)] * 4,
        out_shape=[jax.ShapeDtypeStruct(shape, t) for t in (F32, BF, BF, BF)],
        compiler_params=params(18),
        cost_estimate=cost(10_000_000, 5_000_000),
        name="pair_sum",
    )(*parts)


def plane_sum_kernel(info, own, from_x, from_y, from_d, near, keep):
    quarter = near.shape[2]
    for j, (target, place) in enumerate(((keep, 0), (near, 1), (keep, 2), (near, 3))):
        span = pl.ds(pl.multiple_of((info[1] ^ place) * quarter, 128), quarter)
        summed = own[:, span]
        for part in (from_x, from_y, from_d):
            summed = summed + part[:, span].astype(F32)
        target[j // 2] = summed.astype(target.dtype)


def plane_sum(info, parts):
    rows, columns = parts[0].shape
    shape = (2, rows, columns // 4)
    return pl.pallas_call(
        plane_sum_kernel,
        in_specs=[SCALARS] + [whole(a.shape) for a in parts],
        out_specs=[whole(shape)] * 2,
        out_shape=[jax.ShapeDtypeStruct(shape, t) for t in (BF, F32)],
        compiler_params=params(16),
        cost_estimate=cost(10_000_000, 5_000_000),
        name="plane_sum",
    )(info, *parts)


STEPS = 6


def attention_block(attention, step, number):
    row = pl.multiple_of((step % 3) * 48, 16)
    first = (number % 2) * COLUMNS
    return attention[(step // 3) * 4 + number // 2, pl.ds(row, 48), first : first + COLUMNS]


def feed_block(info, feed_sum, step, number):
    which, rest = divmod(number, 8)
    t, sub = divmod(rest, 2)
    row = pl.multiple_of((info[0] ^ t) * 144 + (step % 3) * 48, 16)
    return feed_sum[(which * 2 + sub) * 2 + step // 3, pl.ds(row, 48), :]


def lanes_sum(value):
    return sum(value[:, j * 128 : (j + 1) * 128] for j in range(value.shape[1] // 128))


def start_attention(info, pieces, target, semaphores):
    copies = []
    for j, piece in enumerate(pieces):
        core = info[2] if j < 2 else 1 - info[2]
        for k in range(2):
            place = core * 4 + (info[1] ^ (2 * k + j % 2))
            copy = pltpu.make_async_copy(piece.at[k], target.at[place], semaphores.at[2 * j + k])
            copy.start()
            copies.append(copy)
    return copies


def attention_scratch(pieces):
    return [pltpu.VMEM((8, *pieces[0].shape[1:]), BF), pltpu.SemaphoreType.DMA((8,))]


def feed_totals_kernel(info, feed_sum, gate, up, gain, gain_grad, squares):
    step = pl.program_id(0)
    total = jnp.zeros((48, 128), F32)
    square = jnp.zeros((48, 128), F32)
    for master, number in ((gate, 0), (up, 8)):
        for j in range(8):
            block = feed_block(info, feed_sum, step, number + j).astype(F32)
            weight = master[:, j * COLUMNS : (j + 1) * COLUMNS].astype(BF).astype(F32)
            total = total + lanes_sum(weight * block)
            square = square + lanes_sum(block * block)
    grad = jnp.sum(total, axis=1, keepdims=True) / gain[...]
    gain_grad[...] = grad
    result = jnp.sum(square.reshape(6, 8, 128), axis=0)
    result = result + jnp.sum(jnp.square(grad)) * (1.0 / 1024)
    row = pl.multiple_of(step * 16, 16)
    for e in range(8):
        for cb in range(3):
            block = feed_sum[e, pl.ds(576 + cb * 96 + row, 16), :].astype(F32)
            part = lanes_sum(block * block)
            result = result + part[:8] + part[8:]

    @pl.when(step == 0)
    def _():
        squares[...] = result

    @pl.when(step > 0)
    def _():
        squares[...] += result


def feed_totals(info, feed_sum, gate, up, gain):
    rows, columns = gate.shape
    wide = pl.BlockSpec((rows // STEPS, columns), lambda i: (i, 0))
    narrow = pl.BlockSpec((rows // STEPS, 1), lambda i: (i, 0))
    return pl.pallas_call(
        feed_totals_kernel,
        grid=(STEPS,),
        in_specs=[SCALARS, once(feed_sum.shape), wide, wide, narrow],
        out_specs=[narrow, whole((8, 128))],
        out_shape=[jax.ShapeDtypeStruct((rows, 1), F32), jax.ShapeDtypeStruct((8, 128), F32)],
        compiler_params=params(60),
        cost_estimate=cost(30_000_000, 13_000_000),
        name="feed_totals",
    )(info, feed_sum, gate, up, gain)


def attention_totals_kernel(info, *refs):
    pieces, (query, key, value, gain, before) = refs[:4], refs[4:9]
    gain_grad, squares, attention, semaphores = refs[9:]
    for copy in start_attention(info, pieces, attention, semaphores):
        copy.wait()
    result = before[...]
    for step in range(STEPS):
        rows = slice(step * 48, (step + 1) * 48)
        total = jnp.zeros((48, 128), F32)
        square = jnp.zeros((48, 128), F32)
        for master, number, count in ((query, 0, 3), (key, 6, 1), (value, 7, 1)):
            for j in range(count):
                block = attention_block(attention, step, number + j).astype(F32)
                square = square + lanes_sum(block * block)
                weight = master[rows, j * COLUMNS : (j + 1) * COLUMNS].astype(BF).astype(F32)
                total = total + lanes_sum(weight * block)
        for j in range(3):
            block = attention_block(attention, step, 3 + j).astype(F32)
            square = square + lanes_sum(block * block)
        grad = jnp.sum(total, axis=1, keepdims=True) / gain[rows, :]
        gain_grad[rows, :] = grad
        result = result + jnp.sum(square.reshape(6, 8, 128), axis=0)
        result = result + jnp.sum(jnp.square(grad)) * (1.0 / 1024)
    squares[...] = result


def attention_totals(info, pieces, query, key, value, gain, before):
    rows = query.shape[0]
    return pl.pallas_call(
        attention_totals_kernel,
        in_specs=[SCALARS]
        + [ANY] * 4
        + [whole(a.shape) for a in (query, key, value, gain, before)],
        out_specs=[whole((rows, 1)), whole((8, 128))],
        out_shape=[jax.ShapeDtypeStruct((rows, 1), F32), jax.ShapeDtypeStruct((8, 128), F32)],
        scratch_shapes=attention_scratch(pieces),
        compiler_params=params(60),
        cost_estimate=cost(10_000_000, 4_000_000),
        name="attention_totals",
    )(info, *pieces, query, key, value, gain, before)


def update_kernel(info, s0, s1, s2, s3, feed_sum, *refs):
    pieces, moments, masters = refs[:4], refs[4:11], refs[11:18]
    new_moments, updates, norm, attention, semaphores = (
        refs[18:25],
        refs[25:32],
        refs[32],
        refs[33],
        refs[34],
    )
    step = pl.program_id(0)

    @pl.when(step == 0)
    def _():
        for copy in start_attention(info, pieces, attention, semaphores):
            copy.wait()

    squares = (s0[...] + s1[...]) + (s2[...] + s3[...])
    length = jnp.sqrt(jnp.sum(squares, keepdims=True))
    norm[...] = length
    clip = jnp.minimum(1.0, jnp.sqrt(F32(PARAMS)) / (length + 1e-06))

    def renew(k, rows, columns, block):
        momentum = momentum_beta * moments[k][rows, columns] + clip * block.astype(F32)
        new_moments[k][rows, columns] = momentum
        updates[k][rows, columns] = (
            masters[k][rows, columns] * (1.0 - learning_rate * weight_decay)
            - learning_rate * momentum
        )

    for k, number, count in ((0, 0, 3), (1, 6, 1), (2, 7, 1), (3, 3, 3)):
        for j in range(count):
            block = attention_block(attention, step, number + j)
            renew(k, slice(0, 48), slice(j * COLUMNS, (j + 1) * COLUMNS), block)
    for k, number in ((4, 0), (5, 8)):
        for j in range(8):
            block = feed_block(info, feed_sum, step, number + j)
            renew(k, slice(0, 48), slice(j * COLUMNS, (j + 1) * COLUMNS), block)
    row = pl.multiple_of(step * 16, 16)
    for e in range(8):
        for cb in range(3):
            block = feed_sum[e, pl.ds(576 + cb * 96 + row, 16), :]
            renew(6, slice(e * 16, (e + 1) * 16), slice(cb * COLUMNS, (cb + 1) * COLUMNS), block)


def update(info, squares, pieces, feed_sum, moments, masters):
    blocks = [
        pl.BlockSpec((a.shape[0] // STEPS, a.shape[1]), lambda i: (i, 0)) for a in masters
    ]
    shapes = [jax.ShapeDtypeStruct(a.shape, F32) for a in masters]
    return pl.pallas_call(
        update_kernel,
        grid=(STEPS,),
        in_specs=[SCALARS]
        + [whole((8, 128))] * 4
        + [once(feed_sum.shape)]
        + [ANY] * 4
        + blocks * 2,
        out_specs=blocks * 2 + [whole((1, 1))],
        out_shape=shapes * 2 + [jax.ShapeDtypeStruct((1, 1), F32)],
        scratch_shapes=attention_scratch(pieces),
        compiler_params=params(60),
        cost_estimate=cost(20_000_000, 64_000_000),
        name="update",
    )(info, *squares, feed_sum, *pieces, *moments, *masters)


def fast_device(
    tokens,
    cotangent,
    picture_starts,
    query_weight,
    key_matrix,
    value_matrix,
    out_weight,
    gate_weight,
    up_weight,
    down_weight,
    attention_gain,
    feed_gain,
    query_moment,
    key_velocity,
    value_velocity,
    out_moment,
    gate_moment,
    up_moment,
    down_moment,
    attention_moment,
    feed_moment,
):
    masters = (
        query_weight,
        key_matrix,
        value_matrix,
        out_weight,
        gate_weight,
        up_weight,
        down_weight,
        attention_gain,
        feed_gain,
    )
    moments = (
        query_moment,
        key_velocity,
        value_velocity,
        out_moment,
        gate_moment,
        up_moment,
        down_moment,
        attention_moment,
        feed_moment,
    )
    me = lax.axis_index("seq")
    line = lax.axis_index("dp") // 2
    core = lax.axis_index("dp") % 2
    rows = tokens.shape[1]
    width = tokens.shape[2]
    shard = query_weight.shape[0]
    half = shard // 2
    hidden_own = down_weight.shape[0]
    places = [me, me ^ 1, me ^ 2, me ^ 3]

    gain_columns = [
        gain.astype(BF).astype(F32)[:, None] for gain in (attention_gain, feed_gain)
    ]
    info = index_array(me, line, core)

    def fetch_rows(own, mine):
        fetched = gather_plane(mine)
        return [own, *fetched, *[swap_core(block) for block in fetched]]

    def core_half(own):
        return lax.dynamic_slice_in_dim(own, core * half, half, 0)

    wide_gains = jnp.pad(jnp.concatenate(gain_columns, axis=1), ((0, 0), (0, 126)))
    projections = (query_weight, key_matrix, value_matrix, wide_gains)
    mine_qkv = jnp.concatenate([core_half(weight) for weight in projections], axis=1).astype(BF)
    own_qkv = jnp.concatenate(projections, axis=1).astype(BF)
    qkv = fetch_rows(own_qkv, mine_qkv)
    own_out = out_weight.astype(BF)
    mine_out = core_half(own_out)

    own_down = down_weight.astype(BF)

    token_positions = me * rows + jnp.arange(rows, dtype=jnp.int32)
    frequency = 10000.0 ** (-jnp.arange(HEAD_SIZE // 2, dtype=F32) / (HEAD_SIZE // 2))
    angles = token_positions.astype(F32)[:, None] * frequency[None, :]
    cosine, sine = jnp.cos(angles), jnp.sin(angles)
    trig = (
        jnp.concatenate([cosine] * 4, axis=1),
        jnp.concatenate([-sine, sine, -sine, sine], axis=1),
    )

    x = tokens[0]
    starts = picture_starts[0]
    bit = line % 2

    def columns_for(place):
        at = (core * half, place * hidden_own)
        size = (half, hidden_own)
        return jnp.where(
            bit == 0, lax.dynamic_slice(gate_weight, at, size), lax.dynamic_slice(up_weight, at, size)
        ).astype(BF)

    sent = [columns_for(place) for place in places[1:]]
    sent, _ = after(sent, qkv[1:3])
    fetched = [swap_x(sent[0]), swap_y(sent[1]), swap_diagonal(sent[2])]
    query, key_value, act_one, gains, full_qkv = project(info, x, *trig, qkv)
    key_sent, fetched = after(key_value, fetched)
    key_x, key_y = swap_x(key_sent), swap_y(key_sent)
    mine_out, _ = after(mine_out, (key_x, key_y))
    out_x, out_y = swap_x(mine_out), swap_y(mine_out)
    key_values = [key_value, key_x, key_y, relay(key_x, key_y)]
    attended = attend(info, starts, query, key_values)
    (out_x, out_y), attended = after((out_x, out_y), attended)
    fetched_out = [out_x, out_y, relay(out_x, out_y)]
    out_rows = [own_out, *fetched_out, *[swap_core(block) for block in fetched_out]]

    near_columns = swap_near(jnp.stack(fetched))
    other_columns = swap_core(jnp.concatenate([jnp.stack(fetched), near_columns]))
    own_columns = [
        lax.dynamic_slice_in_dim(weight, me * hidden_own, hidden_own, 1)
        for weight in (gate_weight, up_weight)
    ]
    gate_up = [
        jnp.concatenate(own_columns, axis=1).astype(BF),
        *fetched,
        near_columns,
        other_columns,
    ]

    upstream_low = cotangent[0]
    upstream_sent, _ = after(upstream_low, attended)
    upstreams = [upstream_low, *gather_plane(upstream_sent)]
    attention, residual, act_two, full_out = out_project(info, attended, x, gains, out_rows)
    act_x, act_y, act_d = gather_parts(act_two)
    acts = [act_two, act_x, act_y]
    hidden, both_back, *act_parts, full_gu = feed_first(
        info, acts, upstreams[:3], gate_up, own_down
    )
    act_d, hidden = after(act_d, hidden)
    acts.append(jnp.concatenate(act_d))
    last_hidden, last_back, act_part = feed_last(acts[3], upstreams[3], full_gu, own_down)
    act_grads = [
        act_parts[0],
        swap_x(act_parts[1]),
        swap_y(act_parts[2]),
        swap_diagonal(act_part),
    ]
    layer_blocks = layer_parts(hidden, last_hidden, own_down)
    parts = feed_gradients(
        info, acts, both_back, last_back, hidden, last_hidden, upstreams
    )
    act_grads, (parts, layer_blocks) = after(act_grads, (parts, layer_blocks))
    output = (residual + scatter_plane(*layer_blocks)).astype(BF)[None]

    grad_residual, grad_low, query_back, *kv_parts = attend_back(
        info,
        starts,
        act_grads,
        upstream_low,
        residual,
        gains,
        query,
        key_values,
        attended,
        trig,
        full_out,
    )
    kv_parts, output = after(kv_parts, output)
    kv_sums = [
        kv_parts[0],
        swap_x(kv_parts[1]),
        swap_y(kv_parts[2]),
        swap_diagonal(kv_parts[3]),
    ]

    def across(own, for_x, for_y, for_d):
        return [own, swap_x(for_x), swap_y(for_y), swap_diagonal(for_d)]

    keep, send = query_gradients(info, act_one, attention, query_back, grad_low)
    kv_sums[0], (keep, send) = after(kv_sums[0], (keep, send))
    received = swap_core(send)
    key_back, second_keep, second_send = key_gradients(info, act_one, kv_sums, trig)
    pair = pair_sum(keep, received, second_keep, swap_core(second_send))
    plane_parts = across(*pair)

    feed_own = lax.psum_scatter(parts, "dp", scatter_dimension=0, tiled=True)[0]
    feed_own, _ = after(feed_own, (second_keep, second_send))
    feed_own = jnp.concatenate(
        [
            feed_own[:half],
            swap_x(feed_own[half : 2 * half]),
            swap_y(feed_own[2 * half : 3 * half]),
            swap_diagonal(feed_own[3 * half : 4 * half]),
            feed_own[4 * half :],
        ]
    )
    feed_whole = lax.all_gather(feed_own, "dp", axis=0)

    input_grad = input_back(query_back, key_back, x, gains, grad_residual, full_qkv)[None]
    plane_parts, input_grad = after(plane_parts, input_grad)
    near_sent, keep = plane_sum(info, plane_parts)
    near = swap_near(near_sent)
    far = swap_far((keep[1] + near[1]).astype(BF))
    line_own = (keep[0] + near[0] + far).astype(BF)
    pair_own = jnp.stack([line_own, swap_far(line_own)])
    near_own = swap_near(pair_own)

    feed_gain_grad, feed_squares = feed_totals(
        info, feed_whole, gate_weight, up_weight, gain_columns[1]
    )
    near_own, feed_squares = after(near_own, feed_squares)
    pieces = [pair_own, near_own, swap_core(pair_own), swap_core(near_own)]
    attention_gain_grad, squares = attention_totals(
        info, pieces, query_weight, key_matrix, value_matrix, gain_columns[0], feed_squares
    )
    *renewed, norm = update(
        info,
        across(squares, squares, squares, squares),
        pieces,
        feed_whole,
        moments[:7],
        masters[:7],
    )
    gradient_norm = norm[0, 0]
    clip_factor = jnp.minimum(1.0, jnp.sqrt(F32(PARAMS)) / (gradient_norm + 1e-06))
    momenta, updated = list(renewed[:7]), list(renewed[7:])
    for k, gradient in ((7, attention_gain_grad[:, 0]), (8, feed_gain_grad[:, 0])):
        momenta.append(momentum_beta * moments[k] + clip_factor * gradient)
        updated.append(
            masters[k] * (1.0 - learning_rate * weight_decay) - learning_rate * momenta[k]
        )
    return (output, input_grad, *momenta, *updated, gradient_norm)


def solution(mesh):
    fits = mesh.shape["seq"] == 4 and mesh.shape["dp"] == 8
    body = fast_device if fits else per_device
    return jax.shard_map(
        body,
        mesh=mesh,
        in_specs=(
            P("dp", "seq", None),
            P("dp", "seq", None),
            P("dp", None),
            P("seq", None),
            P("seq", None),
            P("seq", None),
            P("seq", None),
            P("seq", None),
            P("seq", None),
            P("seq", None),
            P("seq"),
            P("seq"),
            P("seq", None),
            P("seq", None),
            P("seq", None),
            P("seq", None),
            P("seq", None),
            P("seq", None),
            P("seq", None),
            P("seq"),
            P("seq"),
        ),
        out_specs=(
            P("dp", "seq", None),
            P("dp", "seq", None),
            P("seq", None),
            P("seq", None),
            P("seq", None),
            P("seq", None),
            P("seq", None),
            P("seq", None),
            P("seq", None),
            P("seq"),
            P("seq"),
            P("seq", None),
            P("seq", None),
            P("seq", None),
            P("seq", None),
            P("seq", None),
            P("seq", None),
            P("seq", None),
            P("seq"),
            P("seq"),
            P(),
        ),
        check_vma=False,
    )
```

```python
from functools import partial
import math

import jax
import jax.numpy as jnp
from jax import lax
from jax.experimental import pallas as pl
from jax.experimental.pallas import tpu as pltpu
from jax.sharding import PartitionSpec as P

QUERY_HEAD_COUNT = 18
KEY_VALUE_HEADS = 6
HEAD_SIZE = 64
PIECE = 256
PARAMS = 14158080


learning_rate = 0.25
weight_decay = 0.1
momentum_beta = 0.5


def rms_scale(values, scaling):
    return values * lax.rsqrt(jnp.mean(values * values, axis=-1, keepdims=True) + 1e-05) * scaling


def apply_rotary(values, token_positions):
    half_width = values.shape[-1] // 2
    frequency = 10000.0 ** (-jnp.arange(half_width, dtype=jnp.float32) / half_width)
    angles = token_positions.astype(jnp.float32)[:, None] * frequency[None, :]
    cosine = jnp.cos(angles)[:, None, :]
    sine_part = jnp.sin(angles)[:, None, :]
    leading = values[..., :half_width]
    trailing = values[..., half_width:]
    return jnp.concatenate(
        [leading * cosine - trailing * sine_part, trailing * cosine + leading * sine_part], axis=-1
    )


def swiglu(gate_values, up_values):
    return jax.nn.silu(gate_values) * up_values


def piece_number(token_positions, starts):
    inside = (token_positions[:, None] >= starts[None, :]) & (
        token_positions[:, None] < starts[None, :] + PIECE
    )
    numbers = jnp.arange(starts.shape[0], dtype=jnp.int32) + 1
    return jnp.sum(jnp.where(inside, numbers[None, :], 0), axis=1) - 1


def visible(query_position, query_piece, key_position, key_piece):
    earlier = key_position[None, :] <= query_position[:, None]
    same_piece = (query_piece[:, None] == key_piece[None, :]) & (query_piece[:, None] >= 0)
    return earlier | same_piece


def per_device(
    tokens,
    cotangent,
    picture_starts,
    query_weight,
    key_matrix,
    value_matrix,
    out_weight,
    gate_weight,
    up_weight,
    down_weight,
    attention_gain,
    feed_gain,
    query_moment,
    key_velocity,
    value_velocity,
    out_moment,
    gate_moment,
    up_moment,
    down_moment,
    attention_moment,
    feed_moment,
):
    masters = (
        query_weight,
        key_matrix,
        value_matrix,
        out_weight,
        gate_weight,
        up_weight,
        down_weight,
        attention_gain,
        feed_gain,
    )
    moments = (
        query_moment,
        key_velocity,
        value_velocity,
        out_moment,
        gate_moment,
        up_moment,
        down_moment,
        attention_moment,
        feed_moment,
    )
    shard_query = query_weight.astype(jnp.bfloat16)
    shard_key = key_matrix.astype(jnp.bfloat16)
    shard_value = value_matrix.astype(jnp.bfloat16)
    shard_out = out_weight.astype(jnp.bfloat16)
    shard_gate = gate_weight.astype(jnp.bfloat16)
    shard_up = up_weight.astype(jnp.bfloat16)
    shard_down = down_weight.astype(jnp.bfloat16)
    shard_gain_one = attention_gain.astype(jnp.bfloat16)
    shard_gain_two = feed_gain.astype(jnp.bfloat16)
    gathered = (
        lax.all_gather(shard_query, "seq", axis=0, tiled=True),
        lax.all_gather(shard_key, "seq", axis=0, tiled=True),
        lax.all_gather(shard_value, "seq", axis=0, tiled=True),
        lax.all_gather(shard_out, "seq", axis=0, tiled=True),
        lax.all_gather(shard_gate, "seq", axis=0, tiled=True),
        lax.all_gather(shard_up, "seq", axis=0, tiled=True),
        lax.all_gather(shard_down, "seq", axis=0, tiled=True),
        lax.all_gather(shard_gain_one, "seq", axis=0, tiled=True),
        lax.all_gather(shard_gain_two, "seq", axis=0, tiled=True),
    )
    full_query, complete_key, complete_value, full_out, full_gate, full_up, full_down = gathered[:7]
    gain_one = gathered[7].astype(jnp.float32)
    gain_two = gathered[8].astype(jnp.float32)
    group_size = lax.axis_size("seq")
    local_rows = tokens.shape[1]
    sequence_length = local_rows * group_size
    heads_per_group = QUERY_HEAD_COUNT // KEY_VALUE_HEADS
    token_positions = lax.axis_index("seq") * local_rows + jnp.arange(local_rows, dtype=jnp.int32)
    starts = picture_starts[0]
    query_piece = piece_number(token_positions, starts)
    key_positions = jnp.arange(sequence_length, dtype=jnp.int32)
    key_pieces = piece_number(key_positions, starts)
    layer_input = tokens[0].astype(jnp.float32)
    normed_one, pull_norm_one = jax.vjp(rms_scale, layer_input, gain_one)
    first_activation = normed_one.astype(jnp.bfloat16)
    rotation = partial(apply_rotary, token_positions=token_positions)
    query_linear = jnp.dot(
        first_activation, full_query, preferred_element_type=jnp.float32
    ).reshape(local_rows, QUERY_HEAD_COUNT, HEAD_SIZE)
    rotated_query, pull_query = jax.vjp(rotation, query_linear)
    query_reduced = rotated_query.astype(jnp.bfloat16).reshape(
        local_rows, KEY_VALUE_HEADS, heads_per_group, HEAD_SIZE
    )
    key_linear = jnp.dot(
        first_activation, complete_key, preferred_element_type=jnp.float32
    ).reshape(local_rows, KEY_VALUE_HEADS, HEAD_SIZE)
    rotated_key, key_pullback = jax.vjp(rotation, key_linear)
    key_reduced = rotated_key.astype(jnp.bfloat16).reshape(local_rows, KEY_VALUE_HEADS * HEAD_SIZE)
    value_reduced = jnp.dot(
        first_activation, complete_value, preferred_element_type=jnp.float32
    ).astype(jnp.bfloat16)
    every_key_row, every_value_row = (
        lax.all_gather(key_reduced, "seq", axis=0, tiled=True),
        lax.all_gather(value_reduced, "seq", axis=0, tiled=True),
    )
    every_key_row = every_key_row.reshape(sequence_length, KEY_VALUE_HEADS, HEAD_SIZE)
    every_value_row = every_value_row.reshape(sequence_length, KEY_VALUE_HEADS, HEAD_SIZE)
    rows_per_block = math.gcd(512, sequence_length)
    count_of_blocks = sequence_length // rows_per_block
    last_position = token_positions[local_rows - 1]
    last_piece = query_piece[local_rows - 1]

    def needed(number):
        first_row = number * rows_per_block
        return (first_row <= last_position) | (last_piece >= 0) & (
            key_pieces[first_row] == last_piece
        )

    def block_scores(number):
        first_row = number * rows_per_block
        key_block = lax.dynamic_slice_in_dim(every_key_row, first_row, rows_per_block, 0)
        value_block = lax.dynamic_slice_in_dim(every_value_row, first_row, rows_per_block, 0)
        allowed = visible(
            token_positions,
            query_piece,
            lax.dynamic_slice_in_dim(key_positions, first_row, rows_per_block, 0),
            lax.dynamic_slice_in_dim(key_pieces, first_row, rows_per_block, 0),
        )
        raw_scores = jnp.einsum(
            "qhgd,khd->hgqk", query_reduced, key_block, preferred_element_type=jnp.float32
        )
        exponent = jnp.where(allowed[None, None], jnp.exp(raw_scores * 0.125), 0.0)
        return (key_block, value_block, exponent)

    def unchanged(current):
        return current

    def forward_step(number, running):

        def forward_compute(current):
            summed, totals = current
            key_block, value_block, exponent = block_scores(number)
            summed = summed + jnp.einsum(
                "hgqk,khd->hgqd",
                exponent.astype(jnp.bfloat16),
                value_block,
                preferred_element_type=jnp.float32,
            )
            return (summed, totals + jnp.sum(exponent, axis=-1))

        return lax.cond(needed(number), forward_compute, unchanged, running)

    initial_sum = jnp.zeros((KEY_VALUE_HEADS, heads_per_group, local_rows, HEAD_SIZE), jnp.float32)
    initial_total = jnp.zeros((KEY_VALUE_HEADS, heads_per_group, local_rows), jnp.float32)
    summed, totals = lax.fori_loop(0, count_of_blocks, forward_step, (initial_sum, initial_total))
    attended = summed / totals[..., None]
    attention = (
        jnp.transpose(attended, (2, 0, 1, 3))
        .reshape(local_rows, QUERY_HEAD_COUNT * HEAD_SIZE)
        .astype(jnp.bfloat16)
    )
    residual = layer_input + jnp.dot(attention, full_out, preferred_element_type=jnp.float32)
    normed_two, pull_norm_two = jax.vjp(rms_scale, residual, gain_two)
    act_two = normed_two.astype(jnp.bfloat16)
    gate_linear = jnp.dot(act_two, full_gate, preferred_element_type=jnp.float32)
    up_linear = jnp.dot(act_two, full_up, preferred_element_type=jnp.float32)
    hidden_full, pull_swiglu = jax.vjp(swiglu, gate_linear, up_linear)
    hidden = hidden_full.astype(jnp.bfloat16)
    layer_out = residual + jnp.dot(hidden, full_down, preferred_element_type=jnp.float32)
    output = layer_out.astype(jnp.bfloat16)[None]
    upstream = cotangent[0].astype(jnp.float32)
    upstream_low = upstream.astype(jnp.bfloat16)
    grad_down = jnp.einsum("nf,nd->fd", hidden, upstream_low, preferred_element_type=jnp.float32)
    grad_hidden = jnp.einsum(
        "nd,fd->nf", upstream_low, full_down, preferred_element_type=jnp.float32
    )
    grad_gate_full, grad_up_full = pull_swiglu(grad_hidden)
    gate_back = grad_gate_full.astype(jnp.bfloat16)
    up_back = grad_up_full.astype(jnp.bfloat16)
    grad_gate = jnp.einsum("nd,nf->df", act_two, gate_back, preferred_element_type=jnp.float32)
    grad_up = jnp.einsum("nd,nf->df", act_two, up_back, preferred_element_type=jnp.float32)
    grad_act_two = jnp.einsum(
        "nf,df->nd", gate_back, full_gate, preferred_element_type=jnp.float32
    ) + jnp.einsum("nf,df->nd", up_back, full_up, preferred_element_type=jnp.float32)
    residual_norm_grad, grad_gain_two = pull_norm_two(grad_act_two)
    grad_residual = upstream + residual_norm_grad
    residual_back = grad_residual.astype(jnp.bfloat16)
    grad_out = jnp.einsum("nk,nd->kd", attention, residual_back, preferred_element_type=jnp.float32)
    attention_pullback = jnp.einsum(
        "nd,kd->nk", residual_back, full_out, preferred_element_type=jnp.float32
    ).astype(jnp.bfloat16)
    attention_pullback = jnp.transpose(
        attention_pullback.reshape(local_rows, KEY_VALUE_HEADS, heads_per_group, HEAD_SIZE),
        (1, 2, 0, 3),
    )
    back_full = attention_pullback.astype(jnp.float32)
    scaled_back = (back_full / totals[..., None]).astype(jnp.bfloat16)
    total_back = -jnp.sum(back_full * attended, axis=-1) / totals
    query_heads = jnp.transpose(query_reduced, (1, 2, 0, 3))

    def backward_step(number, running):

        def backward_compute(current):
            grad_query_sum, key_gradient_rows, value_gradient_rows = current
            first_row = number * rows_per_block
            key_block, value_block, exponent = block_scores(number)
            through = jnp.einsum(
                "hgqd,khd->hgqk", scaled_back, value_block, preferred_element_type=jnp.float32
            )
            score_back = (exponent * (through + total_back[..., None])).astype(jnp.bfloat16)
            grad_query_sum = (
                grad_query_sum
                + jnp.einsum(
                    "hgqk,khd->hgqd", score_back, key_block, preferred_element_type=jnp.float32
                )
                * 0.125
            )
            key_part = (
                jnp.einsum(
                    "hgqk,hgqd->khd", score_back, query_heads, preferred_element_type=jnp.float32
                )
                * 0.125
            )
            value_part = jnp.einsum(
                "hgqk,hgqd->khd",
                exponent.astype(jnp.bfloat16),
                scaled_back,
                preferred_element_type=jnp.float32,
            )
            key_gradient_rows = lax.dynamic_update_slice_in_dim(
                key_gradient_rows, key_part, first_row, 0
            )
            value_gradient_rows = lax.dynamic_update_slice_in_dim(
                value_gradient_rows, value_part, first_row, 0
            )
            return (grad_query_sum, key_gradient_rows, value_gradient_rows)

        return lax.cond(needed(number), backward_compute, unchanged, running)

    initial_query = jnp.zeros(
        (KEY_VALUE_HEADS, heads_per_group, local_rows, HEAD_SIZE), jnp.float32
    )
    initial_keys = jnp.zeros((sequence_length, KEY_VALUE_HEADS, HEAD_SIZE), jnp.float32)
    grad_query_sum, key_gradient_rows, value_gradient_rows = lax.fori_loop(
        0, count_of_blocks, backward_step, (initial_query, initial_keys, initial_keys)
    )
    local_key_rows, value_own = (
        lax.psum_scatter(
            key_gradient_rows.reshape(sequence_length, KEY_VALUE_HEADS * HEAD_SIZE),
            "seq",
            scatter_dimension=0,
            tiled=True,
        ),
        lax.psum_scatter(
            value_gradient_rows.reshape(sequence_length, KEY_VALUE_HEADS * HEAD_SIZE),
            "seq",
            scatter_dimension=0,
            tiled=True,
        ),
    )
    key_back = (
        key_pullback(local_key_rows.reshape(local_rows, KEY_VALUE_HEADS, HEAD_SIZE))[0]
        .reshape(local_rows, KEY_VALUE_HEADS * HEAD_SIZE)
        .astype(jnp.bfloat16)
    )
    query_rot_grad = jnp.transpose(grad_query_sum, (2, 0, 1, 3)).reshape(
        local_rows, QUERY_HEAD_COUNT, HEAD_SIZE
    )
    query_back = (
        pull_query(query_rot_grad)[0]
        .reshape(local_rows, QUERY_HEAD_COUNT * HEAD_SIZE)
        .astype(jnp.bfloat16)
    )
    value_back = value_own.astype(jnp.bfloat16)
    grad_query = jnp.einsum(
        "nd,nk->dk", first_activation, query_back, preferred_element_type=jnp.float32
    )
    grad_key = jnp.einsum(
        "nd,nk->dk", first_activation, key_back, preferred_element_type=jnp.float32
    )
    grad_value = jnp.einsum(
        "nd,nk->dk", first_activation, value_back, preferred_element_type=jnp.float32
    )
    grad_act_one = jnp.einsum(
        "nk,dk->nd", query_back, full_query, preferred_element_type=jnp.float32
    )
    grad_act_one = grad_act_one + jnp.einsum(
        "nk,dk->nd", key_back, complete_key, preferred_element_type=jnp.float32
    )
    grad_act_one = grad_act_one + jnp.einsum(
        "nk,dk->nd", value_back, complete_value, preferred_element_type=jnp.float32
    )
    input_norm_grad, grad_gain_one = pull_norm_one(grad_act_one)
    input_grad = (grad_residual + input_norm_grad)[None]
    shard_grads = (
        lax.psum_scatter(grad_query, "seq", scatter_dimension=0, tiled=True),
        lax.psum_scatter(grad_key, "seq", scatter_dimension=0, tiled=True),
        lax.psum_scatter(grad_value, "seq", scatter_dimension=0, tiled=True),
        lax.psum_scatter(grad_out, "seq", scatter_dimension=0, tiled=True),
        lax.psum_scatter(grad_gate, "seq", scatter_dimension=0, tiled=True),
        lax.psum_scatter(grad_up, "seq", scatter_dimension=0, tiled=True),
        lax.psum_scatter(grad_down, "seq", scatter_dimension=0, tiled=True),
        lax.psum_scatter(grad_gain_one, "seq", scatter_dimension=0, tiled=True),
        lax.psum_scatter(grad_gain_two, "seq", scatter_dimension=0, tiled=True),
    )
    gradients = lax.psum(
        (
            shard_grads[0],
            shard_grads[1],
            shard_grads[2],
            shard_grads[3],
            shard_grads[4],
            shard_grads[5],
            shard_grads[6],
            shard_grads[7],
            shard_grads[8],
        ),
        "dp",
    )
    squares = jnp.float32(0.0)
    for gradient in gradients:
        squares = squares + jnp.sum(gradient * gradient)
    gradient_norm = jnp.sqrt(lax.psum(squares, "seq"))
    clip_factor = jnp.minimum(1.0, jnp.sqrt(jnp.float32(PARAMS)) / (gradient_norm + 1e-06))
    momenta = [
        momentum_beta * moment + clip_factor * gradient
        for moment, gradient in zip(moments, gradients)
    ]
    updated = [
        master * (1.0 - learning_rate * weight_decay) - learning_rate * momentum
        for master, momentum in zip(masters, momenta)
    ]
    return (
        output,
        input_grad,
        momenta[0],
        momenta[1],
        momenta[2],
        momenta[3],
        momenta[4],
        momenta[5],
        momenta[6],
        momenta[7],
        momenta[8],
        updated[0],
        updated[1],
        updated[2],
        updated[3],
        updated[4],
        updated[5],
        updated[6],
        updated[7],
        updated[8],
        gradient_norm,
    )


BF = jnp.bfloat16
F32 = jnp.float32


def swap_x(value):
    return lax.ppermute(value, "seq", [(i, i ^ 1) for i in range(4)])


def swap_y(value):
    return lax.ppermute(value, "seq", [(i, i ^ 2) for i in range(4)])


def swap_diagonal(value):
    return lax.ppermute(value, "seq", [(i, i ^ 3) for i in range(4)])


def swap_core(value):
    return lax.ppermute(value, "dp", [(i, i ^ 1) for i in range(8)])


def move_up(value):
    return lax.ppermute(value, "dp", [(i, i + 2) for i in range(6)])


def move_down(value):
    return lax.ppermute(value, "dp", [(i + 2, i) for i in range(6)])


def gather_parts(value):
    middle = value.shape[0] // 2
    from_x = swap_x(value)
    from_y = swap_y(value)
    return from_x, from_y, (swap_x(from_y[:middle]), swap_y(from_x[middle:]))


def relay(from_x, from_y):
    middle = from_x.shape[0] // 2
    return jnp.concatenate([swap_x(from_y[:middle]), swap_y(from_x[middle:])])


def gather_plane(value):
    from_x, from_y, from_d = gather_parts(value)
    return from_x, from_y, jnp.concatenate(from_d)


def scatter_plane(own, for_x, for_y, for_d):
    from_x = swap_x(for_x.astype(BF))
    from_y = swap_y(for_y.astype(BF))
    from_d = swap_diagonal(for_d.astype(BF))
    return own.astype(F32) + from_x + from_y + from_d


def swap_near(value):
    return lax.ppermute(value, "dp", [(i, i ^ 2) for i in range(8)])


def swap_far(value):
    return lax.ppermute(value, "dp", [(i, i ^ 4) for i in range(8)])


def after(value, other):
    return lax.optimization_barrier((value, other))


def index_array(*numbers):
    return jnp.stack([jnp.asarray(number, jnp.int32) for number in numbers])


COLUMNS = 384


def whole(shape):
    return pl.BlockSpec(shape, lambda *_: (0,) * len(shape))


def once(shape):
    return pl.BlockSpec(shape, lambda *_: (0,) * len(shape), pipeline_mode=pl.Buffered(1))


ANY = pl.BlockSpec(memory_space=pl.ANY)
SCALARS = pl.BlockSpec(memory_space=pltpu.SMEM)


def params(mebibytes):
    return pltpu.CompilerParams(vmem_limit_bytes=mebibytes * 1024 * 1024)


def cost(flops, transferred):
    return pl.CostEstimate(flops=flops // 1000, bytes_accessed=transferred // 1000, transcendentals=0)


def start_rows(target, blocks, info, semaphores):
    own, fetched, other = blocks[0], blocks[1:4], blocks[4:7]
    shard, half = own.shape[0], own.shape[0] // 2
    copies = [(own, info[0] * shard, shard)]
    for j in range(3):
        first = (info[0] ^ (j + 1)) * shard
        copies.append((fetched[j], first + info[2] * half, half))
        copies.append((other[j], first + (1 - info[2]) * half, half))
    started = []
    for j, (source, row, count) in enumerate(copies):
        row = pl.multiple_of(row, 16)
        copy = pltpu.make_async_copy(source, target.at[pl.ds(row, count)], semaphores.at[j])
        copy.start()
        started.append(copy)
    return started


def partners(value):
    lanes = value.shape[1]
    low = lax.broadcasted_iota(jnp.int32, value.shape, 1) % HEAD_SIZE < HEAD_SIZE // 2
    return jnp.where(low, pltpu.roll(value, lanes - 32, 1), pltpu.roll(value, 32, 1))


def rotate(value, cosine, sine):
    return value * cosine + partners(value) * sine


def transposed(left, right):
    return lax.dot_general(left, right, (((1,), (1,)), ((), ())), preferred_element_type=F32)


def row_mean(value):
    return jnp.mean(value, axis=-1, keepdims=True)


def project_kernel(info, x, cosine, sine, *refs):
    blocks, outs, semaphores = refs[:7], refs[7:12], refs[12]
    query, key_value, act, gains, weight = outs
    copies = start_rows(weight, blocks, info, semaphores)
    values = x[...].astype(F32)
    normed = values * lax.rsqrt(row_mean(values * values) + 1e-05)
    cos = jnp.concatenate([cosine[...]] * 3, axis=1)
    sin = jnp.concatenate([sine[...]] * 3, axis=1)
    for copy in copies:
        copy.wait()
    gains[...] = weight[:, 5 * COLUMNS :].astype(F32).T[:8]
    low = (normed * gains[0:1, :]).astype(BF)
    act[...] = low
    for j in range(5):
        part = jnp.dot(
            low, weight[:, j * COLUMNS : (j + 1) * COLUMNS], preferred_element_type=F32
        )
        if j < 4:
            part = rotate(part, cos, sin)
        part = part.astype(BF)
        if j < 3:
            query[:, j * COLUMNS : (j + 1) * COLUMNS] = part * 0.125
        else:
            key_value[:, (j - 3) * COLUMNS : (j - 2) * COLUMNS] = part


def project(info, x, cosine, sine, blocks):
    rows, width = x.shape
    columns = blocks[0].shape[1]
    shapes = [
        ((rows, width), BF),
        ((rows, 2 * COLUMNS), BF),
        ((rows, width), BF),
        ((8, width), F32),
        ((width, columns), BF),
    ]
    return pl.pallas_call(
        project_kernel,
        in_specs=[SCALARS, *[whole(a.shape) for a in (x, cosine, sine)]] + [ANY] * 7,
        out_specs=[whole(shape) for shape, _ in shapes],
        out_shape=[jax.ShapeDtypeStruct(shape, kind) for shape, kind in shapes],
        scratch_shapes=[pltpu.SemaphoreType.DMA((7,))],
        compiler_params=params(24),
        cost_estimate=cost(2 * rows * width * columns, 8_000_000),
        name="project",
    )(info, x, cosine, sine, *blocks)


def piece_of(positions, starts, count):
    piece = jnp.full(positions.shape, -1, jnp.int32)
    for j in range(count):
        first = starts[j]
        piece = jnp.where((positions >= first) & (positions < first + PIECE), j, piece)
    return piece


def visibility(info, starts, count, rows, keys_first):
    axis = 1 if keys_first else 0
    query_shape = (1, rows) if keys_first else (rows, 1)
    query_at = info[0] * rows + lax.broadcasted_iota(jnp.int32, query_shape, axis)
    query_piece = piece_of(query_at, starts, count)
    biases = []
    for j in range(4):
        key_shape = query_shape[::-1]
        key_at = (info[0] ^ j) * rows + lax.broadcasted_iota(jnp.int32, key_shape, 1 - axis)
        key_piece = piece_of(key_at, starts, count)
        seen = (key_at <= query_at) | ((key_piece == query_piece) & (query_piece >= 0))
        biases.append(jnp.where(seen, 0.0, -1e30).astype(F32))
    return jnp.concatenate(biases, axis=1 - axis)


def attend_kernel(info, starts, query, kv0, kv1, kv2, kv3, attended, every):
    rows = query.shape[0]
    for j, block in enumerate((kv0, kv1, kv2, kv3)):
        every[j * rows : (j + 1) * rows, :] = block[...]
    bias = visibility(info, starts, starts.shape[0], rows, False)

    def pair(p, carry):
        at = pl.multiple_of(p * 128, 128)
        keys = every[:, pl.ds(at, 128)]
        values = every[:, pl.ds(COLUMNS + at, 128)]
        queries = query[:, pl.ds(pl.multiple_of(p * COLUMNS, 128), COLUMNS)]
        results = []
        for k in range(2):
            key = keys[:, k * 64 : (k + 1) * 64]
            value = values[:, k * 64 : (k + 1) * 64]
            for h in range(3):
                at = (k * 3 + h) * 64
                scores = transposed(queries[:, at : at + 64], key)
                exponent = jnp.exp(scores + bias)
                total = jnp.sum(exponent, axis=-1, keepdims=True)
                summed = jnp.dot(exponent.astype(BF), value, preferred_element_type=F32)
                results.append(summed / total)
        attended[:, pl.ds(pl.multiple_of(p * COLUMNS, 128), COLUMNS)] = jnp.concatenate(
            results, axis=1
        )
        return carry

    lax.fori_loop(0, 3, pair, 0)


def attend(info, starts, query, key_values):
    rows, width = query.shape
    square = whole((rows, width))
    return pl.pallas_call(
        attend_kernel,
        in_specs=[SCALARS, SCALARS, square] + [whole(a.shape) for a in key_values],
        out_specs=square,
        out_shape=jax.ShapeDtypeStruct((rows, width), F32),
        scratch_shapes=[pltpu.VMEM((4 * rows, 2 * COLUMNS), BF)],
        compiler_params=params(20),
        cost_estimate=cost(4 * rows * 4 * rows * width * 4, 10_000_000),
        name="attend",
    )(info, starts, query, *key_values)


def out_project_kernel(info, attended, x, gains, *refs):
    blocks, (attention, residual, act, weight), semaphores = refs[:7], refs[7:11], refs[11]
    copies = start_rows(weight, blocks, info, semaphores)
    low = attended[...].astype(BF)
    attention[...] = low
    for copy in copies:
        copy.wait()
    summed = x[...].astype(F32) + jnp.dot(low, weight[...], preferred_element_type=F32)
    residual[...] = summed
    scale = lax.rsqrt(row_mean(summed * summed) + 1e-05)
    act[...] = (summed * scale * gains[1:2, :]).astype(BF)


def out_project(info, attended, x, gains, blocks):
    rows, width = x.shape
    square = whole((rows, width))
    return pl.pallas_call(
        out_project_kernel,
        in_specs=[SCALARS, square, square, whole(gains.shape)] + [ANY] * 7,
        out_specs=[square] * 3 + [whole((width, width))],
        out_shape=[jax.ShapeDtypeStruct((rows, width), t) for t in (BF, F32, BF)]
        + [jax.ShapeDtypeStruct((width, width), BF)],
        scratch_shapes=[pltpu.SemaphoreType.DMA((7,))],
        compiler_params=params(18),
        cost_estimate=cost(2 * rows * width * width, 6_000_000),
        name="out_project",
    )(info, attended, x, gains, *blocks)


def feed_blocks(acts, ups, weight, down, hidden, back, outs):
    rows = acts[0].shape[0]
    units = down.shape[0]
    for j in range(len(acts)):
        span = slice(j * rows, (j + 1) * rows)
        both = jnp.dot(acts[j][...], weight[...], preferred_element_type=F32)
        gate, up = both[:, :units], both[:, units:]
        grad = transposed(ups[j][...], down[...])
        logistic = 1.0 / (1.0 + jnp.exp(-gate))
        smooth = gate * logistic
        hidden[span, :] = (smooth * up).astype(BF)
        slope = logistic * (1.0 + gate * (1.0 - logistic))
        back[span, :units] = (grad * up * slope).astype(BF)
        back[span, units:] = (grad * smooth).astype(BF)
        outs[j][...] = transposed(back[span, :], weight[...]).astype(outs[j].dtype)


def feed_first_kernel(info, *refs):
    acts, ups, refs = refs[:3], refs[3:6], refs[6:]
    own, fetched, near, other, down = refs[0], refs[1:4], refs[4], refs[5], refs[6]
    hidden, back, outs, weight, semaphores = refs[7], refs[8], refs[9:12], refs[12], refs[13]
    units = down.shape[0]
    shard, half = own.shape[0], own.shape[0] // 2
    bit = info[1] % 2
    copies = [(own, weight.at[pl.ds(pl.multiple_of(info[0] * shard, 16), shard)])]
    for j in range(3):
        first = (info[0] ^ (j + 1)) * shard
        mine = pl.ds(pl.multiple_of(first + info[2] * half, 16), half)
        theirs = pl.ds(pl.multiple_of(first + (1 - info[2]) * half, 16), half)
        same = pl.ds(pl.multiple_of(bit * units, 128), units)
        opposite = pl.ds(pl.multiple_of((1 - bit) * units, 128), units)
        copies.append((fetched[j], weight.at[mine, same]))
        copies.append((near.at[j], weight.at[mine, opposite]))
        copies.append((other.at[j], weight.at[theirs, same]))
        copies.append((other.at[3 + j], weight.at[theirs, opposite]))
    started = []
    for j, (source, target) in enumerate(copies):
        copy = pltpu.make_async_copy(source, target, semaphores.at[j])
        copy.start()
        started.append(copy)
    for copy in started:
        copy.wait()
    feed_blocks(acts, ups, weight, down, hidden, back, outs)


def feed_last_kernel(act, up, weight, down, hidden, back, out):
    feed_blocks([act], [up], weight, down, hidden, back, [out])


def feed(kernel, info, acts, ups, weights, specs, down, kinds, extra, scratch):
    count = len(acts)
    rows, width = acts[0].shape
    units = down.shape[0]
    square = whole((rows, width))
    shapes = [((count * rows, units), BF), ((count * rows, 2 * units), BF)]
    shapes += [((rows, width), kind) for kind in kinds] + extra
    return pl.pallas_call(
        kernel,
        in_specs=[SCALARS] * len(info) + [square] * (2 * count) + specs + [whole(down.shape)],
        out_specs=[whole(shape) for shape, _ in shapes],
        out_shape=[jax.ShapeDtypeStruct(shape, kind) for shape, kind in shapes],
        scratch_shapes=scratch,
        compiler_params=params(28 if count == 3 else 20),
        cost_estimate=cost(10 * count * rows * width * units, 20_000_000),
        name="feed",
    )(*info, *acts, *ups, *weights, down)


def feed_first(info, acts, ups, blocks, down):
    full = (acts[0].shape[1], 2 * down.shape[0])
    return feed(
        feed_first_kernel,
        [info],
        acts,
        ups,
        blocks,
        [ANY] * 6,
        down,
        (F32, BF, BF),
        [(full, BF)],
        [pltpu.SemaphoreType.DMA((13,))],
    )


def feed_last(act, up, weight, down):
    return feed(
        feed_last_kernel, [], [act], [up], [weight], [whole(weight.shape)], down, (BF,), [], []
    )


def layer_parts_kernel(hidden, last, down, *outs):
    rows = last.shape[0]
    for j in range(4):
        left = last[...] if j == 3 else hidden[j * rows : (j + 1) * rows, :]
        outs[j][...] = jnp.dot(left, down[...], preferred_element_type=F32).astype(outs[j].dtype)


def layer_parts(hidden, last, down):
    rows, units = last.shape
    width = down.shape[1]
    return pl.pallas_call(
        layer_parts_kernel,
        in_specs=[whole(hidden.shape), whole(last.shape), whole(down.shape)],
        out_specs=[whole((rows, width))] * 4,
        out_shape=[jax.ShapeDtypeStruct((rows, width), t) for t in (F32, BF, BF, BF)],
        compiler_params=params(14),
        cost_estimate=cost(8 * rows * units * width, 8_000_000),
        name="layer_parts",
    )(hidden, last, down)


def attend_back_kernel(info, starts, g0, g1, g2, g3, upstream, residual, gains, query, *refs):
    kvs, attended, cosine, sine, weight = refs[:4], refs[4], refs[5], refs[6], refs[7]
    grad_residual, grad_low, query_back, outs = refs[8], refs[9], refs[10], refs[11:15]
    every, back = refs[15:]
    rows = query.shape[0]
    for j, block in enumerate(kvs):
        every[j * rows : (j + 1) * rows, :] = block[...]
    act_back = g0[...] + g1[...].astype(F32) + g2[...].astype(F32) + g3[...].astype(F32)
    weighted = act_back * gains[1:2, :]
    values = residual[...]
    scale = lax.rsqrt(row_mean(values * values) + 1e-05)
    grad = upstream[...].astype(F32) + scale * (
        weighted - values * (scale * scale * row_mean(weighted * values))
    )
    grad_residual[...] = grad
    low = grad.astype(BF)
    grad_low[...] = low
    back[...] = transposed(low, weight[...]).astype(BF)
    bias = visibility(info, starts, starts.shape[0], rows, True)
    cos = jnp.concatenate([cosine[...]] * 3, axis=1)
    sin = jnp.concatenate([sine[...]] * 3, axis=1)

    def pair(p, carry):
        at = pl.multiple_of(p * 128, 128)
        wide = pl.ds(pl.multiple_of(p * COLUMNS, 128), COLUMNS)
        keys = every[:, pl.ds(at, 128)]
        values = every[:, pl.ds(COLUMNS + at, 128)]
        queries = query[:, wide]
        backs = back[:, wide].astype(F32).T
        products = backs * attended[:, wide].T
        query_parts, key_parts, value_parts = [], [], []
        for k in range(2):
            key = keys[:, k * 64 : (k + 1) * 64]
            value = values[:, k * 64 : (k + 1) * 64]
            key_t = key.T
            key_sum = value_sum = None
            for h in range(3):
                at = (k * 3 + h) * 64
                one = queries[:, at : at + 64]
                exponent = jnp.exp(transposed(key, one) + bias)
                total = jnp.sum(exponent, axis=0, keepdims=True)
                scaled = (backs[at : at + 64] / total).astype(BF)
                shift = -jnp.sum(products[at : at + 64], axis=0, keepdims=True) / total
                through = jnp.dot(value, scaled, preferred_element_type=F32)
                score = (exponent * (through + shift)).astype(BF)
                query_parts.append(jnp.dot(key_t, score, preferred_element_type=F32))
                key_part = jnp.dot(score, one, preferred_element_type=F32)
                value_part = transposed(exponent.astype(BF), scaled)
                key_sum = key_part if key_sum is None else key_sum + key_part
                value_sum = value_part if value_sum is None else value_sum + value_part
            key_parts.append(key_sum)
            value_parts.append(value_sum)
        turned = jnp.concatenate(query_parts, axis=0).T * 0.125
        query_back[:, wide] = rotate(turned, cos, -sin).astype(BF)
        key_pair = jnp.concatenate(key_parts, axis=1)
        value_pair = jnp.concatenate(value_parts, axis=1)
        for j in range(4):
            span = slice(j * rows, (j + 1) * rows)
            kind = outs[j].dtype
            at = pl.multiple_of(p * 128, 128)
            outs[j][:, pl.ds(at, 128)] = key_pair[span].astype(kind)
            outs[j][:, pl.ds(COLUMNS + at, 128)] = value_pair[span].astype(kind)
        return carry

    lax.fori_loop(0, 3, pair, 0)


def attend_back(info, starts, grads, upstream, residual, gains, query, kvs, attended, trig, weight):
    rows, width = query.shape
    square = whole((rows, width))
    table = whole(trig[0].shape)
    pair = whole((rows, 2 * COLUMNS))
    return pl.pallas_call(
        attend_back_kernel,
        in_specs=[SCALARS, SCALARS]
        + [square] * 6
        + [whole(gains.shape), square]
        + [pair] * 4
        + [square, table, table, whole(weight.shape)],
        out_specs=[square] * 3 + [pair] * 4,
        out_shape=[jax.ShapeDtypeStruct((rows, width), t) for t in (F32, BF, BF)]
        + [jax.ShapeDtypeStruct((rows, 2 * COLUMNS), t) for t in (F32, BF, BF, BF)],
        scratch_shapes=[
            pltpu.VMEM((4 * rows, 2 * COLUMNS), BF),
            pltpu.VMEM((rows, width), BF),
        ],
        compiler_params=params(60),
        cost_estimate=cost(10 * rows * 4 * rows * width * 4, 15_000_000),
        name="attend_back",
    )(info, starts, *grads, upstream, residual, gains, query, *kvs, attended, *trig, weight)


def split_rows(info, product, keep, send, columns):
    half = keep.shape[1]
    for sr in range(4):
        row = (info[0] ^ sr) * (2 * half)
        kept = pl.multiple_of(row + info[2] * half, 16)
        sent = pl.multiple_of(row + (1 - info[2]) * half, 16)
        keep[sr, :, columns] = product[pl.ds(kept, half), :].astype(BF)
        send[sr, :, columns] = product[pl.ds(sent, half), :].astype(BF)


def query_gradients_kernel(info, act, att, query_back, grad_low, keep, send, product):
    for first, (left, right) in enumerate(((act, query_back), (att, grad_low))):
        left_t = left[...].T
        for j in range(3):
            columns = slice(j * COLUMNS, (j + 1) * COLUMNS)
            product[...] = jnp.dot(left_t, right[:, columns], preferred_element_type=F32)
            at = (first * 3 + j) * COLUMNS
            split_rows(info, product, keep, send, slice(at, at + COLUMNS))


def query_gradients(info, act, att, query_back, grad_low):
    rows, width = act.shape
    half = width // 8
    square = whole((rows, width))
    out = (4, half, 2 * width)
    return pl.pallas_call(
        query_gradients_kernel,
        in_specs=[SCALARS] + [square] * 4,
        out_specs=[whole(out)] * 2,
        out_shape=[jax.ShapeDtypeStruct(out, BF)] * 2,
        scratch_shapes=[pltpu.VMEM((width, COLUMNS), F32)],
        compiler_params=params(20),
        cost_estimate=cost(4 * rows * width * width, 9_000_000),
        name="query_gradients",
    )(info, act, att, query_back, grad_low)


def key_gradients_kernel(info, act, p0, p1, p2, p3, cosine, sine, back, keep, send, product):
    summed = p0[...] + p1[...].astype(F32) + p2[...].astype(F32) + p3[...].astype(F32)
    cos = jnp.concatenate([cosine[...]] * 3, axis=1)
    sin = jnp.concatenate([sine[...]] * 3, axis=1)
    back[:, :COLUMNS] = rotate(summed[:, :COLUMNS], cos, -sin).astype(BF)
    back[:, COLUMNS:] = summed[:, COLUMNS:].astype(BF)
    left_t = act[...].T
    for j in range(2):
        columns = slice(j * COLUMNS, (j + 1) * COLUMNS)
        product[...] = jnp.dot(left_t, back[:, columns], preferred_element_type=F32)
        split_rows(info, product, keep, send, columns)


def key_gradients(info, act, parts, trig):
    rows, width = act.shape
    half = width // 8
    out = (4, half, 2 * COLUMNS)
    pair = whole((rows, 2 * COLUMNS))
    table = whole(trig[0].shape)
    return pl.pallas_call(
        key_gradients_kernel,
        in_specs=[SCALARS, whole((rows, width))] + [pair] * 4 + [table, table],
        out_specs=[pair, whole(out), whole(out)],
        out_shape=[jax.ShapeDtypeStruct((rows, 2 * COLUMNS), BF)]
        + [jax.ShapeDtypeStruct(out, BF)] * 2,
        scratch_shapes=[pltpu.VMEM((width, COLUMNS), F32)],
        compiler_params=params(14),
        cost_estimate=cost(4 * rows * width * COLUMNS, 5_000_000),
        name="key_gradients",
    )(info, act, *parts, *trig)


def input_back_kernel(query_back, key_back, x, gains, grad_residual, weight, out):
    width = x.shape[1]
    act_back = transposed(query_back[...], weight[:, :width])
    act_back = act_back + transposed(key_back[...], weight[:, width : width + 2 * COLUMNS])
    values = x[...].astype(F32)
    scale = lax.rsqrt(row_mean(values * values) + 1e-05)
    weighted = act_back * gains[0:1, :]
    out[...] = grad_residual[...] + scale * (
        weighted - values * (scale * scale * row_mean(weighted * values))
    )


def input_back(*operands):
    rows, width = operands[0].shape
    return pl.pallas_call(
        input_back_kernel,
        in_specs=[whole(a.shape) for a in operands],
        out_specs=whole((rows, width)),
        out_shape=jax.ShapeDtypeStruct((rows, width), F32),
        compiler_params=params(20),
        cost_estimate=cost(10 * rows * width * COLUMNS, 9_000_000),
        name="input_back",
    )(*operands)


def feed_gradients_kernel(
    info, a0, a1, a2, a3, back, back_last, hidden, last, u0, u1, u2, u3, out, act_t, hid_t, acc
):
    rows = a0.shape[0]
    half = a0.shape[1] // 8
    z = pl.program_id(0)

    @pl.when(z == 0)
    def _():
        for j, block in enumerate((a0, a1, a2, a3)):
            act_t[:, j * rows : (j + 1) * rows] = block[...].T
            block = last[...] if j == 3 else hidden[j * rows : (j + 1) * rows, :]
            hid_t[:, j * rows : (j + 1) * rows] = block.T

    acc[...] = jnp.dot(
        act_t[:, : 3 * rows], back[...], preferred_element_type=F32
    ) + jnp.dot(act_t[:, 3 * rows :], back_last[...], preferred_element_type=F32)
    for c in range(2):
        for sr in range(4):
            row = pl.multiple_of((info[0] ^ sr) * (2 * half) + c * half, 16)
            out[c, sr * half : (sr + 1) * half, :] = acc[pl.ds(row, half), :].astype(BF)
    left = jnp.concatenate(
        [hid_t[pl.ds(pl.multiple_of(i * 128 + z * 32, 32), 32), :] for i in range(6)]
    )
    down = jnp.zeros((192, u0.shape[1]), F32)
    for j, block in enumerate((u0, u1, u2, u3)):
        down = down + jnp.dot(
            left[:, j * rows : (j + 1) * rows], block[...], preferred_element_type=F32
        )
    for c in range(2):
        rows_of_c = jnp.concatenate(
            [down[i * 32 + c * 16 : i * 32 + (c + 1) * 16] for i in range(6)]
        ).astype(BF)
        for cb in range(3):
            first = 4 * half + cb * 96
            out[c, first : first + 96, :] = rows_of_c[:, cb * COLUMNS : (cb + 1) * COLUMNS]


def feed_gradients(info, acts, back, back_last, hidden, last, ups):
    rows, width = acts[0].shape
    units = hidden.shape[1]
    return pl.pallas_call(
        feed_gradients_kernel,
        grid=(4,),
        in_specs=[SCALARS]
        + [once((rows, width))] * 4
        + [
            pl.BlockSpec((3 * rows, COLUMNS), lambda z: (0, z)),
            pl.BlockSpec((rows, COLUMNS), lambda z: (0, z)),
            once(hidden.shape),
            once(last.shape),
        ]
        + [once((rows, width))] * 4,
        out_specs=pl.BlockSpec((2, 864, COLUMNS), lambda z: (z, 0, 0)),
        scratch_shapes=[
            pltpu.VMEM((width, 4 * rows), BF),
            pltpu.VMEM((units, 4 * rows), BF),
            pltpu.VMEM((width, COLUMNS), F32),
        ],
        out_shape=jax.ShapeDtypeStruct((8, 864, COLUMNS), BF),
        compiler_params=params(26),
        cost_estimate=cost(2 * 4 * rows * width * 3 * units, 20_000_000),
        name="feed_gradients",
    )(info, *acts, back, back_last, hidden, last, *ups)


def pair_sum_kernel(keep, received, second_keep, second_received, *outs):
    columns = keep.shape[2]
    for j in range(4):
        for span, one, other in (
            (slice(0, columns), keep, received),
            (slice(columns, None), second_keep, second_received),
        ):
            outs[j][:, span] = (one[j].astype(F32) + other[j].astype(F32)).astype(outs[j].dtype)


def pair_sum(*parts):
    shape = (parts[0].shape[1], parts[0].shape[2] + parts[2].shape[2])
    return pl.pallas_call(
        pair_sum_kernel,
        in_specs=[whole(a.shape) for a in parts],
        out_specs=[whole(shape)] * 4,
        out_shape=[jax.ShapeDtypeStruct(shape, t) for t in (F32, BF, BF, BF)],
        compiler_params=params(18),
        cost_estimate=cost(10_000_000, 5_000_000),
        name="pair_sum",
    )(*parts)


def plane_sum_kernel(info, own, from_x, from_y, from_d, near, keep):
    quarter = near.shape[2]
    for j, (target, place) in enumerate(((keep, 0), (near, 1), (keep, 2), (near, 3))):
        span = pl.ds(pl.multiple_of((info[1] ^ place) * quarter, 128), quarter)
        summed = own[:, span]
        for part in (from_x, from_y, from_d):
            summed = summed + part[:, span].astype(F32)
        target[j // 2] = summed.astype(target.dtype)


def plane_sum(info, parts):
    rows, columns = parts[0].shape
    shape = (2, rows, columns // 4)
    return pl.pallas_call(
        plane_sum_kernel,
        in_specs=[SCALARS] + [whole(a.shape) for a in parts],
        out_specs=[whole(shape)] * 2,
        out_shape=[jax.ShapeDtypeStruct(shape, t) for t in (BF, F32)],
        compiler_params=params(16),
        cost_estimate=cost(10_000_000, 5_000_000),
        name="plane_sum",
    )(info, *parts)


STEPS = 6


def attention_block(attention, step, number):
    row = pl.multiple_of((step % 3) * 48, 16)
    first = (number % 2) * COLUMNS
    return attention[(step // 3) * 4 + number // 2, pl.ds(row, 48), first : first + COLUMNS]


def feed_block(info, feed_sum, step, number):
    which, rest = divmod(number, 8)
    t, sub = divmod(rest, 2)
    row = pl.multiple_of((info[0] ^ t) * 144 + (step % 3) * 48, 16)
    return feed_sum[(which * 2 + sub) * 2 + step // 3, pl.ds(row, 48), :]


def lanes_sum(value):
    return sum(value[:, j * 128 : (j + 1) * 128] for j in range(value.shape[1] // 128))


def start_attention(info, pieces, target, semaphores):
    copies = []
    for j, piece in enumerate(pieces):
        core = info[2] if j < 2 else 1 - info[2]
        for k in range(2):
            place = core * 4 + (info[1] ^ (2 * k + j % 2))
            copy = pltpu.make_async_copy(piece.at[k], target.at[place], semaphores.at[2 * j + k])
            copy.start()
            copies.append(copy)
    return copies


def attention_scratch(pieces):
    return [pltpu.VMEM((8, *pieces[0].shape[1:]), BF), pltpu.SemaphoreType.DMA((8,))]


def feed_totals_kernel(info, feed_sum, gate, up, gain, gain_grad, squares):
    step = pl.program_id(0)
    total = jnp.zeros((48, 128), F32)
    square = jnp.zeros((48, 128), F32)
    for master, number in ((gate, 0), (up, 8)):
        for j in range(8):
            block = feed_block(info, feed_sum, step, number + j).astype(F32)
            weight = master[:, j * COLUMNS : (j + 1) * COLUMNS].astype(BF).astype(F32)
            total = total + lanes_sum(weight * block)
            square = square + lanes_sum(block * block)
    grad = jnp.sum(total, axis=1, keepdims=True) / gain[...]
    gain_grad[...] = grad
    result = jnp.sum(square.reshape(6, 8, 128), axis=0)
    result = result + jnp.sum(jnp.square(grad)) * (1.0 / 1024)
    row = pl.multiple_of(step * 16, 16)
    for e in range(8):
        for cb in range(3):
            block = feed_sum[e, pl.ds(576 + cb * 96 + row, 16), :].astype(F32)
            part = lanes_sum(block * block)
            result = result + part[:8] + part[8:]

    @pl.when(step == 0)
    def _():
        squares[...] = result

    @pl.when(step > 0)
    def _():
        squares[...] += result


def feed_totals(info, feed_sum, gate, up, gain):
    rows, columns = gate.shape
    wide = pl.BlockSpec((rows // STEPS, columns), lambda i: (i, 0))
    narrow = pl.BlockSpec((rows // STEPS, 1), lambda i: (i, 0))
    return pl.pallas_call(
        feed_totals_kernel,
        grid=(STEPS,),
        in_specs=[SCALARS, once(feed_sum.shape), wide, wide, narrow],
        out_specs=[narrow, whole((8, 128))],
        out_shape=[jax.ShapeDtypeStruct((rows, 1), F32), jax.ShapeDtypeStruct((8, 128), F32)],
        compiler_params=params(20),
        cost_estimate=cost(30_000_000, 13_000_000),
        name="feed_totals",
    )(info, feed_sum, gate, up, gain)


def attention_totals_kernel(info, *refs):
    pieces, (query, key, value, gain, before) = refs[:4], refs[4:9]
    gain_grad, squares, attention, semaphores = refs[9:]
    for copy in start_attention(info, pieces, attention, semaphores):
        copy.wait()
    result = before[...]
    for step in range(STEPS):
        rows = slice(step * 48, (step + 1) * 48)
        total = jnp.zeros((48, 128), F32)
        square = jnp.zeros((48, 128), F32)
        for master, number, count in ((query, 0, 3), (key, 6, 1), (value, 7, 1)):
            for j in range(count):
                block = attention_block(attention, step, number + j).astype(F32)
                square = square + lanes_sum(block * block)
                weight = master[rows, j * COLUMNS : (j + 1) * COLUMNS].astype(BF).astype(F32)
                total = total + lanes_sum(weight * block)
        for j in range(3):
            block = attention_block(attention, step, 3 + j).astype(F32)
            square = square + lanes_sum(block * block)
        grad = jnp.sum(total, axis=1, keepdims=True) / gain[rows, :]
        gain_grad[rows, :] = grad
        result = result + jnp.sum(square.reshape(6, 8, 128), axis=0)
        result = result + jnp.sum(jnp.square(grad)) * (1.0 / 1024)
    squares[...] = result


def attention_totals(info, pieces, query, key, value, gain, before):
    rows = query.shape[0]
    return pl.pallas_call(
        attention_totals_kernel,
        in_specs=[SCALARS]
        + [ANY] * 4
        + [whole(a.shape) for a in (query, key, value, gain, before)],
        out_specs=[whole((rows, 1)), whole((8, 128))],
        out_shape=[jax.ShapeDtypeStruct((rows, 1), F32), jax.ShapeDtypeStruct((8, 128), F32)],
        scratch_shapes=attention_scratch(pieces),
        compiler_params=params(12),
        cost_estimate=cost(10_000_000, 4_000_000),
        name="attention_totals",
    )(info, *pieces, query, key, value, gain, before)


def update_kernel(info, s0, s1, s2, s3, feed_sum, *refs):
    pieces, moments, masters = refs[:4], refs[4:11], refs[11:18]
    new_moments, updates, norm, attention, semaphores = (
        refs[18:25],
        refs[25:32],
        refs[32],
        refs[33],
        refs[34],
    )
    step = pl.program_id(0)

    @pl.when(step == 0)
    def _():
        for copy in start_attention(info, pieces, attention, semaphores):
            copy.wait()

    squares = (s0[...] + s1[...]) + (s2[...] + s3[...])
    length = jnp.sqrt(jnp.sum(squares, keepdims=True))
    norm[...] = length
    clip = jnp.minimum(1.0, jnp.sqrt(F32(PARAMS)) / (length + 1e-06))

    def renew(k, rows, columns, block):
        momentum = momentum_beta * moments[k][rows, columns] + clip * block.astype(F32)
        new_moments[k][rows, columns] = momentum
        updates[k][rows, columns] = (
            masters[k][rows, columns] * (1.0 - learning_rate * weight_decay)
            - learning_rate * momentum
        )

    for k, number, count in ((0, 0, 3), (1, 6, 1), (2, 7, 1), (3, 3, 3)):
        for j in range(count):
            block = attention_block(attention, step, number + j)
            renew(k, slice(0, 48), slice(j * COLUMNS, (j + 1) * COLUMNS), block)
    for k, number in ((4, 0), (5, 8)):
        for j in range(8):
            block = feed_block(info, feed_sum, step, number + j)
            renew(k, slice(0, 48), slice(j * COLUMNS, (j + 1) * COLUMNS), block)
    row = pl.multiple_of(step * 16, 16)
    for e in range(8):
        for cb in range(3):
            block = feed_sum[e, pl.ds(576 + cb * 96 + row, 16), :]
            renew(6, slice(e * 16, (e + 1) * 16), slice(cb * COLUMNS, (cb + 1) * COLUMNS), block)


def update(info, squares, pieces, feed_sum, moments, masters):
    blocks = [
        pl.BlockSpec((a.shape[0] // STEPS, a.shape[1]), lambda i: (i, 0)) for a in masters
    ]
    shapes = [jax.ShapeDtypeStruct(a.shape, F32) for a in masters]
    return pl.pallas_call(
        update_kernel,
        grid=(STEPS,),
        in_specs=[SCALARS]
        + [whole((8, 128))] * 4
        + [once(feed_sum.shape)]
        + [ANY] * 4
        + blocks * 2,
        out_specs=blocks * 2 + [whole((1, 1))],
        out_shape=shapes * 2 + [jax.ShapeDtypeStruct((1, 1), F32)],
        scratch_shapes=attention_scratch(pieces),
        compiler_params=params(60),
        cost_estimate=cost(20_000_000, 64_000_000),
        name="update",
    )(info, *squares, feed_sum, *pieces, *moments, *masters)


def fast_device(
    tokens,
    cotangent,
    picture_starts,
    query_weight,
    key_matrix,
    value_matrix,
    out_weight,
    gate_weight,
    up_weight,
    down_weight,
    attention_gain,
    feed_gain,
    query_moment,
    key_velocity,
    value_velocity,
    out_moment,
    gate_moment,
    up_moment,
    down_moment,
    attention_moment,
    feed_moment,
):
    masters = (
        query_weight,
        key_matrix,
        value_matrix,
        out_weight,
        gate_weight,
        up_weight,
        down_weight,
        attention_gain,
        feed_gain,
    )
    moments = (
        query_moment,
        key_velocity,
        value_velocity,
        out_moment,
        gate_moment,
        up_moment,
        down_moment,
        attention_moment,
        feed_moment,
    )
    me = lax.axis_index("seq")
    line = lax.axis_index("dp") // 2
    core = lax.axis_index("dp") % 2
    rows = tokens.shape[1]
    width = tokens.shape[2]
    shard = query_weight.shape[0]
    half = shard // 2
    hidden_own = down_weight.shape[0]
    places = [me, me ^ 1, me ^ 2, me ^ 3]

    gain_columns = [
        gain.astype(BF).astype(F32)[:, None] for gain in (attention_gain, feed_gain)
    ]
    info = index_array(me, line, core)

    def fetch_rows(own, mine):
        fetched = gather_plane(mine)
        return [own, *fetched, *[swap_core(block) for block in fetched]]

    def core_half(own):
        return lax.dynamic_slice_in_dim(own, core * half, half, 0)

    wide_gains = jnp.pad(jnp.concatenate(gain_columns, axis=1), ((0, 0), (0, 126)))
    projections = (query_weight, key_matrix, value_matrix, wide_gains)
    mine_qkv = jnp.concatenate([core_half(weight) for weight in projections], axis=1).astype(BF)
    own_qkv = jnp.concatenate(projections, axis=1).astype(BF)
    qkv = fetch_rows(own_qkv, mine_qkv)
    own_out = out_weight.astype(BF)
    mine_out = core_half(own_out)

    own_down = down_weight.astype(BF)

    token_positions = me * rows + jnp.arange(rows, dtype=jnp.int32)
    frequency = 10000.0 ** (-jnp.arange(HEAD_SIZE // 2, dtype=F32) / (HEAD_SIZE // 2))
    angles = token_positions.astype(F32)[:, None] * frequency[None, :]
    cosine, sine = jnp.cos(angles), jnp.sin(angles)
    trig = (
        jnp.concatenate([cosine] * 4, axis=1),
        jnp.concatenate([-sine, sine, -sine, sine], axis=1),
    )

    x = tokens[0]
    starts = picture_starts[0]
    bit = line % 2

    def columns_for(place):
        at = (core * half, place * hidden_own)
        size = (half, hidden_own)
        return jnp.where(
            bit == 0, lax.dynamic_slice(gate_weight, at, size), lax.dynamic_slice(up_weight, at, size)
        ).astype(BF)

    sent = [columns_for(place) for place in places[1:]]
    sent, _ = after(sent, qkv[1:3])
    fetched = [swap_x(sent[0]), swap_y(sent[1]), swap_diagonal(sent[2])]
    query, key_value, act_one, gains, full_qkv = project(info, x, *trig, qkv)
    key_sent, fetched = after(key_value, fetched)
    key_x, key_y = swap_x(key_sent), swap_y(key_sent)
    mine_out, _ = after(mine_out, (key_x, key_y))
    out_x, out_y = swap_x(mine_out), swap_y(mine_out)
    key_values = [key_value, key_x, key_y, relay(key_x, key_y)]
    attended = attend(info, starts, query, key_values)
    (out_x, out_y), attended = after((out_x, out_y), attended)
    fetched_out = [out_x, out_y, relay(out_x, out_y)]
    out_rows = [own_out, *fetched_out, *[swap_core(block) for block in fetched_out]]

    near_columns = swap_near(jnp.stack(fetched))
    other_columns = swap_core(jnp.concatenate([jnp.stack(fetched), near_columns]))
    own_columns = [
        lax.dynamic_slice_in_dim(weight, me * hidden_own, hidden_own, 1)
        for weight in (gate_weight, up_weight)
    ]
    gate_up = [
        jnp.concatenate(own_columns, axis=1).astype(BF),
        *fetched,
        near_columns,
        other_columns,
    ]

    upstream_low = cotangent[0]
    upstream_sent, _ = after(upstream_low, attended)
    upstreams = [upstream_low, *gather_plane(upstream_sent)]
    attention, residual, act_two, full_out = out_project(info, attended, x, gains, out_rows)
    act_x, act_y, act_d = gather_parts(act_two)
    acts = [act_two, act_x, act_y]
    hidden, both_back, *act_parts, full_gu = feed_first(
        info, acts, upstreams[:3], gate_up, own_down
    )
    act_d, hidden = after(act_d, hidden)
    acts.append(jnp.concatenate(act_d))
    last_hidden, last_back, act_part = feed_last(acts[3], upstreams[3], full_gu, own_down)
    act_grads = [
        act_parts[0],
        swap_x(act_parts[1]),
        swap_y(act_parts[2]),
        swap_diagonal(act_part),
    ]
    layer_blocks = layer_parts(hidden, last_hidden, own_down)
    parts = feed_gradients(
        info, acts, both_back, last_back, hidden, last_hidden, upstreams
    )
    act_grads, (parts, layer_blocks) = after(act_grads, (parts, layer_blocks))
    output = (residual + scatter_plane(*layer_blocks)).astype(BF)[None]

    grad_residual, grad_low, query_back, *kv_parts = attend_back(
        info,
        starts,
        act_grads,
        upstream_low,
        residual,
        gains,
        query,
        key_values,
        attended,
        trig,
        full_out,
    )
    kv_parts, output = after(kv_parts, output)
    kv_sums = [
        kv_parts[0],
        swap_x(kv_parts[1]),
        swap_y(kv_parts[2]),
        swap_diagonal(kv_parts[3]),
    ]

    def across(own, for_x, for_y, for_d):
        return [own, swap_x(for_x), swap_y(for_y), swap_diagonal(for_d)]

    keep, send = query_gradients(info, act_one, attention, query_back, grad_low)
    kv_sums[0], (keep, send) = after(kv_sums[0], (keep, send))
    received = swap_core(send)
    key_back, second_keep, second_send = key_gradients(info, act_one, kv_sums, trig)
    pair = pair_sum(keep, received, second_keep, swap_core(second_send))
    plane_parts = across(*pair)

    feed_own = lax.psum_scatter(parts, "dp", scatter_dimension=0, tiled=True)[0]
    feed_own, _ = after(feed_own, (second_keep, second_send))
    feed_own = jnp.concatenate(
        [
            feed_own[:half],
            swap_x(feed_own[half : 2 * half]),
            swap_y(feed_own[2 * half : 3 * half]),
            swap_diagonal(feed_own[3 * half : 4 * half]),
            feed_own[4 * half :],
        ]
    )
    feed_whole = lax.all_gather(feed_own, "dp", axis=0)

    input_grad = input_back(query_back, key_back, x, gains, grad_residual, full_qkv)[None]
    plane_parts, input_grad = after(plane_parts, input_grad)
    near_sent, keep = plane_sum(info, plane_parts)
    near = swap_near(near_sent)
    far = swap_far((keep[1] + near[1]).astype(BF))
    line_own = (keep[0] + near[0] + far).astype(BF)
    pair_own = jnp.stack([line_own, swap_far(line_own)])
    near_own = swap_near(pair_own)

    feed_gain_grad, feed_squares = feed_totals(
        info, feed_whole, gate_weight, up_weight, gain_columns[1]
    )
    near_own, feed_squares = after(near_own, feed_squares)
    pieces = [pair_own, near_own, swap_core(pair_own), swap_core(near_own)]
    attention_gain_grad, squares = attention_totals(
        info, pieces, query_weight, key_matrix, value_matrix, gain_columns[0], feed_squares
    )
    *renewed, norm = update(
        info,
        across(squares, squares, squares, squares),
        pieces,
        feed_whole,
        moments[:7],
        masters[:7],
    )
    gradient_norm = norm[0, 0]
    clip_factor = jnp.minimum(1.0, jnp.sqrt(F32(PARAMS)) / (gradient_norm + 1e-06))
    momenta, updated = list(renewed[:7]), list(renewed[7:])
    for k, gradient in ((7, attention_gain_grad[:, 0]), (8, feed_gain_grad[:, 0])):
        momenta.append(momentum_beta * moments[k] + clip_factor * gradient)
        updated.append(
            masters[k] * (1.0 - learning_rate * weight_decay) - learning_rate * momenta[k]
        )
    return (output, input_grad, *momenta, *updated, gradient_norm)


def solution(mesh):
    fits = mesh.shape["seq"] == 4 and mesh.shape["dp"] == 8
    body = fast_device if fits else per_device
    return jax.shard_map(
        body,
        mesh=mesh,
        in_specs=(
            P("dp", "seq", None),
            P("dp", "seq", None),
            P("dp", None),
            P("seq", None),
            P("seq", None),
            P("seq", None),
            P("seq", None),
            P("seq", None),
            P("seq", None),
            P("seq", None),
            P("seq"),
            P("seq"),
            P("seq", None),
            P("seq", None),
            P("seq", None),
            P("seq", None),
            P("seq", None),
            P("seq", None),
            P("seq", None),
            P("seq"),
            P("seq"),
        ),
        out_specs=(
            P("dp", "seq", None),
            P("dp", "seq", None),
            P("seq", None),
            P("seq", None),
            P("seq", None),
            P("seq", None),
            P("seq", None),
            P("seq", None),
            P("seq", None),
            P("seq"),
            P("seq"),
            P("seq", None),
            P("seq", None),
            P("seq", None),
            P("seq", None),
            P("seq", None),
            P("seq", None),
            P("seq", None),
            P("seq"),
            P("seq"),
            P(),
        ),
        check_vma=False,
    )
```
